32 devices in a mesh: dp: 8 (over y, x, core), tensor: 4 (over z).
Axes of the slice: x: 2, y: 2, z: 4, core: 2. Of those that a mesh axis runs over, the one named last changes fastest.
Arguments:
- tokens: bfloat16 [24576, 1280], P(('dp', 'tensor')), may hold values from -6 to 6
- lengths: int32 [16], P('dp'), may hold values from 1383 to 1536
- cotangent: bfloat16 [24576, 1280], P(('dp', 'tensor')), may hold values from -6 to 6
- norm1_gain: float32 [1280], replicated, may hold values from 0.5 to 1.5
- norm1_shift: float32 [1280], replicated, may hold values from -2 to 2
- query_weight: bfloat16 [1280, 1280], P('dp', 'tensor'), may hold values from -0.15625 to 0.15625
- query_bias: float32 [1280], P('tensor'), may hold values from -2 to 2
- key_weight: bfloat16 [1280, 1280], P('dp', 'tensor'), may hold values from -0.15625 to 0.15625
- value_weight: bfloat16 [1280, 1280], P('dp', 'tensor'), may hold values from -0.15625 to 0.15625
- value_bias: float32 [1280], P('tensor'), may hold values from -2 to 2
- out_weight: bfloat16 [1280, 1280], P('tensor', 'dp'), may hold values from -3.5 to 3.5
- out_bias: float32 [1280], replicated, may hold values from -2 to 2
- norm2_gain: float32 [1280], replicated, may hold values from 0.5 to 1.5
- norm2_shift: float32 [1280], replicated, may hold values from -2 to 2
- up_weight: bfloat16 [1280, 5120], P('dp', 'tensor'), may hold values from -0.15625 to 0.15625
- up_bias: float32 [5120], P('tensor'), may hold values from -2 to 2
- down_weight: bfloat16 [5120, 1280], P('tensor', 'dp'), may hold values from -0.078125 to 0.078125
- down_bias: float32 [1280], replicated, may hold values from -2 to 2
Outputs:
- layer_out: bfloat16 [24576, 1280], P(('dp', 'tensor'))
- grad_tokens: bfloat16 [24576, 1280], P(('dp', 'tensor'))
- grad_norm1_gain: float32 [1280], replicated
- grad_norm1_shift: float32 [1280], replicated
- grad_query_weight: float32 [1280, 1280], P('dp', 'tensor')
- grad_query_bias: float32 [1280], P('tensor')
- grad_key_weight: float32 [1280, 1280], P('dp', 'tensor')
- grad_value_weight: float32 [1280, 1280], P('dp', 'tensor')
- grad_value_bias: float32 [1280], P('tensor')
- grad_out_weight: float32 [1280, 1280], P('tensor', 'dp')
- grad_out_bias: float32 [1280], replicated
- grad_norm2_gain: float32 [1280], replicated
- grad_norm2_shift: float32 [1280], replicated
- grad_up_weight: float32 [1280, 5120], P('dp', 'tensor')
- grad_up_bias: float32 [5120], P('tensor')
- grad_down_weight: float32 [5120, 1280], P('tensor', 'dp')
- grad_down_bias: float32 [1280], replicated
The draws below stay inside these ranges and needn't reach their ends.
All inputs are finite; a program needn't handle non-finite values.
Results may differ from the reference program's by a relative error of at most 0.02.
Values may be sent and summed in bfloat16 or wider, within the bound.
A program may use at most 256 MiB of HBM per device.

```python
import jax
import jax.numpy as jnp
from jax import lax

D = 1280
HEADS = 16
HDIM = 80
FF = 5120
SEQ = 1536
CLIPS = 16
TOKENS = 24576


def place_ends(values, key, smallest, largest):
    shape = values.shape
    index_at = [jax.random.randint(jax.random.fold_in(key, axis), (), 0, shape[axis]) for axis in range(len(shape))]
    values = values.at[tuple(index_at)].set(smallest)
    longest = shape.index(max(shape))
    index_at[longest] = (index_at[longest] + 1) % shape[longest]
    return values.at[tuple(index_at)].set(largest)


def shard_levels(own_key, dims, split, least, top_value):
    gain = 1.0
    for dim, shards_of in split:
        draws = jax.random.uniform(jax.random.fold_in(jax.random.fold_in(own_key, 6), dim), (shards_of,), jnp.float32, least / len(split), top_value / len(split))
        gain = gain * jnp.repeat(jnp.exp(draws), dims[dim] // shards_of).reshape((-1,) + (1,) * (len(dims) - 1 - dim))
    return gain


def noise(own_key, dims, scale, bound, cuts=(), kind=jnp.bfloat16):
    entries = jax.random.normal(own_key, dims, jnp.float32) * scale
    if len(cuts) > 0:
        entries = shard_levels(own_key, dims, cuts, -0.22, 0.18) * entries
    return jnp.clip(entries, min=-bound, max=bound).astype(kind)


def setup_inputs(seed: int = 0) -> dict:
    keys = jax.random.split(jax.random.key(seed), 19)
    tokens = noise(keys[0], (TOKENS, D), 1.0, 6.0, ((0, 32),))
    lengths = place_ends(jax.random.randint(keys[1], (CLIPS,), SEQ - SEQ // 10, SEQ + 1), jax.random.fold_in(keys[1], 1), SEQ - SEQ // 10, SEQ).astype(jnp.int32)
    cotangent = noise(keys[2], (TOKENS, D), 1.0, 6.0, ((0, 32),))
    norm1_gain = jnp.clip(1.0 + 0.1 * jax.random.normal(keys[3], (D,), jnp.float32), 0.5, 1.5)
    norm1_shift = noise(keys[4], (D,), 0.3, 2.0, (), jnp.float32)
    query_weight = noise(keys[5], (D, D), D ** -0.5, 0.15625, ((0, 8), (1, 4)))
    query_bias = noise(keys[6], (D,), 0.3, 2.0, ((0, 4),), jnp.float32)
    key_weight = noise(keys[7], (D, D), D ** -0.5, 0.15625, ((0, 8), (1, 4)))
    value_weight = noise(keys[8], (D, D), D ** -0.5, 0.15625, ((0, 8), (1, 4)))
    value_bias = noise(keys[9], (D,), 0.3, 2.0, ((0, 4),), jnp.float32)
    out_weight = noise(keys[10], (D, D), (max(1, 4 * D // SEQ)) ** -0.5, 3.5, ((0, 4), (1, 8)))
    out_bias = noise(keys[11], (D,), 0.3, 2.0, (), jnp.float32)
    norm2_gain = jnp.clip(1.0 + 0.1 * jax.random.normal(keys[12], (D,), jnp.float32), 0.5, 1.5)
    norm2_shift = noise(keys[13], (D,), 0.3, 2.0, (), jnp.float32)
    up_weight = noise(keys[14], (D, FF), D ** -0.5, 0.15625, ((0, 8), (1, 4)))
    up_bias = noise(keys[15], (FF,), 0.3, 2.0, ((0, 4),), jnp.float32)
    down_weight = noise(keys[16], (FF, D), FF ** -0.5, 0.078125, ((0, 4), (1, 8)))
    down_bias = noise(keys[17], (D,), 0.3, 2.0, (), jnp.float32)
    return {"tokens": tokens, "lengths": lengths, "cotangent": cotangent, "norm1_gain": norm1_gain, "norm1_shift": norm1_shift, "query_weight": query_weight, "query_bias": query_bias, "key_weight": key_weight, "value_weight": value_weight, "value_bias": value_bias, "out_weight": out_weight, "out_bias": out_bias, "norm2_gain": norm2_gain, "norm2_shift": norm2_shift, "up_weight": up_weight, "up_bias": up_bias, "down_weight": down_weight, "down_bias": down_bias}


EPS = 1e-05
HIGH = lax.Precision.HIGHEST

@jax.custom_vjp
def low(v):
    return lax.optimization_barrier(v.astype(jnp.bfloat16)).astype(jnp.float32)

@jax.custom_vjp
def low_back(v):
    return v

def low_keep(v):
    return (low(v), None)

def low_pass(kept, grad):
    return (grad,)

def back_keep(v):
    return (v, None)

def back_low(kept, grad):
    return (low(grad),)
low.defvjp(low_keep, low_pass)
low_back.defvjp(back_keep, back_low)

def matmul_high(left, right):
    return jnp.dot(left, right, precision=HIGH, preferred_element_type=jnp.float32)

def norm_rows(values, norm_gain, norm_shift):
    center = values - lax.optimization_barrier(jnp.mean(values, -1, keepdims=True))
    spread = lax.optimization_barrier(jnp.mean(center * center, -1, keepdims=True))
    return center * lax.rsqrt(spread + EPS) * norm_gain + norm_shift

def clip_layer(params, clip_rows, clip_length):
    gain_one, shift_one, query_weight, query_bias, key_weight, value_weight, value_bias, out_weight, out_bias, gain_two, shift_two, up_weight, up_bias, down_weight, down_bias = params
    head_shape = (SEQ, HEADS, HDIM)
    first_in = low(norm_rows(clip_rows, gain_one, shift_one))
    queries = low(low_back(matmul_high(first_in, query_weight)) + query_bias)
    key_rows = low(low_back(matmul_high(first_in, key_weight)))
    value_rows = low(low_back(matmul_high(first_in, value_weight)) + value_bias)
    scores = jnp.einsum('qhd,khd->hqk', queries.reshape(head_shape), key_rows.reshape(head_shape), precision=HIGH)
    scores = low_back(scores * HDIM ** (-0.5))
    visible = (jnp.arange(SEQ) < clip_length)[None, None, :]
    scores = jnp.where(visible, scores, -1e+30)
    row_max = lax.optimization_barrier(jnp.max(scores, -1, keepdims=True))
    exp_scores = jnp.exp(scores - row_max)
    attn_probs = low(exp_scores / lax.optimization_barrier(jnp.sum(exp_scores, -1, keepdims=True)))
    mixed_heads = jnp.einsum('hqk,khd->qhd', attn_probs, value_rows.reshape(head_shape), precision=HIGH)
    heads_out = low(low_back(mixed_heads.reshape(SEQ, D)))
    middle = clip_rows + low_back(matmul_high(heads_out, out_weight)) + out_bias
    second_in = low(norm_rows(middle, gain_two, shift_two))
    hidden_pre = low_back(matmul_high(second_in, up_weight)) + up_bias
    hidden = low(jax.nn.gelu(hidden_pre, approximate=False))
    return middle + low_back(matmul_high(hidden, down_weight)) + down_bias

def reference(tokens, lengths, cotangent, norm1_gain, norm1_shift, query_weight, query_bias, key_weight, value_weight, value_bias, out_weight, out_bias, norm2_gain, norm2_shift, up_weight, up_bias, down_weight, down_bias):
    params = tuple((member.astype(jnp.float32) for member in (norm1_gain, norm1_shift, query_weight, query_bias, key_weight, value_weight, value_bias, out_weight, out_bias, norm2_gain, norm2_shift, up_weight, up_bias, down_weight, down_bias)))
    source = tokens.astype(jnp.float32)

    def forward(inputs, *weights_all):

        def one_clip(member):
            return clip_layer(weights_all, member[0], member[1])
        outputs = lax.map(jax.checkpoint(one_clip), (inputs.reshape(CLIPS, SEQ, D), lengths))
        return outputs.reshape(TOKENS, D)
    layer_out, pullback = jax.vjp(forward, source, *params)
    visible = (jnp.arange(SEQ)[None, :] < lengths[:, None]).reshape(TOKENS, 1)
    seed_grad = cotangent.astype(jnp.float32) * visible.astype(jnp.float32)
    grads = pullback(seed_grad)
    return (layer_out.astype(jnp.bfloat16), grads[0].astype(jnp.bfloat16), grads[1], grads[2], grads[3], grads[4], grads[5], grads[6], grads[7], grads[8], grads[9], grads[10], grads[11], grads[12], grads[13], grads[14], grads[15])
```

```python
import functools

import jax
import jax.numpy as jnp
from jax import lax
from jax.experimental import pallas as pl
from jax.experimental.pallas import tpu as pltpu
from jax.sharding import PartitionSpec as P

HDIM = 80
EPS = 1e-05
LOG2E = 1.4426950408889634
F32 = jnp.float32
BF16 = jnp.bfloat16


def norm_rows(values, norm_gain, norm_shift):
    center = values - jnp.mean(values, -1, keepdims=True)
    spread = jnp.mean(center * center, -1, keepdims=True)
    return center * lax.rsqrt(spread + EPS) * norm_gain + norm_shift


def norm_back(values, norm_gain, grad):
    center = values - jnp.mean(values, -1, keepdims=True)
    scale = lax.rsqrt(jnp.mean(center * center, -1, keepdims=True) + EPS)
    normed = center * scale
    scaled = grad * norm_gain
    back = scaled - jnp.mean(scaled, -1, keepdims=True)
    back = (back - normed * jnp.mean(scaled * normed, -1, keepdims=True)) * scale
    return back, jnp.sum(grad * normed, 0), jnp.sum(grad, 0)


def dot_nn(left, right):
    return jnp.dot(left, right, preferred_element_type=F32)


def dot_tn(left, right):
    return lax.dot_general(left, right, (((0,), (0,)), ((), ())), preferred_element_type=F32)


def dot_nt(left, right):
    return lax.dot_general(left, right, (((1,), (1,)), ((), ())), preferred_element_type=F32)


def up_kernel(rows_ref, weight_ref, bias_ref, hidden_ref, slope_ref):
    pre = dot_nn(rows_ref[...], weight_ref[...]) + bias_ref[...]
    cdf = 0.5 * lax.erf(pre * (0.5**0.5)) + 0.5
    density = jnp.exp(-0.5 * pre * pre) * 0.3989422804014327
    hidden_ref[...] = (pre * cdf).astype(BF16)
    slope_ref[...] = (cdf + pre * density).astype(BF16)


def up_gelu(rows, weight, bias):
    count, depth = rows.shape
    cols = weight.shape[1]
    block_rows, block_cols = min(512, count), min(640, cols)
    return pl.pallas_call(
        up_kernel,
        grid=(cols // block_cols, count // block_rows),
        in_specs=[
            pl.BlockSpec((block_rows, depth), lambda n, m: (m, 0)),
            pl.BlockSpec((depth, block_cols), lambda n, m: (0, n)),
            pl.BlockSpec((1, block_cols), lambda n, m: (0, n)),
        ],
        out_specs=[
            pl.BlockSpec((block_rows, block_cols), lambda n, m: (m, n)),
            pl.BlockSpec((block_rows, block_cols), lambda n, m: (m, n)),
        ],
        out_shape=[jax.ShapeDtypeStruct((count, cols), BF16)] * 2,
        cost_estimate=pl.CostEstimate(
            flops=2 * count * depth * cols, bytes_accessed=20_000_000, transcendentals=0
        ),
        compiler_params=pltpu.CompilerParams(vmem_limit_bytes=40 << 20),
        name="up_gelu",
    )(rows, weight, bias)


def attend_kernel(heads, scaling, query_ref, all_ref, mask_ref, out_ref, total_ref):
    width = heads * HDIM
    queries = query_ref[...]
    mask = mask_ref[...]
    outs, totals = [], []
    for head in range(heads):
        low = head * HDIM
        query = queries[:, low : low + HDIM]
        key = all_ref[:, width + low : width + low + HDIM]
        value = all_ref[:, 2 * width + low : 2 * width + low + HDIM]
        scores = dot_nt(query, key) * (scaling * LOG2E) + mask
        row_max = jnp.max(scores, -1, keepdims=True)
        exp_scores = jnp.exp2(scores - row_max)
        total = jnp.sum(exp_scores, -1, keepdims=True)
        mixed = dot_nn(exp_scores.astype(BF16), value)
        outs.append(mixed * (1.0 / total))
        totals.append(row_max + jnp.log2(total))
    out_ref[...] = jnp.concatenate(outs, -1).astype(BF16)
    for head in range(heads):
        wide = jnp.broadcast_to(totals[head], (totals[head].shape[0], 128))
        total_ref[head : head + 1, :] = wide.T[0:1, :]


def attend(joined, mask_row, heads, scaling):
    count, cols = joined.shape
    block_rows = min(256, count)
    width = heads * HDIM
    return pl.pallas_call(
        functools.partial(attend_kernel, heads, scaling),
        grid=(count // block_rows,),
        in_specs=[
            pl.BlockSpec((block_rows, cols), lambda m: (m, 0)),
            pl.BlockSpec((count, cols), lambda m: (0, 0)),
            pl.BlockSpec((1, count), lambda m: (0, 0)),
        ],
        out_specs=[
            pl.BlockSpec((block_rows, width), lambda m: (m, 0)),
            pl.BlockSpec((heads, block_rows), lambda m: (0, m)),
        ],
        out_shape=[
            jax.ShapeDtypeStruct((count, width), BF16),
            jax.ShapeDtypeStruct((heads, count), F32),
        ],
        cost_estimate=pl.CostEstimate(
            flops=2 * heads * count * count * 512,
            bytes_accessed=4_000_000,
            transcendentals=heads * count * count,
        ),
        compiler_params=pltpu.CompilerParams(vmem_limit_bytes=48 << 20),
        name="attend",
    )(joined, joined, mask_row)


def attend_back_kernel(
    heads, scaling, query_ref, all_ref, grad_ref, total_ref, mask_ref,
    out_ref, sums_ref, key_sum, value_sum,
):
    step = pl.program_id(0)
    steps = pl.num_programs(0)
    width = heads * HDIM
    block_rows = query_ref.shape[0]

    @pl.when(step == 0)
    def _():
        key_sum[...] = jnp.zeros_like(key_sum)
        value_sum[...] = jnp.zeros_like(value_sum)
        sums_ref[...] = jnp.zeros_like(sums_ref)

    queries = query_ref[...]
    grads = grad_ref[...]
    query_outs = []
    for head in range(heads):
        low = head * HDIM
        query = queries[:, low : low + HDIM]
        grad = grads[:, low : low + HDIM]
        key = all_ref[:, width + low : width + low + HDIM]
        value = all_ref[:, 2 * width + low : 2 * width + low + HDIM]
        scores = dot_nt(key, query) * (scaling * LOG2E) + mask_ref[...]
        probs = jnp.exp2(scores - total_ref[head : head + 1, :])
        grad_probs = dot_nt(value, grad)
        shared = jnp.sum(probs * grad_probs, 0, keepdims=True)
        grad_scores = (probs * (grad_probs - shared)).astype(BF16)
        value_sum[head, :, :HDIM] += dot_nn(probs.astype(BF16), grad)
        key_sum[head, :, :HDIM] += dot_nn(grad_scores, query)
        query_outs.append(dot_tn(grad_scores, key) * scaling)
    joined = jnp.concatenate(query_outs, -1)
    sums_ref[0:1, :width] += jnp.sum(joined, 0, keepdims=True)
    rows = pl.ds(pl.multiple_of(step * block_rows, block_rows), block_rows)
    out_ref[rows, :width] = joined.astype(BF16)

    @pl.when(step == steps - 1)
    def _():
        keys = jnp.concatenate([key_sum[head, :, :HDIM] for head in range(heads)], -1)
        values = jnp.concatenate([value_sum[head, :, :HDIM] for head in range(heads)], -1)
        sums_ref[1:2, :width] = jnp.sum(values, 0, keepdims=True)
        out_ref[:, width:] = jnp.concatenate([keys * scaling, values], -1).astype(BF16)


def attend_back(joined, grad_heads, totals, mask_col, heads, scaling):
    count, cols = joined.shape
    block_rows = min(256, count)
    width = heads * HDIM
    return pl.pallas_call(
        functools.partial(attend_back_kernel, heads, scaling),
        grid=(count // block_rows,),
        in_specs=[
            pl.BlockSpec((block_rows, cols), lambda m: (m, 0)),
            pl.BlockSpec((count, cols), lambda m: (0, 0)),
            pl.BlockSpec((block_rows, width), lambda m: (m, 0)),
            pl.BlockSpec((heads, block_rows), lambda m: (0, m)),
            pl.BlockSpec((count, 1), lambda m: (0, 0)),
        ],
        out_specs=[
            pl.BlockSpec((count, cols), lambda m: (0, 0)),
            pl.BlockSpec((8, 256), lambda m: (0, 0)),
        ],
        out_shape=[
            jax.ShapeDtypeStruct((count, cols), BF16),
            jax.ShapeDtypeStruct((8, 256), F32),
        ],
        scratch_shapes=[
            pltpu.VMEM((heads, count, 128), F32),
            pltpu.VMEM((heads, count, 128), F32),
        ],
        cost_estimate=pl.CostEstimate(
            flops=2 * heads * count * count * 1280,
            bytes_accessed=5_000_000,
            transcendentals=heads * count * count,
        ),
        compiler_params=pltpu.CompilerParams(vmem_limit_bytes=56 << 20),
        name="attend_back",
    )(joined, joined, grad_heads, totals, mask_col)


class Links:
    def __init__(self):
        self.dp = lax.axis_size("dp")
        self.tensor = lax.axis_size("tensor")
        self.dp_pos = lax.axis_index("dp")
        self.tensor_pos = lax.axis_index("tensor")
        self.chips = self.dp == 8 and self.tensor == 4
        self.half = (self.dp_pos if self.chips else self.tensor_pos) % 2
        if self.chips:
            self.x_odd = (self.dp_pos // 2) % 2 == 1
            self.y_odd = self.dp_pos // 4 == 1

    def pair(self, value):
        if self.chips:
            return lax.ppermute(value, "dp", [(i, i ^ 1) for i in range(self.dp)])
        return lax.ppermute(value, "tensor", [(i, i ^ 1) for i in range(self.tensor)])

    def along_x(self, value):
        return lax.ppermute(value, "dp", [(i, i ^ 2) for i in range(8)])

    def along_y(self, value):
        return lax.ppermute(value, "dp", [(i, i ^ 4) for i in range(8)])

    def along_z(self, value, shift):
        return lax.ppermute(value, "tensor", [(i, (i + shift) % 4) for i in range(4)])

    def move_rows(self, value):
        if not self.chips:
            return value
        swaps = [
            (a * 4 + b, (a ^ 1) * 4 + (b ^ 1)) for a in range(8) for b in range(4) if a % 2 != b % 2
        ]
        moved = lax.ppermute(value, ("dp", "tensor"), swaps)
        return jnp.where(self.half == self.tensor_pos % 2, value, moved)

    def turn(self, value):
        if not self.chips:
            return value
        cut = value.shape[-1] // 4
        parts = [value[..., i * cut : (i + 1) * cut] for i in range(4)]
        value = jnp.where(
            self.x_odd, jnp.concatenate([parts[1], parts[0], parts[3], parts[2]], -1), value
        )
        return jnp.where(
            self.y_odd, jnp.concatenate([value[..., 2 * cut :], value[..., : 2 * cut]], -1), value
        )

    def clip_length(self, lengths):
        if not self.chips:
            own, place = lengths, self.tensor_pos // 2
        else:
            own = jnp.where(self.half == self.tensor_pos % 2, lengths, self.pair(lengths))
            place = self.tensor_pos // 2
        return jnp.sum(jnp.where(jnp.arange(own.shape[0]) == place, own, 0))

    def columns(self, shard):
        rows, _, width = shard.shape
        if not self.chips:
            whole = lax.all_gather(shard, ("dp", "tensor"), axis=0)
            whole = lax.dynamic_index_in_dim(whole, self.half, 2, keepdims=False)
            whole = whole.reshape(self.dp, self.tensor, rows, width)
            return [whole[:, k].reshape(self.dp * rows, width) for k in range(self.tensor)]
        first = self.half == 0
        keep = jnp.where(first, shard[:, 0], shard[:, 1])
        got = self.pair(jnp.where(first, shard[:, 1], shard[:, 0]))
        own = jnp.where(first, jnp.concatenate([keep, got]), jnp.concatenate([got, keep]))
        blocks = []
        for k in range(4):
            here = own if k == 0 else self.along_z(own, k)
            if k % 2 == 0:
                by_x, by_y = self.along_x(here), self.along_y(here)
                by_both = self.along_y(by_x)
            else:
                by_y, by_x = self.along_y(here), self.along_x(here)
                by_both = self.along_x(by_y)
            blocks.append(jnp.concatenate([here, by_x, by_y, by_both]))
        return blocks

    def vectors(self, value):
        if not self.chips:
            whole = lax.all_gather(value, "tensor", axis=0)
            return [whole[k] for k in range(self.tensor)]
        return [value if k == 0 else self.along_z(value, k) for k in range(4)]

    def place(self, pieces):
        halves = (jnp.arange(2) == self.half)[None, :, None]
        total = 0.0
        for k, piece in enumerate(pieces):
            owner = (self.tensor_pos - k) % self.tensor if self.chips else k
            blocks = (jnp.arange(self.tensor) == owner)[:, None, None]
            total = total + jnp.where(halves & blocks, piece[None, None, :], 0.0)
        return total

    def total(self, value):
        if not self.chips:
            return lax.psum(value, ("dp", "tensor"))
        for bit in (1, 2, 4):
            value = value + lax.ppermute(value, "dp", [(i, i ^ bit) for i in range(8)])
        for bit in (1, 2):
            value = value + lax.ppermute(value, "tensor", [(i, i ^ bit) for i in range(4)])
        return value

    def scatter_plane(self, left, right, x_first):
        cut = left.shape[1] // 4

        def part(index):
            return dot_tn(left[:, index * cut : (index + 1) * cut], right)

        near, far = (1, 2) if x_first else (2, 1)
        go, follow = (self.along_x, self.along_y) if x_first else (self.along_y, self.along_x)
        sent_far = go(part(3).astype(BF16))
        sent_near = go(part(near).astype(BF16))
        second = (part(far) + sent_far.astype(F32)).astype(BF16)
        first = part(0) + sent_near.astype(F32)
        return (first + follow(second).astype(F32)).astype(BF16)

    def scatter_line(self, blocks):
        total = blocks[0].astype(F32)
        for k in range(1, 4):
            total = total + self.along_z(blocks[k], -k).astype(F32)
        return total

    def own_rows(self, total):
        rows = total.shape[0] // 2
        first = self.half == 0
        keep = jnp.where(first, total[:rows], total[rows:])
        got = self.pair(jnp.where(first, total[rows:], total[:rows]))
        return jnp.where(
            first, jnp.stack([keep, got], 1), jnp.stack([got, keep], 1)
        )

    def gradient(self, left, rights):
        if not self.chips:
            pieces = []
            for right, count, _ in rights:
                product = dot_tn(left, right).astype(BF16)
                width = product.shape[1] // count
                pieces += [product[:, i * width : (i + 1) * width] for i in range(count)]
            whole = jnp.stack(pieces, 0)
            features, width = whole.shape[1:]
            whole = whole.reshape(self.tensor, self.dp, features // self.dp, width)
            whole = jnp.moveaxis(whole, 1, 0)[:, :, :, None, :]
            halves = (jnp.arange(2) == self.half)[None, None, None, :, None]
            whole = jnp.where(halves, whole, jnp.zeros((), BF16))
            whole = whole.reshape((self.dp * self.tensor,) + whole.shape[2:])
            return lax.psum_scatter(whole, ("dp", "tensor"), tiled=False).astype(F32)
        blocks = []
        for right, count, x_first in rights:
            product = self.scatter_plane(left, right, x_first)
            width = product.shape[1] // count
            blocks += [product[:, i * width : (i + 1) * width] for i in range(count)]
        return self.own_rows(self.scatter_line(blocks))

    def merged(self, partial_of):
        got = self.pair(partial_of(1).astype(BF16))
        return partial_of(0) + got.astype(F32)


def local(
    tokens,
    lengths,
    cotangent,
    norm1_gain,
    norm1_shift,
    query_weight,
    query_bias,
    key_weight,
    value_weight,
    value_bias,
    out_weight,
    out_bias,
    norm2_gain,
    norm2_shift,
    up_weight,
    up_bias,
    down_weight,
    down_bias,
):
    links = Links()
    rows = tokens.shape[0]
    scaling = HDIM ** (-0.5)
    width = query_weight.shape[1] // 2
    heads = width // HDIM
    units = up_weight.shape[1] // 2
    count = links.tensor

    def halves(weight):
        return weight.reshape(weight.shape[0], 2, weight.shape[1] // 2)

    shard_attn = jnp.concatenate(
        [halves(query_weight), halves(key_weight), halves(value_weight), halves(out_weight.T)], -1
    )
    w_attn = links.columns(shard_attn)
    w_up = links.columns(halves(up_weight))
    w_down = links.columns(halves(down_weight.T))
    w_qkv = [block[:, : 3 * width] for block in w_attn]
    w_out = [block[:, 3 * width :] for block in w_attn]

    order = [0, 2, 1, 3] if links.chips else list(range(count))
    small = jnp.concatenate(
        [query_bias.reshape(2, width), value_bias.reshape(2, width), up_bias.reshape(2, units)], -1
    )
    small = links.vectors(jnp.where(links.half == 0, small[0], small[1]))
    bias_qkv = [
        jnp.concatenate([v[:width], jnp.zeros((width,), F32), v[width : 2 * width]]) for v in small
    ]
    bias_up = jnp.concatenate([small[k][2 * width :] for k in order])
    gain_one, shift_one, gain_two, shift_two, bias_out, bias_down = (
        links.turn(v)
        for v in (norm1_gain, norm1_shift, norm2_gain, norm2_shift, out_bias, down_bias)
    )

    clip_length = links.clip_length(lengths)
    frames = jnp.arange(rows)
    frames = jnp.concatenate([links.half * rows + frames, (1 - links.half) * rows + frames])
    visible = frames < clip_length
    mask = jnp.where(visible, 0.0, -1e30).astype(F32)

    source = links.turn(links.move_rows(tokens)).astype(F32)
    first_own = norm_rows(source, gain_one, shift_one).astype(BF16)
    first = jnp.concatenate([first_own, links.pair(first_own)])
    joined, heads_out, totals = [], [], []
    for k in range(count):
        joined.append((dot_nn(first, w_qkv[k]) + bias_qkv[k]).astype(BF16))
        mixed, total = attend(joined[k], mask[None, :], heads, scaling)
        heads_out.append(mixed)
        totals.append(total)
    heads_all = jnp.concatenate(heads_out, 1)
    w_out_all = jnp.concatenate(w_out, 1)
    branch = links.merged(
        lambda part: dot_nt(heads_all[part * rows : (part + 1) * rows], w_out_all)
    )
    middle = source + branch + bias_out
    second_own = norm_rows(middle, gain_two, shift_two).astype(BF16)
    second = jnp.concatenate([second_own, links.pair(second_own)])
    w_up_all = jnp.concatenate([w_up[k] for k in order], 1)
    hidden, slope = up_gelu(second, w_up_all, bias_up[None, :])
    w_down_all = jnp.concatenate([w_down[k] for k in order], 1)

    valid = visible[:rows].astype(BF16)[:, None]
    out_own = links.turn(links.move_rows(cotangent)) * valid
    out_grad = jnp.concatenate([out_own, links.pair(out_own)])
    if links.chips:
        groups = [(slice(0, 2 * units), 2, True), (slice(2 * units, 4 * units), 2, False)]
    else:
        groups = [(slice(0, count * units), count, True)]
    order_back = [order.index(k) for k in range(count)]

    def blocks_of(value):
        return [(value[:, cols], number, x_first) for cols, number, x_first in groups]

    grad_down = links_gradient(links, out_grad, blocks_of(hidden), order)

    down_out = links.merged(
        lambda part: dot_nt(hidden[part * rows : (part + 1) * rows], w_down_all)
    )
    layer_out = (middle + down_out + bias_down).astype(BF16)
    layer_out = links.move_rows(links.turn(layer_out))

    grad_pre = (dot_nn(out_grad, w_down_all) * slope.astype(F32)).astype(BF16)
    grad_up = links_gradient(links, second, blocks_of(grad_pre), order)
    grad_second = links.merged(
        lambda part: dot_nt(grad_pre[part * rows : (part + 1) * rows], w_up_all)
    )
    back_two, grad_gain_two, grad_shift_two = norm_back(middle, gain_two, grad_second)
    grad_middle = out_own.astype(F32) + back_two
    branch_own = grad_middle.astype(BF16)
    branch_grad = jnp.concatenate([branch_own, links.pair(branch_own)])
    grad_heads = [dot_nn(branch_grad, w_out[k]).astype(BF16) for k in range(count)]
    grad_out_w = links_gradient(links, branch_grad, [(heads_all, count, True)], None)
    grad_joined, grad_qkv, sums = [], [], []
    for k in range(count):
        back, sum_k = attend_back(joined[k], grad_heads[k], totals[k], mask[:, None], heads, scaling)
        grad_joined.append(back)
        sums.append(sum_k)
    grad_qkv = links_gradient(
        links, first, [(grad_joined[k], 1, k % 2 == 0) for k in range(count)], None
    )
    grad_all = jnp.concatenate(grad_joined, 1)
    w_qkv_all = jnp.concatenate(w_qkv, 1)
    grad_first = links.merged(
        lambda part: dot_nt(grad_all[part * rows : (part + 1) * rows], w_qkv_all)
    )
    back_one, grad_gain_one, grad_shift_one = norm_back(source, gain_one, grad_first)
    grad_tokens = (grad_middle + back_one).astype(BF16)
    grad_tokens = links.move_rows(links.turn(grad_tokens))

    up_sum = jnp.sum(grad_pre.astype(F32), 0)
    up_pieces = [
        up_sum[order_back[k] * units : (order_back[k] + 1) * units] for k in range(count)
    ]
    early = [links.place(up_pieces).reshape(-1)] + [
        links.turn(v)
        for v in (
            jnp.sum(grad_middle, 0),
            grad_gain_two,
            grad_shift_two,
            jnp.sum(out_own.astype(F32), 0),
        )
    ]
    late = [
        links.place([s[0, :width] for s in sums]).reshape(-1),
        links.place([s[1, :width] for s in sums]).reshape(-1),
        links.turn(grad_gain_one),
        links.turn(grad_shift_one),
    ]

    def summed(vectors):
        whole = links.total(jnp.concatenate(vectors))
        at = 0
        result = []
        for vector in vectors:
            result.append(whole[at : at + vector.shape[0]])
            at += vector.shape[0]
        return result

    sum_up, sum_out, sum_gain_two, sum_shift_two, sum_down = summed(early)
    sum_query, sum_value, sum_gain_one, sum_shift_one = summed(late)

    def own(vector):
        size = vector.shape[0] // count
        return lax.dynamic_slice_in_dim(vector, links.tensor_pos * size, size, 0)

    def flat(piece):
        return piece.reshape(piece.shape[0], -1)

    return (
        layer_out,
        grad_tokens,
        sum_gain_one,
        sum_shift_one,
        flat(grad_qkv[:, :, :width]),
        own(sum_query),
        flat(grad_qkv[:, :, width : 2 * width]),
        flat(grad_qkv[:, :, 2 * width :]),
        own(sum_value),
        flat(grad_out_w).T,
        sum_out,
        sum_gain_two,
        sum_shift_two,
        flat(grad_up),
        own(sum_up),
        flat(grad_down).T,
        sum_down,
    )


def links_gradient(links, left, rights, order):
    if order is None or not links.chips:
        return links.gradient(left, rights)
    blocks = []
    for right, count, x_first in rights:
        product = links.scatter_plane(left, right, x_first)
        size = product.shape[1] // count
        blocks += [product[:, i * size : (i + 1) * size] for i in range(count)]
    return links.own_rows(links.scatter_line([blocks[order.index(k)] for k in range(4)]))


def solution(mesh):
    rows = P(("dp", "tensor"), None)
    wide, tall = P("dp", "tensor"), P("tensor", "dp")
    piece, same = P("tensor"), P()
    return jax.shard_map(
        local,
        mesh=mesh,
        in_specs=(
            rows, P("dp"), rows, same, same, wide, piece, wide, wide, piece, tall, same, same, same,
            wide, piece, tall, same,
        ),
        out_specs=(
            rows, rows, same, same, wide, piece, wide, wide, piece, tall, same, same, same, wide, piece,
            tall, same,
        ),
        check_vma=False,
    )
```

```python
import functools

import jax
import jax.numpy as jnp
from jax import lax
from jax.experimental import pallas as pl
from jax.experimental.pallas import tpu as pltpu
from jax.sharding import PartitionSpec as P

HDIM = 80
EPS = 1e-05
LOG2E = 1.4426950408889634
F32 = jnp.float32
BF16 = jnp.bfloat16


def norm_rows(values, norm_gain, norm_shift):
    center = values - jnp.mean(values, -1, keepdims=True)
    spread = jnp.mean(center * center, -1, keepdims=True)
    return center * lax.rsqrt(spread + EPS) * norm_gain + norm_shift


def norm_back(values, norm_gain, grad):
    center = values - jnp.mean(values, -1, keepdims=True)
    scale = lax.rsqrt(jnp.mean(center * center, -1, keepdims=True) + EPS)
    normed = center * scale
    scaled = grad * norm_gain
    back = scaled - jnp.mean(scaled, -1, keepdims=True)
    back = (back - normed * jnp.mean(scaled * normed, -1, keepdims=True)) * scale
    return back, jnp.sum(grad * normed, 0), jnp.sum(grad, 0)


def dot_nn(left, right):
    return jnp.dot(left, right, preferred_element_type=F32)


def dot_tn(left, right):
    return lax.dot_general(left, right, (((0,), (0,)), ((), ())), preferred_element_type=F32)


def dot_nt(left, right):
    return lax.dot_general(left, right, (((1,), (1,)), ((), ())), preferred_element_type=F32)


def up_kernel(rows_ref, weight_ref, bias_ref, hidden_ref, slope_ref):
    pre = dot_nn(rows_ref[...], weight_ref[...]) + bias_ref[...]
    cdf = 0.5 * lax.erf(pre * (0.5**0.5)) + 0.5
    density = jnp.exp(-0.5 * pre * pre) * 0.3989422804014327
    hidden_ref[...] = (pre * cdf).astype(BF16)
    slope_ref[...] = (cdf + pre * density).astype(BF16)


def up_gelu(rows, weight, bias):
    count, depth = rows.shape
    cols = weight.shape[1]
    block_rows, block_cols = min(512, count), min(640, cols)
    return pl.pallas_call(
        up_kernel,
        grid=(cols // block_cols, count // block_rows),
        in_specs=[
            pl.BlockSpec((block_rows, depth), lambda n, m: (m, 0)),
            pl.BlockSpec((depth, block_cols), lambda n, m: (0, n)),
            pl.BlockSpec((1, block_cols), lambda n, m: (0, n)),
        ],
        out_specs=[
            pl.BlockSpec((block_rows, block_cols), lambda n, m: (m, n)),
            pl.BlockSpec((block_rows, block_cols), lambda n, m: (m, n)),
        ],
        out_shape=[jax.ShapeDtypeStruct((count, cols), BF16)] * 2,
        cost_estimate=pl.CostEstimate(
            flops=2 * count * depth * cols, bytes_accessed=20_000_000, transcendentals=0
        ),
        compiler_params=pltpu.CompilerParams(vmem_limit_bytes=40 << 20),
        name="up_gelu",
    )(rows, weight, bias)


def attend_kernel(heads, scaling, query_ref, all_ref, mask_ref, out_ref, total_ref):
    width = heads * HDIM
    queries = query_ref[...]
    mask = mask_ref[...]
    outs, totals = [], []
    for head in range(heads):
        low = head * HDIM
        query = queries[:, low : low + HDIM]
        key = all_ref[:, width + low : width + low + HDIM]
        value = all_ref[:, 2 * width + low : 2 * width + low + HDIM]
        scores = dot_nt(query, key) * (scaling * LOG2E) + mask
        row_max = jnp.max(scores, -1, keepdims=True)
        exp_scores = jnp.exp2(scores - row_max)
        total = jnp.sum(exp_scores, -1, keepdims=True)
        mixed = dot_nn(exp_scores.astype(BF16), value)
        outs.append(mixed * (1.0 / total))
        totals.append(row_max + jnp.log2(total))
    out_ref[...] = jnp.concatenate(outs, -1).astype(BF16)
    for head in range(heads):
        wide = jnp.broadcast_to(totals[head], (totals[head].shape[0], 128))
        total_ref[head : head + 1, :] = wide.T[0:1, :]


def attend(joined, mask_row, heads, scaling):
    count, cols = joined.shape
    block_rows = min(256, count)
    width = heads * HDIM
    return pl.pallas_call(
        functools.partial(attend_kernel, heads, scaling),
        grid=(count // block_rows,),
        in_specs=[
            pl.BlockSpec((block_rows, cols), lambda m: (m, 0)),
            pl.BlockSpec((count, cols), lambda m: (0, 0)),
            pl.BlockSpec((1, count), lambda m: (0, 0)),
        ],
        out_specs=[
            pl.BlockSpec((block_rows, width), lambda m: (m, 0)),
            pl.BlockSpec((heads, block_rows), lambda m: (0, m)),
        ],
        out_shape=[
            jax.ShapeDtypeStruct((count, width), BF16),
            jax.ShapeDtypeStruct((heads, count), F32),
        ],
        cost_estimate=pl.CostEstimate(
            flops=2 * heads * count * count * 512,
            bytes_accessed=4_000_000,
            transcendentals=heads * count * count,
        ),
        compiler_params=pltpu.CompilerParams(vmem_limit_bytes=48 << 20),
        name="attend",
    )(joined, joined, mask_row)


def attend_back_kernel(
    heads, scaling, query_ref, all_ref, grad_ref, total_ref, mask_ref,
    out_ref, sums_ref, key_sum, value_sum,
):
    step = pl.program_id(0)
    steps = pl.num_programs(0)
    width = heads * HDIM
    block_rows = query_ref.shape[0]

    @pl.when(step == 0)
    def _():
        key_sum[...] = jnp.zeros_like(key_sum)
        value_sum[...] = jnp.zeros_like(value_sum)
        sums_ref[...] = jnp.zeros_like(sums_ref)

    queries = query_ref[...]
    grads = grad_ref[...]
    query_outs = []
    for head in range(heads):
        low = head * HDIM
        query = queries[:, low : low + HDIM]
        grad = grads[:, low : low + HDIM]
        key = all_ref[:, width + low : width + low + HDIM]
        value = all_ref[:, 2 * width + low : 2 * width + low + HDIM]
        scores = dot_nt(key, query) * (scaling * LOG2E) + mask_ref[...]
        probs = jnp.exp2(scores - total_ref[head : head + 1, :])
        grad_probs = dot_nt(value, grad)
        shared = jnp.sum(probs * grad_probs, 0, keepdims=True)
        grad_scores = (probs * (grad_probs - shared)).astype(BF16)
        value_sum[head, :, :HDIM] += dot_nn(probs.astype(BF16), grad)
        key_sum[head, :, :HDIM] += dot_nn(grad_scores, query)
        query_outs.append(dot_tn(grad_scores, key) * scaling)
    joined = jnp.concatenate(query_outs, -1)
    sums_ref[0:1, :width] += jnp.sum(joined, 0, keepdims=True)
    rows = pl.ds(pl.multiple_of(step * block_rows, block_rows), block_rows)
    out_ref[rows, :width] = joined.astype(BF16)

    @pl.when(step == steps - 1)
    def _():
        keys = jnp.concatenate([key_sum[head, :, :HDIM] for head in range(heads)], -1)
        values = jnp.concatenate([value_sum[head, :, :HDIM] for head in range(heads)], -1)
        sums_ref[1:2, :width] = jnp.sum(values, 0, keepdims=True)
        out_ref[:, width:] = jnp.concatenate([keys * scaling, values], -1).astype(BF16)


def attend_back(joined, grad_heads, totals, mask_col, heads, scaling):
    count, cols = joined.shape
    block_rows = min(256, count)
    width = heads * HDIM
    return pl.pallas_call(
        functools.partial(attend_back_kernel, heads, scaling),
        grid=(count // block_rows,),
        in_specs=[
            pl.BlockSpec((block_rows, cols), lambda m: (m, 0)),
            pl.BlockSpec((count, cols), lambda m: (0, 0)),
            pl.BlockSpec((block_rows, width), lambda m: (m, 0)),
            pl.BlockSpec((heads, block_rows), lambda m: (0, m)),
            pl.BlockSpec((count, 1), lambda m: (0, 0)),
        ],
        out_specs=[
            pl.BlockSpec((count, cols), lambda m: (0, 0)),
            pl.BlockSpec((8, 256), lambda m: (0, 0)),
        ],
        out_shape=[
            jax.ShapeDtypeStruct((count, cols), BF16),
            jax.ShapeDtypeStruct((8, 256), F32),
        ],
        scratch_shapes=[
            pltpu.VMEM((heads, count, 128), F32),
            pltpu.VMEM((heads, count, 128), F32),
        ],
        cost_estimate=pl.CostEstimate(
            flops=2 * heads * count * count * 1280,
            bytes_accessed=5_000_000,
            transcendentals=heads * count * count,
        ),
        compiler_params=pltpu.CompilerParams(vmem_limit_bytes=56 << 20),
        name="attend_back",
    )(joined, joined, grad_heads, totals, mask_col)


UNIT = 320
SPAN = 640
TURNS = 4


def clamp_rows(ref, start, size):
    return ref.at[pl.ds(pl.multiple_of(start, 16), size)]


def forward_kernel(
    scaling,
    attn_shard, up_shard, down_shard, tokens, cotangent, mask_in, bias_in,
    gain_one, shift_one, gain_two, shift_two, bias_out,
    w_attn_out, w_up_out, w_down, tokens_out, cot_out, mask_out, first_out, second_out, joined_out,
    heads_out, totals_out, middle_out, hidden_out, slope_out,
    w_attn, w_up, tok, first, second, joined, heads, middle, send_rows, got_rows, hidden, slope,
    mask, totals, bias, send_sem, recv_sem, local_sem,
):
    dp, z = lax.axis_index("dp"), lax.axis_index("tensor")
    core, plane = lax.rem(dp, 2), lax.div(dp, 2)
    x_bit, y_bit = lax.rem(plane, 2), lax.div(plane, 2)
    half = tok.shape[0]
    count = 2 * half
    to_x = (y_bit * 4 + (1 - x_bit) * 2 + core, z)
    to_y = ((1 - y_bit) * 4 + x_bit * 2 + core, z)
    to_core = (plane * 2 + 1 - core, z)
    to_clip = (plane * 2 + 1 - core, z + 1 - 2 * lax.rem(z, 2))
    to_z = [(dp, lax.rem(z + k, TURNS)) for k in range(TURNS)]
    moves = core != lax.rem(z, 2)
    plane_x = y_bit * 2 + 1 - x_bit
    plane_y = (1 - y_bit) * 2 + x_bit
    plane_xy = (1 - y_bit) * 2 + 1 - x_bit
    turn = [lax.rem(z + TURNS - k, TURNS) for k in range(TURNS)]

    barrier = pltpu.get_barrier_semaphore()
    partners = [to_x, to_y, to_core, to_clip] + to_z[1:]
    for partner in partners:
        pl.semaphore_signal(barrier, inc=1, device_id=partner, device_id_type=pl.DeviceIdType.MESH)
    pl.semaphore_wait(barrier, len(partners))

    def remote(source, target, sem, device):
        return pltpu.make_async_remote_copy(
            src_ref=source,
            dst_ref=target,
            send_sem=send_sem.at[sem],
            recv_sem=recv_sem.at[sem],
            device_id=device,
            device_id_type=pl.DeviceIdType.MESH,
        )

    sent = []

    def send(source, target, sem, device):
        copy = remote(source, target, sem, device)
        copy.start()
        sent.append(copy)

    def arrived(target, sem):
        remote(target, target, sem, to_core).wait_recv()

    weights = [w_attn, w_up, w_down]
    shards = [attn_shard, up_shard, down_shard]

    def block(array, k, place):
        return weights[array].at[
            pl.ds(pl.multiple_of(place * UNIT, 16), UNIT),
            pl.ds(pl.multiple_of(turn[k] * SPAN, 128), SPAN),
        ]

    def own_half(array, which):
        rows = UNIT // 2
        return weights[array].at[
            pl.ds(pl.multiple_of(plane * UNIT + which * rows, 16), rows),
            pl.ds(pl.multiple_of(z * SPAN, 128), SPAN),
        ]

    def pair_start(array):
        send(shards[array].at[1 - core], own_half(array, core), 48 + array, to_core)
        copy = pltpu.make_async_copy(
            shards[array].at[core], own_half(array, core), local_sem.at[array]
        )
        copy.start()
        return copy

    def pair_wait(array, copy):
        copy.wait()
        arrived(own_half(array, 1 - core), 48 + array)

    def go_plane(array, k):
        send(block(array, k, plane), block(array, k, plane), 16 * array + 4 + k, to_x)
        send(block(array, k, plane), block(array, k, plane), 16 * array + 8 + k, to_y)

    def go_line(array):
        for k in range(1, TURNS):
            send(block(array, 0, plane), block(array, 0, plane), 16 * array + k, to_z[k])

    def from_line(array, k):
        arrived(block(array, k, plane), 16 * array + k)
        go_plane(array, k)

    def forward_on(array, k):
        if k % 2 == 0:
            arrived(block(array, k, plane_x), 16 * array + 4 + k)
            send(block(array, k, plane_x), block(array, k, plane_x), 16 * array + 12 + k, to_y)
        else:
            arrived(block(array, k, plane_y), 16 * array + 8 + k)
            send(block(array, k, plane_y), block(array, k, plane_y), 16 * array + 12 + k, to_x)

    def complete(array, k):
        if k % 2 == 0:
            arrived(block(array, k, plane_y), 16 * array + 8 + k)
        else:
            arrived(block(array, k, plane_x), 16 * array + 4 + k)
        arrived(block(array, k, plane_xy), 16 * array + 12 + k)

    pairs = [pair_start(0)]
    tok_copy = pltpu.make_async_copy(tokens, tok, local_sem.at[3])
    mask_copy = pltpu.make_async_copy(mask_in, mask, local_sem.at[4])
    clip_tok = remote(tokens, tok, 51, to_clip)
    clip_mask = remote(mask_in, mask, 52, to_clip)
    cot_copy = pltpu.make_async_copy(cotangent, cot_out, local_sem.at[5])
    clip_cot = remote(cotangent, cot_out, 59, to_clip)

    @pl.when(moves)
    def _():
        clip_mask.start()
        clip_tok.start()

    @pl.when(jnp.logical_not(moves))
    def _():
        tok_copy.start()
        mask_copy.start()

    bias_copy = pltpu.make_async_copy(bias_in, bias.at[z], local_sem.at[6])
    bias_copy.start()
    for k in range(1, TURNS):
        send(bias_in, bias.at[z], 52 + k, to_z[k])
    pairs += [pair_start(1), pair_start(2)]
    pair_wait(0, pairs[0])
    go_plane(0, 0)
    go_line(0)
    pair_wait(1, pairs[1])
    go_plane(1, 0)
    pair_wait(2, pairs[2])

    @pl.when(moves)
    def _():
        clip_mask.wait()
        clip_tok.wait()

    @pl.when(jnp.logical_not(moves))
    def _():
        tok_copy.wait()
        mask_copy.wait()

    outs = []

    def put(source, target, sem):
        copy = pltpu.make_async_copy(source, target, local_sem.at[sem])
        copy.start()
        outs.append(copy)
        return copy

    put(tok, tokens_out, 7)
    put(mask, mask_out, 8)
    base = pl.multiple_of(core * half, 256)
    other = pl.multiple_of((1 - core) * half, 256)

    def norm_loop(step, _):
        rows = pl.ds(pl.multiple_of(step * 256, 256), 256)
        values = tok[rows, :].astype(F32)
        normed = norm_rows(values, gain_one[...], shift_one[...])
        first[pl.ds(pl.multiple_of(base + step * 256, 256), 256), :] = normed.astype(BF16)
        return 0

    lax.fori_loop(0, half // 256, norm_loop, 0)
    own_rows, other_rows = pl.ds(base, half), pl.ds(other, half)
    send(first.at[own_rows], first.at[own_rows], 56, to_core)
    forward_on(0, 0)
    arrived(first.at[other_rows], 56)
    put(first, first_out, 9)
    bias_copy.wait()
    for k in range(1, TURNS):
        arrived(bias.at[turn[k]], 52 + k)
    forward_on(1, 0)
    for k in range(1, TURNS):
        from_line(0, k)
    go_line(1)

    def project(k):
        complete(0, k)
        columns = pl.ds(pl.multiple_of(turn[k] * SPAN, 128), 480)

        def step_rows(step, _):
            rows = pl.ds(pl.multiple_of(step * half, half), half)
            product = dot_nn(first[rows, :], w_attn[:, columns]) + bias[turn[k], 0:1, :480]
            joined[k, rows, :] = product.astype(BF16)
            return 0

        lax.fori_loop(0, 2, step_rows, 0)
        put(joined.at[k], joined_out.at[turn[k]], 10 + k)

    def attention(k, part):
        def step_rows(step, _):
            rows = pl.ds(pl.multiple_of(step * 256, 256), 256)
            queries = joined[k, rows, :]
            mixes, logs = [jnp.zeros((256, 96), F32)], []
            for head in range(2):
                low = head * HDIM
                query = queries[:, low : low + HDIM]
                key = joined[k, :, 160 + low : 160 + low + HDIM]
                value = joined[k, :, 320 + low : 320 + low + HDIM]
                scores = dot_nt(query, key) * (scaling * LOG2E) + mask[0:1, :]
                row_max = jnp.max(scores, -1, keepdims=True)
                exp_scores = jnp.exp2(scores - row_max)
                total = jnp.sum(exp_scores, -1, keepdims=True)
                mixes.append(dot_nn(exp_scores.astype(BF16), value) * (1.0 / total))
                logs.append(row_max + jnp.log2(total))
            heads[k, rows, :] = jnp.concatenate(mixes, -1).astype(BF16)
            for head in range(2):
                wide = jnp.broadcast_to(logs[head], (256, 128))
                totals[k, head : head + 1, rows] = wide.T[0:1, :]
            return 0

        lax.fori_loop(3 * part, 3 * part + 3, step_rows, 0)
        if part == 1:
            put(heads.at[k], heads_out.at[turn[k]], 14 + k)
            put(totals.at[k], totals_out.at[turn[k]], 18 + k)

    project(0)
    attention(0, 0)
    forward_on(0, 1)
    attention(0, 1)
    forward_on(0, 2)
    forward_on(0, 3)
    project(1)
    attention(1, 0)
    for k in range(1, TURNS):
        from_line(1, k)
    go_plane(2, 0)
    go_line(2)

    @pl.when(moves)
    def _():
        clip_cot.start()

    @pl.when(jnp.logical_not(moves))
    def _():
        cot_copy.start()

    attention(1, 1)
    project(2)
    attention(2, 0)
    forward_on(1, 1)
    forward_on(1, 2)
    attention(2, 1)
    forward_on(1, 3)
    project(3)
    put(w_attn, w_attn_out, 22)
    attention(3, 0)
    forward_on(2, 0)
    attention(3, 1)

    def branch(rows):
        total = None
        for k in range(TURNS):
            columns = pl.ds(pl.multiple_of(turn[k] * SPAN + 384, 128), 256)
            product = dot_nt(heads[k, rows, :], w_attn[:, columns])
            total = product if total is None else total + product
        return total

    def branch_other(step, _):
        rows = pl.ds(pl.multiple_of(other + step * 256, 256), 256)
        send_rows[pl.ds(pl.multiple_of(step * 256, 256), 256), :] = branch(rows).astype(BF16)
        return 0

    lax.fori_loop(0, half // 256, branch_other, 0)
    send(send_rows, got_rows, 57, to_core)
    for k in range(1, TURNS):
        from_line(2, k)

    def branch_own(step, _):
        rows = pl.ds(pl.multiple_of(base + step * 256, 256), 256)
        low = pl.ds(pl.multiple_of(step * 256, 256), 256)
        middle[low, :] = branch(rows) + tok[low, :].astype(F32) + bias_out[...]
        return 0

    lax.fori_loop(0, half // 256, branch_own, 0)
    arrived(got_rows, 57)

    def norm_two(step, _):
        low = pl.ds(pl.multiple_of(step * 256, 256), 256)
        values = middle[low, :] + got_rows[low, :].astype(F32)
        middle[low, :] = values
        normed = norm_rows(values, gain_two[...], shift_two[...])
        second[pl.ds(pl.multiple_of(base + step * 256, 256), 256), :] = normed.astype(BF16)
        return 0

    lax.fori_loop(0, half // 256, norm_two, 0)
    send(second.at[own_rows], second.at[own_rows], 58, to_core)
    put(middle, middle_out, 23)
    forward_on(2, 1)
    arrived(second.at[other_rows], 58)
    put(second, second_out, 24)

    waits = [None, None]

    def lift(k):
        complete(1, k)
        slot = k % 2
        if waits[slot] is not None:
            for copy in waits[slot]:
                copy.wait()
        columns = pl.ds(pl.multiple_of(turn[k] * SPAN, 128), SPAN)

        def step_rows(step, _):
            rows = pl.ds(pl.multiple_of(step * 256, 256), 256)
            pre = dot_nn(second[rows, :], w_up[:, columns]) + bias[turn[k], 1:2, :]
            cdf = 0.5 * lax.erf(pre * (0.5**0.5)) + 0.5
            density = jnp.exp(-0.5 * pre * pre) * 0.3989422804014327
            hidden[slot, rows, :] = (pre * cdf).astype(BF16)
            slope[slot, rows, :] = (cdf + pre * density).astype(BF16)
            return 0

        lax.fori_loop(0, count // 256, step_rows, 0)
        waits[slot] = [
            put(hidden.at[slot], hidden_out.at[:, columns], 25 + slot),
            put(slope.at[slot], slope_out.at[:, columns], 27 + slot),
        ]
        for _ in range(2):
            outs.pop()

    lift(0)
    forward_on(2, 2)
    lift(1)
    forward_on(2, 3)
    lift(2)
    lift(3)
    put(w_up, w_up_out, 29)
    for k in range(TURNS):
        complete(2, k)

    @pl.when(moves)
    def _():
        clip_cot.wait()

    @pl.when(jnp.logical_not(moves))
    def _():
        cot_copy.wait()

    for copy in outs + waits[0] + waits[1]:
        copy.wait()
    for copy in sent:
        copy.wait_send()


def forward_pass(
    shards, tokens, cotangent, mask, bias, gain_one, shift_one, gain_two, shift_two, bias_out
):
    half, features = tokens.shape
    count = 2 * half
    any_space = pl.BlockSpec(memory_space=pl.ANY)
    vmem = pl.BlockSpec(memory_space=pltpu.VMEM)
    wide = (features, TURNS * SPAN)
    shapes = [
        (wide, BF16), (wide, BF16), (wide, BF16), ((half, features), BF16), ((half, features), BF16),
        ((8, count), F32), ((count, features), BF16), ((count, features), BF16),
        ((TURNS, count, 480), BF16), ((TURNS, count, 256), BF16), ((TURNS, 8, count), F32),
        ((half, features), F32), ((count, TURNS * SPAN), BF16), ((count, TURNS * SPAN), BF16),
    ]
    return pl.pallas_call(
        functools.partial(forward_kernel, HDIM ** (-0.5)),
        in_specs=[any_space] * 7 + [vmem] * 5,
        out_specs=[any_space] * len(shapes),
        out_shape=[jax.ShapeDtypeStruct(shape, kind) for shape, kind in shapes],
        scratch_shapes=[
            pltpu.VMEM(wide, BF16),
            pltpu.VMEM(wide, BF16),
            pltpu.VMEM((half, features), BF16),
            pltpu.VMEM((count, features), BF16),
            pltpu.VMEM((count, features), BF16),
            pltpu.VMEM((TURNS, count, 480), BF16),
            pltpu.VMEM((TURNS, count, 256), BF16),
            pltpu.VMEM((half, features), F32),
            pltpu.VMEM((half, features), BF16),
            pltpu.VMEM((half, features), BF16),
            pltpu.VMEM((2, count, SPAN), BF16),
            pltpu.VMEM((2, count, SPAN), BF16),
            pltpu.VMEM((8, count), F32),
            pltpu.VMEM((TURNS, 8, count), F32),
            pltpu.VMEM((TURNS, 8, SPAN), F32),
            pltpu.SemaphoreType.DMA((64,)),
            pltpu.SemaphoreType.DMA((64,)),
            pltpu.SemaphoreType.DMA((32,)),
        ],
        cost_estimate=pl.CostEstimate(
            flops=2 * count * features * 6400, bytes_accessed=80_000_000, transcendentals=30_000_000
        ),
        compiler_params=pltpu.CompilerParams(
            vmem_limit_bytes=60 << 20, collective_id=0, has_side_effects=True
        ),
        name="forward_pass",
    )(*shards, tokens, cotangent, mask, bias, gain_one, shift_one, gain_two, shift_two, bias_out)


class Links:
    def __init__(self):
        self.dp = lax.axis_size("dp")
        self.tensor = lax.axis_size("tensor")
        self.tensor_pos = lax.axis_index("tensor")
        self.half = self.tensor_pos % 2

    def pair(self, value):
        return lax.ppermute(value, "tensor", [(i, i ^ 1) for i in range(self.tensor)])

    def columns(self, shard):
        rows, _, width = shard.shape
        whole = lax.all_gather(shard, ("dp", "tensor"), axis=0)
        whole = lax.dynamic_index_in_dim(whole, self.half, 2, keepdims=False)
        whole = whole.reshape(self.dp, self.tensor, rows, width)
        return [whole[:, k].reshape(self.dp * rows, width) for k in range(self.tensor)]

    def vectors(self, value):
        whole = lax.all_gather(value, "tensor", axis=0)
        return [whole[k] for k in range(self.tensor)]

    def place(self, pieces):
        halves = (jnp.arange(2) == self.half)[None, :, None]
        return jnp.where(halves, jnp.stack(pieces)[:, None, :], 0.0)

    def gradient(self, left, rights):
        whole = jnp.stack([dot_tn(left, right).astype(BF16) for right in rights], 0)
        features, width = whole.shape[1:]
        whole = whole.reshape(self.tensor, self.dp, features // self.dp, width)
        whole = jnp.moveaxis(whole, 1, 0)[:, :, :, None, :]
        halves = (jnp.arange(2) == self.half)[None, None, None, :, None]
        whole = jnp.where(halves, whole, jnp.zeros((), BF16))
        whole = whole.reshape((self.dp * self.tensor,) + whole.shape[2:])
        return lax.psum_scatter(whole, ("dp", "tensor"), tiled=False).astype(F32)

    def merged(self, partial_of):
        got = self.pair(partial_of(1).astype(BF16))
        return partial_of(0) + got.astype(F32)


def summed(vectors, total):
    whole = total(jnp.concatenate(vectors))
    at = 0
    result = []
    for vector in vectors:
        result.append(whole[at : at + vector.shape[0]])
        at += vector.shape[0]
    return result


def halves_of(weight):
    return weight.reshape(weight.shape[0], 2, weight.shape[1] // 2)


def flat(piece):
    return piece.reshape(piece.shape[0], -1)


def local_any(
    tokens,
    lengths,
    cotangent,
    norm1_gain,
    norm1_shift,
    query_weight,
    query_bias,
    key_weight,
    value_weight,
    value_bias,
    out_weight,
    out_bias,
    norm2_gain,
    norm2_shift,
    up_weight,
    up_bias,
    down_weight,
    down_bias,
):
    links = Links()
    rows = tokens.shape[0]
    scaling = HDIM ** (-0.5)
    width = query_weight.shape[1] // 2
    heads = width // HDIM
    units = up_weight.shape[1] // 2
    count = links.tensor

    shard_attn = [query_weight, key_weight, value_weight, out_weight.T]
    w_attn = links.columns(jnp.concatenate([halves_of(w) for w in shard_attn], -1))
    w_up = jnp.concatenate(links.columns(halves_of(up_weight)), 1)
    w_down = jnp.concatenate(links.columns(halves_of(down_weight.T)), 1)
    w_qkv = [block[:, : 3 * width] for block in w_attn]
    w_out = [block[:, 3 * width :] for block in w_attn]
    small = [query_bias.reshape(2, width), value_bias.reshape(2, width), up_bias.reshape(2, units)]
    small = jnp.concatenate(small, -1)
    small = links.vectors(jnp.where(links.half == 0, small[0], small[1]))
    bias_qkv = [
        jnp.concatenate([v[:width], jnp.zeros((width,), F32), v[width : 2 * width]]) for v in small
    ]
    bias_up = jnp.concatenate([v[2 * width :] for v in small])

    place = links.tensor_pos // 2
    clip_length = jnp.sum(jnp.where(jnp.arange(lengths.shape[0]) == place, lengths, 0))
    frames = jnp.arange(rows)
    frames = jnp.concatenate([links.half * rows + frames, (1 - links.half) * rows + frames])
    visible = frames < clip_length
    mask = jnp.where(visible, 0.0, -1e30).astype(F32)

    def part_of(value, part):
        return value[part * rows : (part + 1) * rows]

    def both(value):
        return jnp.concatenate([value, links.pair(value)])

    source = tokens.astype(F32)
    first = both(norm_rows(source, norm1_gain, norm1_shift).astype(BF16))
    joined, heads_out, totals = [], [], []
    for k in range(count):
        joined.append((dot_nn(first, w_qkv[k]) + bias_qkv[k]).astype(BF16))
        mixed, total = attend(joined[k], mask[None, :], heads, scaling)
        heads_out.append(mixed)
        totals.append(total)
    heads_all = jnp.concatenate(heads_out, 1)
    w_out_all = jnp.concatenate(w_out, 1)
    branch = links.merged(lambda part: dot_nt(part_of(heads_all, part), w_out_all))
    middle = source + branch + out_bias
    second = both(norm_rows(middle, norm2_gain, norm2_shift).astype(BF16))
    hidden, slope = up_gelu(second, w_up, bias_up[None, :])
    out_own = cotangent * visible[:rows].astype(BF16)[:, None]
    out_grad = both(out_own)

    def cut(value):
        return [value[:, k * units : (k + 1) * units] for k in range(count)]

    grad_down = links.gradient(out_grad, cut(hidden))
    down_out = links.merged(lambda part: dot_nt(part_of(hidden, part), w_down))
    layer_out = (middle + down_out + down_bias).astype(BF16)
    grad_pre = (dot_nn(out_grad, w_down) * slope.astype(F32)).astype(BF16)
    grad_up = links.gradient(second, cut(grad_pre))
    grad_second = links.merged(lambda part: dot_nt(part_of(grad_pre, part), w_up))
    back_two, grad_gain_two, grad_shift_two = norm_back(middle, norm2_gain, grad_second)
    grad_middle = out_own.astype(F32) + back_two
    branch_grad = both(grad_middle.astype(BF16))
    grad_heads = [dot_nn(branch_grad, w_out[k]).astype(BF16) for k in range(count)]
    grad_out_w = links.gradient(branch_grad, heads_out)
    grad_joined, sums = [], []
    for k in range(count):
        back, sum_k = attend_back(joined[k], grad_heads[k], totals[k], mask[:, None], heads, scaling)
        grad_joined.append(back)
        sums.append(sum_k)
    grad_qkv = links.gradient(first, grad_joined)
    grad_all = jnp.concatenate(grad_joined, 1)
    w_qkv_all = jnp.concatenate(w_qkv, 1)
    grad_first = links.merged(lambda part: dot_nt(part_of(grad_all, part), w_qkv_all))
    back_one, grad_gain_one, grad_shift_one = norm_back(source, norm1_gain, grad_first)
    grad_tokens = (grad_middle + back_one).astype(BF16)

    vectors = [
        links.place([v[0] for v in cut(jnp.sum(grad_pre.astype(F32), 0)[None, :])]).reshape(-1),
        links.place([s[0, :width] for s in sums]).reshape(-1),
        links.place([s[1, :width] for s in sums]).reshape(-1),
        grad_gain_one,
        grad_shift_one,
        jnp.sum(grad_middle, 0),
        grad_gain_two,
        grad_shift_two,
        jnp.sum(out_own.astype(F32), 0),
    ]
    sum_up, sum_query, sum_value, *rest = summed(
        vectors, lambda value: lax.psum(value, ("dp", "tensor"))
    )
    sum_gain_one, sum_shift_one, sum_out, sum_gain_two, sum_shift_two, sum_down = rest

    def own(vector):
        size = vector.shape[0] // count
        return lax.dynamic_slice_in_dim(vector, links.tensor_pos * size, size, 0)

    return (
        layer_out,
        grad_tokens,
        sum_gain_one,
        sum_shift_one,
        flat(grad_qkv[:, :, :width]),
        own(sum_query),
        flat(grad_qkv[:, :, width : 2 * width]),
        flat(grad_qkv[:, :, 2 * width :]),
        own(sum_value),
        flat(grad_out_w).T,
        sum_out,
        sum_gain_two,
        sum_shift_two,
        flat(grad_up),
        own(sum_up),
        flat(grad_down).T,
        sum_down,
    )


def local_chips(
    tokens,
    lengths,
    cotangent,
    norm1_gain,
    norm1_shift,
    query_weight,
    query_bias,
    key_weight,
    value_weight,
    value_bias,
    out_weight,
    out_bias,
    norm2_gain,
    norm2_shift,
    up_weight,
    up_bias,
    down_weight,
    down_bias,
):
    dp, z = lax.axis_index("dp"), lax.axis_index("tensor")
    core, plane = dp % 2, dp // 2
    half = tokens.shape[0]
    count = 2 * half
    scaling = HDIM ** (-0.5)
    width, units = 160, SPAN

    def split(weight):
        return jnp.moveaxis(halves_of(weight), 1, 0)

    shards = (
        jnp.concatenate([split(w) for w in (query_weight, key_weight, value_weight, out_weight.T)], -1),
        split(up_weight),
        split(down_weight.T),
    )
    place = jnp.sum(jnp.where(jnp.arange(lengths.shape[0]) == z // 2, lengths, 0))
    mask = jnp.where(jnp.arange(count) < place, 0.0, -1e30).astype(F32)
    mask = jnp.broadcast_to(mask[None, :], (8, count))
    small = [query_bias.reshape(2, width), jnp.zeros((2, width), F32), value_bias.reshape(2, width)]
    small = jnp.concatenate(small + [jnp.zeros((2, width), F32)], -1)
    small = jnp.stack([small, up_bias.reshape(2, units)], 1)
    small = jnp.pad(jnp.where(core == 0, small[0], small[1]), ((0, 6), (0, 0)))
    (
        w_attn, w_up, w_down, tok, cot, mask, first, second, joined, heads, totals, middle, hidden, slope,
    ) = forward_pass(
        shards, tokens, cotangent, mask, small,
        norm1_gain[None, :], norm1_shift[None, :], norm2_gain[None, :], norm2_shift[None, :],
        out_bias[None, :],
    )

    def pair(value):
        return lax.ppermute(value, "dp", [(i, i ^ 1) for i in range(8)])

    def along_x(value):
        return lax.ppermute(value, "dp", [(i, i ^ 2) for i in range(8)])

    def along_y(value):
        return lax.ppermute(value, "dp", [(i, i ^ 4) for i in range(8)])

    def along_z(value, shift):
        return lax.ppermute(value, "tensor", [(i, (i + shift) % 4) for i in range(4)])

    def move_rows(value):
        swaps = [
            (a * 4 + b, (a ^ 1) * 4 + (b ^ 1)) for a in range(8) for b in range(4) if a % 2 != b % 2
        ]
        moved = lax.ppermute(value, ("dp", "tensor"), swaps)
        return jnp.where(core == z % 2, value, moved)

    def part_of(value, part):
        start = (core if part == 0 else 1 - core) * half
        return lax.dynamic_slice_in_dim(value, start, half, 0)

    def both(value):
        got = pair(value)
        first_one = core == 0
        return jnp.concatenate([jnp.where(first_one, value, got), jnp.where(first_one, got, value)])

    def merged(partial_of):
        got = pair(partial_of(1).astype(BF16))
        return partial_of(0) + got.astype(F32)

    def scatter(left, right, x_first, blocks):
        def part(index):
            columns = lax.dynamic_slice_in_dim(left, (plane ^ index) * UNIT, UNIT, 1)
            return dot_tn(columns, right)

        near, far = (1, 2) if x_first else (2, 1)
        go, follow = (along_x, along_y) if x_first else (along_y, along_x)
        sent_far = go(part(3).astype(BF16))
        sent_near = go(part(near).astype(BF16))
        second_part = (part(far) + sent_far.astype(F32)).astype(BF16)
        first_part = part(0) + sent_near.astype(F32)
        product = (first_part + follow(second_part).astype(F32)).astype(BF16)
        size = product.shape[1] // blocks
        return [product[:, i * size : (i + 1) * size] for i in range(blocks)]

    def finish(blocks):
        stacked = jnp.stack(blocks)
        picked = [
            lax.dynamic_index_in_dim(stacked, (z - k) % 4, 0, keepdims=False) for k in range(4)
        ]
        total = picked[0].astype(F32)
        for k in range(1, 4):
            total = total + along_z(picked[k], -k).astype(F32)
        rows = UNIT // 2
        first_one = core == 0
        keep = jnp.where(first_one, total[:rows], total[rows:])
        got = pair(jnp.where(first_one, total[rows:], total[:rows]))
        return jnp.where(first_one, jnp.stack([keep, got], 1), jnp.stack([got, keep], 1))

    def gradient(left, right):
        cut = right.shape[1] // 2
        return finish(
            scatter(left, right[:, :cut], True, 2) + scatter(left, right[:, cut:], False, 2)
        )

    def total(value):
        for bit in (1, 2, 4):
            value = value + lax.ppermute(value, "dp", [(i, i ^ bit) for i in range(8)])
        for bit in (1, 2):
            value = value + lax.ppermute(value, "tensor", [(i, i ^ bit) for i in range(4)])
        return value

    def spread(pieces):
        halves = (jnp.arange(2) == core)[None, :, None]
        return jnp.where(halves, jnp.stack(pieces)[:, None, :], 0.0).reshape(-1)

    source = tok.astype(F32)
    valid = (part_of(mask[0], 0) == 0.0).astype(BF16)[:, None]
    out_own = cot * valid
    out_grad = both(out_own)
    grad_down = gradient(out_grad, hidden)
    down_out = merged(lambda part: dot_nt(part_of(hidden, part), w_down))
    layer_out = move_rows((middle + down_out + down_bias).astype(BF16))
    grad_pre = (dot_nn(out_grad, w_down) * slope.astype(F32)).astype(BF16)
    grad_up = gradient(second, grad_pre)
    grad_second = merged(lambda part: dot_nt(part_of(grad_pre, part), w_up))
    back_two, grad_gain_two, grad_shift_two = norm_back(middle, norm2_gain, grad_second)
    grad_middle = out_own.astype(F32) + back_two
    branch_grad = both(grad_middle.astype(BF16))
    w_qkv = [w_attn[:, k * SPAN : k * SPAN + 480] for k in range(4)]
    w_out = [w_attn[:, k * SPAN + 480 : (k + 1) * SPAN] for k in range(4)]
    grad_heads = [dot_nn(branch_grad, w_out[k]).astype(BF16) for k in range(4)]
    heads_all = jnp.concatenate([heads[k, :, 96:] for k in range(4)], 1)
    grad_out_w = finish(scatter(branch_grad, heads_all, True, 4))
    grad_joined, sums = [], []
    for k in range(4):
        back, sum_k = attend_back(
            joined[k], grad_heads[k], totals[k, :2], mask[0][:, None], 2, scaling
        )
        grad_joined.append(back)
        sums.append(sum_k)
    grad_qkv = finish(
        [scatter(first, grad_joined[k], k % 2 == 0, 1)[0] for k in range(4)]
    )
    grad_all = jnp.concatenate(grad_joined, 1)
    w_qkv_all = jnp.concatenate(w_qkv, 1)
    grad_first = merged(lambda part: dot_nt(part_of(grad_all, part), w_qkv_all))
    back_one, grad_gain_one, grad_shift_one = norm_back(source, norm1_gain, grad_first)
    grad_tokens = move_rows((grad_middle + back_one).astype(BF16))

    up_sum = jnp.sum(grad_pre.astype(F32), 0)
    sum_up, sum_out, sum_gain_two, sum_shift_two, sum_down = summed(
        [
            spread([up_sum[k * units : (k + 1) * units] for k in range(4)]),
            jnp.sum(grad_middle, 0),
            grad_gain_two,
            grad_shift_two,
            jnp.sum(out_own.astype(F32), 0),
        ],
        total,
    )
    sum_query, sum_value, sum_gain_one, sum_shift_one = summed(
        [
            spread([s[0, :width] for s in sums]),
            spread([s[1, :width] for s in sums]),
            grad_gain_one,
            grad_shift_one,
        ],
        total,
    )

    def own(vector):
        size = vector.shape[0] // 4
        return lax.dynamic_slice_in_dim(vector, z * size, size, 0)

    return (
        layer_out,
        grad_tokens,
        sum_gain_one,
        sum_shift_one,
        flat(grad_qkv[:, :, :width]),
        own(sum_query),
        flat(grad_qkv[:, :, width : 2 * width]),
        flat(grad_qkv[:, :, 2 * width :]),
        own(sum_value),
        flat(grad_out_w).T,
        sum_out,
        sum_gain_two,
        sum_shift_two,
        flat(grad_up),
        own(sum_up),
        flat(grad_down).T,
        sum_down,
    )


def solution(mesh):
    rows = P(("dp", "tensor"), None)
    wide, tall = P("dp", "tensor"), P("tensor", "dp")
    piece, same = P("tensor"), P()
    chips = mesh.shape["dp"] == 8 and mesh.shape["tensor"] == 4
    return jax.shard_map(
        local_chips if chips else local_any,
        mesh=mesh,
        in_specs=(
            rows, P("dp"), rows, same, same, wide, piece, wide, wide, piece, tall, same, same, same,
            wide, piece, tall, same,
        ),
        out_specs=(
            rows, rows, same, same, wide, piece, wide, wide, piece, tall, same, same, same, wide, piece,
            tall, same,
        ),
        check_vma=False,
    )
```

```python
import functools

import jax
import jax.numpy as jnp
from jax import lax
from jax.experimental import pallas as pl
from jax.experimental.pallas import tpu as pltpu
from jax.sharding import PartitionSpec as P

HDIM = 80
EPS = 1e-05
LOG2E = 1.4426950408889634
F32 = jnp.float32
BF16 = jnp.bfloat16


def norm_rows(values, norm_gain, norm_shift):
    center = values - jnp.mean(values, -1, keepdims=True)
    spread = jnp.mean(center * center, -1, keepdims=True)
    return center * lax.rsqrt(spread + EPS) * norm_gain + norm_shift


def norm_back(values, norm_gain, grad):
    center = values - jnp.mean(values, -1, keepdims=True)
    scale = lax.rsqrt(jnp.mean(center * center, -1, keepdims=True) + EPS)
    normed = center * scale
    scaled = grad * norm_gain
    back = scaled - jnp.mean(scaled, -1, keepdims=True)
    back = (back - normed * jnp.mean(scaled * normed, -1, keepdims=True)) * scale
    return back, jnp.sum(grad * normed, 0), jnp.sum(grad, 0)


def dot_nn(left, right):
    return jnp.dot(left, right, preferred_element_type=F32)


def dot_tn(left, right):
    return lax.dot_general(left, right, (((0,), (0,)), ((), ())), preferred_element_type=F32)


def dot_nt(left, right):
    return lax.dot_general(left, right, (((1,), (1,)), ((), ())), preferred_element_type=F32)


def up_kernel(rows_ref, weight_ref, bias_ref, hidden_ref, slope_ref):
    pre = dot_nn(rows_ref[...], weight_ref[...]) + bias_ref[...]
    cdf = 0.5 * lax.erf(pre * (0.5**0.5)) + 0.5
    density = jnp.exp(-0.5 * pre * pre) * 0.3989422804014327
    hidden_ref[...] = (pre * cdf).astype(BF16)
    slope_ref[...] = (cdf + pre * density).astype(BF16)


def up_gelu(rows, weight, bias):
    count, depth = rows.shape
    cols = weight.shape[1]
    block_rows, block_cols = min(512, count), min(640, cols)
    return pl.pallas_call(
        up_kernel,
        grid=(cols // block_cols, count // block_rows),
        in_specs=[
            pl.BlockSpec((block_rows, depth), lambda n, m: (m, 0)),
            pl.BlockSpec((depth, block_cols), lambda n, m: (0, n)),
            pl.BlockSpec((1, block_cols), lambda n, m: (0, n)),
        ],
        out_specs=[
            pl.BlockSpec((block_rows, block_cols), lambda n, m: (m, n)),
            pl.BlockSpec((block_rows, block_cols), lambda n, m: (m, n)),
        ],
        out_shape=[jax.ShapeDtypeStruct((count, cols), BF16)] * 2,
        cost_estimate=pl.CostEstimate(
            flops=2 * count * depth * cols, bytes_accessed=20_000_000, transcendentals=0
        ),
        compiler_params=pltpu.CompilerParams(vmem_limit_bytes=40 << 20),
        name="up_gelu",
    )(rows, weight, bias)


def attend_kernel(heads, scaling, query_ref, all_ref, mask_ref, out_ref, total_ref):
    width = heads * HDIM
    queries = query_ref[...]
    mask = mask_ref[...]
    outs, totals = [], []
    for head in range(heads):
        low = head * HDIM
        query = queries[:, low : low + HDIM]
        key = all_ref[:, width + low : width + low + HDIM]
        value = all_ref[:, 2 * width + low : 2 * width + low + HDIM]
        scores = dot_nt(query, key) * (scaling * LOG2E) + mask
        row_max = jnp.max(scores, -1, keepdims=True)
        exp_scores = jnp.exp2(scores - row_max)
        total = jnp.sum(exp_scores, -1, keepdims=True)
        mixed = dot_nn(exp_scores.astype(BF16), value)
        outs.append(mixed * (1.0 / total))
        totals.append(row_max + jnp.log2(total))
    out_ref[...] = jnp.concatenate(outs, -1).astype(BF16)
    for head in range(heads):
        wide = jnp.broadcast_to(totals[head], (totals[head].shape[0], 128))
        total_ref[head : head + 1, :] = wide.T[0:1, :]


def attend(joined, mask_row, heads, scaling):
    count, cols = joined.shape
    block_rows = min(256, count)
    width = heads * HDIM
    return pl.pallas_call(
        functools.partial(attend_kernel, heads, scaling),
        grid=(count // block_rows,),
        in_specs=[
            pl.BlockSpec((block_rows, cols), lambda m: (m, 0)),
            pl.BlockSpec((count, cols), lambda m: (0, 0)),
            pl.BlockSpec((1, count), lambda m: (0, 0)),
        ],
        out_specs=[
            pl.BlockSpec((block_rows, width), lambda m: (m, 0)),
            pl.BlockSpec((heads, block_rows), lambda m: (0, m)),
        ],
        out_shape=[
            jax.ShapeDtypeStruct((count, width), BF16),
            jax.ShapeDtypeStruct((heads, count), F32),
        ],
        cost_estimate=pl.CostEstimate(
            flops=2 * heads * count * count * 512,
            bytes_accessed=4_000_000,
            transcendentals=heads * count * count,
        ),
        compiler_params=pltpu.CompilerParams(vmem_limit_bytes=48 << 20),
        name="attend",
    )(joined, joined, mask_row)


def attend_back_kernel(
    heads, scaling, query_ref, all_ref, grad_ref, total_ref, mask_ref,
    out_ref, sums_ref, key_sum, value_sum,
):
    step = pl.program_id(0)
    steps = pl.num_programs(0)
    width = heads * HDIM
    block_rows = query_ref.shape[0]

    @pl.when(step == 0)
    def _():
        key_sum[...] = jnp.zeros_like(key_sum)
        value_sum[...] = jnp.zeros_like(value_sum)
        sums_ref[...] = jnp.zeros_like(sums_ref)

    queries = query_ref[...]
    grads = grad_ref[...]
    query_outs = []
    for head in range(heads):
        low = head * HDIM
        query = queries[:, low : low + HDIM]
        grad = grads[:, low : low + HDIM]
        key = all_ref[:, width + low : width + low + HDIM]
        value = all_ref[:, 2 * width + low : 2 * width + low + HDIM]
        scores = dot_nt(key, query) * (scaling * LOG2E) + mask_ref[...]
        probs = jnp.exp2(scores - total_ref[head : head + 1, :])
        grad_probs = dot_nt(value, grad)
        shared = jnp.sum(probs * grad_probs, 0, keepdims=True)
        grad_scores = (probs * (grad_probs - shared)).astype(BF16)
        value_sum[head, :, :HDIM] += dot_nn(probs.astype(BF16), grad)
        key_sum[head, :, :HDIM] += dot_nn(grad_scores, query)
        query_outs.append(dot_tn(grad_scores, key) * scaling)
    joined = jnp.concatenate(query_outs, -1)
    sums_ref[0:1, :width] += jnp.sum(joined, 0, keepdims=True)
    rows = pl.ds(pl.multiple_of(step * block_rows, block_rows), block_rows)
    out_ref[rows, :width] = joined.astype(BF16)

    @pl.when(step == steps - 1)
    def _():
        keys = jnp.concatenate([key_sum[head, :, :HDIM] for head in range(heads)], -1)
        values = jnp.concatenate([value_sum[head, :, :HDIM] for head in range(heads)], -1)
        sums_ref[1:2, :width] = jnp.sum(values, 0, keepdims=True)
        out_ref[:, width:] = jnp.concatenate([keys * scaling, values], -1).astype(BF16)


def attend_back(joined, grad_heads, totals, mask_col, heads, scaling):
    count, cols = joined.shape
    block_rows = min(256, count)
    width = heads * HDIM
    return pl.pallas_call(
        functools.partial(attend_back_kernel, heads, scaling),
        grid=(count // block_rows,),
        in_specs=[
            pl.BlockSpec((block_rows, cols), lambda m: (m, 0)),
            pl.BlockSpec((count, cols), lambda m: (0, 0)),
            pl.BlockSpec((block_rows, width), lambda m: (m, 0)),
            pl.BlockSpec((heads, block_rows), lambda m: (0, m)),
            pl.BlockSpec((count, 1), lambda m: (0, 0)),
        ],
        out_specs=[
            pl.BlockSpec((count, cols), lambda m: (0, 0)),
            pl.BlockSpec((8, 256), lambda m: (0, 0)),
        ],
        out_shape=[
            jax.ShapeDtypeStruct((count, cols), BF16),
            jax.ShapeDtypeStruct((8, 256), F32),
        ],
        scratch_shapes=[
            pltpu.VMEM((heads, count, 128), F32),
            pltpu.VMEM((heads, count, 128), F32),
        ],
        cost_estimate=pl.CostEstimate(
            flops=2 * heads * count * count * 1280,
            bytes_accessed=5_000_000,
            transcendentals=heads * count * count,
        ),
        compiler_params=pltpu.CompilerParams(vmem_limit_bytes=56 << 20),
        name="attend_back",
    )(joined, joined, grad_heads, totals, mask_col)


UNIT = 320
SPAN = 640
TURNS = 4


def clamp_rows(ref, start, size):
    return ref.at[pl.ds(pl.multiple_of(start, 16), size)]


def forward_kernel(
    scaling,
    attn_shard, up_shard, down_shard, tokens, cotangent, mask_in, bias_in,
    gain_one, shift_one, gain_two, shift_two, bias_out,
    w_attn_out, w_up_out, w_down, tokens_out, grad_out, mask_out, first_out, second_out, joined_out,
    heads_out, totals_out, middle_out, hidden_out, slope_out,
    w_attn, w_up, tok, first, second, joined, heads, middle, send_rows, got_rows, hidden, slope,
    mask, totals, bias, send_sem, recv_sem, local_sem,
):
    dp, z = lax.axis_index("dp"), lax.axis_index("tensor")
    core, plane = lax.rem(dp, 2), lax.div(dp, 2)
    x_bit, y_bit = lax.rem(plane, 2), lax.div(plane, 2)
    half = tok.shape[0]
    count = 2 * half
    to_x = (y_bit * 4 + (1 - x_bit) * 2 + core, z)
    to_y = ((1 - y_bit) * 4 + x_bit * 2 + core, z)
    to_core = (plane * 2 + 1 - core, z)
    to_clip = (plane * 2 + 1 - core, z + 1 - 2 * lax.rem(z, 2))
    to_z = [(dp, lax.rem(z + k, TURNS)) for k in range(TURNS)]
    moves = core != lax.rem(z, 2)
    plane_x = y_bit * 2 + 1 - x_bit
    plane_y = (1 - y_bit) * 2 + x_bit
    plane_xy = (1 - y_bit) * 2 + 1 - x_bit
    turn = [lax.rem(z + TURNS - k, TURNS) for k in range(TURNS)]

    barrier = pltpu.get_barrier_semaphore()
    partners = [to_x, to_y, to_core, to_clip] + to_z[1:]
    for partner in partners:
        pl.semaphore_signal(barrier, inc=1, device_id=partner, device_id_type=pl.DeviceIdType.MESH)
    pl.semaphore_wait(barrier, len(partners))

    def remote(source, target, sem, device):
        return pltpu.make_async_remote_copy(
            src_ref=source,
            dst_ref=target,
            send_sem=send_sem.at[sem],
            recv_sem=recv_sem.at[sem],
            device_id=device,
            device_id_type=pl.DeviceIdType.MESH,
        )

    sent = []

    def send(source, target, sem, device):
        copy = remote(source, target, sem, device)
        copy.start()
        sent.append(copy)

    def arrived(target, sem):
        remote(target, target, sem, to_core).wait_recv()

    weights = [w_attn, w_up, w_down]
    shards = [attn_shard, up_shard, down_shard]

    def block(array, k, place):
        return weights[array].at[
            pl.ds(pl.multiple_of(place * UNIT, 16), UNIT),
            pl.ds(pl.multiple_of(turn[k] * SPAN, 128), SPAN),
        ]

    def own_half(array, which):
        rows = UNIT // 2
        return weights[array].at[
            pl.ds(pl.multiple_of(plane * UNIT + which * rows, 16), rows),
            pl.ds(pl.multiple_of(z * SPAN, 128), SPAN),
        ]

    def pair_start(array):
        send(shards[array].at[1 - core], own_half(array, core), 48 + array, to_core)
        copy = pltpu.make_async_copy(
            shards[array].at[core], own_half(array, core), local_sem.at[array]
        )
        copy.start()
        return copy

    def pair_wait(array, copy):
        copy.wait()
        arrived(own_half(array, 1 - core), 48 + array)

    def go_plane(array, k):
        send(block(array, k, plane), block(array, k, plane), 16 * array + 4 + k, to_x)
        send(block(array, k, plane), block(array, k, plane), 16 * array + 8 + k, to_y)

    def go_line(array):
        for k in range(1, TURNS):
            send(block(array, 0, plane), block(array, 0, plane), 16 * array + k, to_z[k])

    def from_line(array, k):
        arrived(block(array, k, plane), 16 * array + k)
        go_plane(array, k)

    def forward_on(array, k):
        if k % 2 == 0:
            arrived(block(array, k, plane_x), 16 * array + 4 + k)
            send(block(array, k, plane_x), block(array, k, plane_x), 16 * array + 12 + k, to_y)
        else:
            arrived(block(array, k, plane_y), 16 * array + 8 + k)
            send(block(array, k, plane_y), block(array, k, plane_y), 16 * array + 12 + k, to_x)

    def complete(array, k):
        if k % 2 == 0:
            arrived(block(array, k, plane_y), 16 * array + 8 + k)
        else:
            arrived(block(array, k, plane_x), 16 * array + 4 + k)
        arrived(block(array, k, plane_xy), 16 * array + 12 + k)

    pairs = [pair_start(0)]
    tok_copy = pltpu.make_async_copy(tokens, tok, local_sem.at[3])
    mask_copy = pltpu.make_async_copy(mask_in, mask, local_sem.at[4])
    clip_tok = remote(tokens, tok, 51, to_clip)
    clip_mask = remote(mask_in, mask, 52, to_clip)
    there = grad_out.at[pl.ds(pl.multiple_of((1 - core) * half, 256), half)]
    here = grad_out.at[pl.ds(pl.multiple_of(core * half, 256), half)]
    cot_copy = pltpu.make_async_copy(cotangent, here, local_sem.at[5])
    clip_cot = remote(cotangent, there, 59, to_clip)

    @pl.when(moves)
    def _():
        clip_mask.start()
        clip_tok.start()

    @pl.when(jnp.logical_not(moves))
    def _():
        tok_copy.start()
        mask_copy.start()

    bias_copy = pltpu.make_async_copy(bias_in, bias.at[z], local_sem.at[6])
    bias_copy.start()
    for k in range(1, TURNS):
        send(bias_in, bias.at[z], 52 + k, to_z[k])
    pairs += [pair_start(1), pair_start(2)]
    pair_wait(0, pairs[0])
    go_plane(0, 0)
    go_line(0)
    pair_wait(1, pairs[1])
    go_plane(1, 0)
    pair_wait(2, pairs[2])

    @pl.when(moves)
    def _():
        clip_mask.wait()
        clip_tok.wait()

    @pl.when(jnp.logical_not(moves))
    def _():
        tok_copy.wait()
        mask_copy.wait()

    outs = []

    def put(source, target, sem):
        copy = pltpu.make_async_copy(source, target, local_sem.at[sem])
        copy.start()
        outs.append(copy)
        return copy

    put(tok, tokens_out, 7)
    put(mask, mask_out, 8)
    base = pl.multiple_of(core * half, 256)
    other = pl.multiple_of((1 - core) * half, 256)

    def norm_loop(step, _):
        rows = pl.ds(pl.multiple_of(step * 256, 256), 256)
        values = tok[rows, :].astype(F32)
        normed = norm_rows(values, gain_one[...], shift_one[...])
        first[pl.ds(pl.multiple_of(base + step * 256, 256), 256), :] = normed.astype(BF16)
        return 0

    lax.fori_loop(0, half // 256, norm_loop, 0)
    own_rows, other_rows = pl.ds(base, half), pl.ds(other, half)
    send(first.at[own_rows], first.at[own_rows], 56, to_core)
    forward_on(0, 0)
    arrived(first.at[other_rows], 56)
    put(first, first_out, 9)
    bias_copy.wait()
    for k in range(1, TURNS):
        arrived(bias.at[turn[k]], 52 + k)
    forward_on(1, 0)
    for k in range(1, TURNS):
        from_line(0, k)
    go_line(1)

    def project(k):
        complete(0, k)
        columns = pl.ds(pl.multiple_of(turn[k] * SPAN, 128), 480)

        def step_rows(step, _):
            rows = pl.ds(pl.multiple_of(step * half, half), half)
            product = dot_nn(first[rows, :], w_attn[:, columns]) + bias[turn[k], 0:1, :480]
            joined[k, rows, :480] = product.astype(BF16)
            return 0

        lax.fori_loop(0, 2, step_rows, 0)
        put(joined.at[k], joined_out.at[turn[k]], 10 + k)

    def attention(k, part):
        def step_rows(step, _):
            rows = pl.ds(pl.multiple_of(step * 256, 256), 256)
            queries = joined[k, rows, :160]
            mixes, logs = [jnp.zeros((256, 96), F32)], []
            for head in range(2):
                low = head * HDIM
                query = queries[:, low : low + HDIM]
                key = joined[k, :, 160 + low : 160 + low + HDIM]
                value = joined[k, :, 320 + low : 320 + low + HDIM]
                scores = dot_nt(query, key) * (scaling * LOG2E) + mask[0:1, :]
                row_max = jnp.max(scores, -1, keepdims=True)
                exp_scores = jnp.exp2(scores - row_max)
                total = jnp.sum(exp_scores, -1, keepdims=True)
                mixes.append(dot_nn(exp_scores.astype(BF16), value) * (1.0 / total))
                logs.append(row_max + jnp.log2(total))
            heads[k, rows, :] = jnp.concatenate(mixes, -1).astype(BF16)
            for head in range(2):
                wide = jnp.broadcast_to(logs[head], (256, 128))
                totals[k, head : head + 1, rows] = wide.T[0:1, :]
            return 0

        lax.fori_loop(3 * part, 3 * part + 3, step_rows, 0)
        if part == 1:
            put(heads.at[k], heads_out.at[turn[k]], 14 + k)
            put(totals.at[k], totals_out.at[turn[k]], 18 + k)

    project(0)
    attention(0, 0)
    forward_on(0, 1)
    attention(0, 1)
    forward_on(0, 2)
    forward_on(0, 3)
    project(1)
    attention(1, 0)
    for k in range(1, TURNS):
        from_line(1, k)
    go_plane(2, 0)
    go_line(2)

    @pl.when(moves)
    def _():
        clip_cot.start()

    @pl.when(jnp.logical_not(moves))
    def _():
        cot_copy.start()

    attention(1, 1)
    project(2)
    attention(2, 0)
    forward_on(1, 1)
    forward_on(1, 2)
    attention(2, 1)
    forward_on(1, 3)
    project(3)
    put(w_attn, w_attn_out, 22)
    attention(3, 0)
    forward_on(2, 0)
    attention(3, 1)

    def branch(rows):
        total = None
        for k in range(TURNS):
            columns = pl.ds(pl.multiple_of(turn[k] * SPAN + 384, 128), 256)
            product = dot_nt(heads[k, rows, :], w_attn[:, columns])
            total = product if total is None else total + product
        return total

    def branch_other(step, _):
        rows = pl.ds(pl.multiple_of(other + step * 256, 256), 256)
        send_rows[pl.ds(pl.multiple_of(step * 256, 256), 256), :] = branch(rows).astype(BF16)
        return 0

    lax.fori_loop(0, half // 256, branch_other, 0)
    send(send_rows, got_rows, 57, to_core)
    for k in range(1, TURNS):
        from_line(2, k)

    def branch_own(step, _):
        rows = pl.ds(pl.multiple_of(base + step * 256, 256), 256)
        low = pl.ds(pl.multiple_of(step * 256, 256), 256)
        middle[low, :] = branch(rows) + tok[low, :].astype(F32) + bias_out[...]
        return 0

    lax.fori_loop(0, half // 256, branch_own, 0)
    arrived(got_rows, 57)

    def norm_two(step, _):
        low = pl.ds(pl.multiple_of(step * 256, 256), 256)
        values = middle[low, :] + got_rows[low, :].astype(F32)
        middle[low, :] = values
        normed = norm_rows(values, gain_two[...], shift_two[...])
        second[pl.ds(pl.multiple_of(base + step * 256, 256), 256), :] = normed.astype(BF16)
        return 0

    lax.fori_loop(0, half // 256, norm_two, 0)
    send(second.at[own_rows], second.at[own_rows], 58, to_core)
    put(middle, middle_out, 23)
    forward_on(2, 1)
    arrived(second.at[other_rows], 58)
    put(second, second_out, 24)

    waits = [None, None]

    def lift(k):
        complete(1, k)
        slot = k % 2
        if waits[slot] is not None:
            for copy in waits[slot]:
                copy.wait()
        columns = pl.ds(pl.multiple_of(turn[k] * SPAN, 128), SPAN)

        def step_rows(step, _):
            rows = pl.ds(pl.multiple_of(step * 256, 256), 256)
            pre = dot_nn(second[rows, :], w_up[:, columns]) + bias[turn[k], 1:2, :]
            cdf = 0.5 * lax.erf(pre * (0.5**0.5)) + 0.5
            density = jnp.exp(-0.5 * pre * pre) * 0.3989422804014327
            hidden[slot, rows, :] = (pre * cdf).astype(BF16)
            slope[slot, rows, :] = (cdf + pre * density).astype(BF16)
            return 0

        lax.fori_loop(0, count // 256, step_rows, 0)
        waits[slot] = [
            put(hidden.at[slot], hidden_out.at[:, columns], 25 + slot),
            put(slope.at[slot], slope_out.at[:, columns], 27 + slot),
        ]
        for _ in range(2):
            outs.pop()

    lift(0)
    forward_on(2, 2)
    lift(1)
    forward_on(2, 3)
    lift(2)
    lift(3)
    put(w_up, w_up_out, 29)

    @pl.when(moves)
    def _():
        clip_cot.wait_send()
        arrived(here, 59)

    @pl.when(jnp.logical_not(moves))
    def _():
        cot_copy.wait()

    send(here, here, 60, to_core)
    for k in range(TURNS):
        complete(2, k)
    arrived(there, 60)
    for copy in outs + waits[0] + waits[1]:
        copy.wait()
    for copy in sent:
        copy.wait_send()


def forward_pass(
    shards, tokens, cotangent, mask, bias, gain_one, shift_one, gain_two, shift_two, bias_out
):
    half, features = tokens.shape
    count = 2 * half
    any_space = pl.BlockSpec(memory_space=pl.ANY)
    vmem = pl.BlockSpec(memory_space=pltpu.VMEM)
    wide = (features, TURNS * SPAN)
    shapes = [
        (wide, BF16), (wide, BF16), (wide, BF16), ((half, features), BF16), ((count, features), BF16),
        ((8, count), F32), ((count, features), BF16), ((count, features), BF16),
        ((TURNS, count, SPAN), BF16), ((TURNS, count, 256), BF16), ((TURNS, 8, count), F32),
        ((half, features), F32), ((count, TURNS * SPAN), BF16), ((count, TURNS * SPAN), BF16),
    ]
    return pl.pallas_call(
        functools.partial(forward_kernel, HDIM ** (-0.5)),
        in_specs=[any_space] * 7 + [vmem] * 5,
        out_specs=[any_space] * len(shapes),
        out_shape=[jax.ShapeDtypeStruct(shape, kind) for shape, kind in shapes],
        scratch_shapes=[
            pltpu.VMEM(wide, BF16),
            pltpu.VMEM(wide, BF16),
            pltpu.VMEM((half, features), BF16),
            pltpu.VMEM((count, features), BF16),
            pltpu.VMEM((count, features), BF16),
            pltpu.VMEM((TURNS, count, SPAN), BF16),
            pltpu.VMEM((TURNS, count, 256), BF16),
            pltpu.VMEM((half, features), F32),
            pltpu.VMEM((half, features), BF16),
            pltpu.VMEM((half, features), BF16),
            pltpu.VMEM((2, count, SPAN), BF16),
            pltpu.VMEM((2, count, SPAN), BF16),
            pltpu.VMEM((8, count), F32),
            pltpu.VMEM((TURNS, 8, count), F32),
            pltpu.VMEM((TURNS, 8, SPAN), F32),
            pltpu.SemaphoreType.DMA((64,)),
            pltpu.SemaphoreType.DMA((64,)),
            pltpu.SemaphoreType.DMA((32,)),
        ],
        cost_estimate=pl.CostEstimate(
            flops=2 * count * features * 6400, bytes_accessed=80_000_000, transcendentals=30_000_000
        ),
        compiler_params=pltpu.CompilerParams(
            vmem_limit_bytes=60 << 20, collective_id=0, has_side_effects=True
        ),
        name="forward_pass",
    )(*shards, tokens, cotangent, mask, bias, gain_one, shift_one, gain_two, shift_two, bias_out)


def backward_kernel(
    scaling,
    w_attn_in, w_up_in, w_down_in, tok_in, grad_in, first_in, second_in, joined_in, heads_in, middle_in,
    hidden_in, slope_in, totals_in, key_mask, gain_one, gain_two,
    tokens_out, down_out, up_out, attn_out, sums_out, pre_out,
    weight, grad, left, wide, right, grad_heads, totals, middle, send_rows, got_rows, key_sum, value_sum,
    product, near_got, far_got, turn_got, line_got, line_own, final, final_got, sums, sums_got,
    send_sem, recv_sem, local_sem, credit,
):
    dp, z = lax.axis_index("dp"), lax.axis_index("tensor")
    core, plane = lax.rem(dp, 2), lax.div(dp, 2)
    x_bit, y_bit = lax.rem(plane, 2), lax.div(plane, 2)
    half = middle.shape[0]
    count = 2 * half
    features = middle.shape[1]
    to_x = (y_bit * 4 + (1 - x_bit) * 2 + core, z)
    to_y = ((1 - y_bit) * 4 + x_bit * 2 + core, z)
    to_core = (plane * 2 + 1 - core, z)
    to_clip = (plane * 2 + 1 - core, z + 1 - 2 * lax.rem(z, 2))
    to_z = [(dp, lax.rem(z + k, TURNS)) for k in range(TURNS)]
    to_z_pair = (dp, z + 1 - 2 * lax.rem(z, 2))
    moves = core != lax.rem(z, 2)
    plane_x = y_bit * 2 + 1 - x_bit
    plane_y = (1 - y_bit) * 2 + x_bit
    plane_xy = (1 - y_bit) * 2 + 1 - x_bit
    turn = [lax.rem(z + TURNS - k, TURNS) for k in range(TURNS)]
    base = pl.multiple_of(core * half, 256)
    other = pl.multiple_of((1 - core) * half, 256)
    own_rows, other_rows = pl.ds(base, half), pl.ds(other, half)

    barrier = pltpu.get_barrier_semaphore()
    partners = [to_x, to_y, to_core, to_clip] + to_z[1:]
    for partner in partners:
        pl.semaphore_signal(barrier, inc=1, device_id=partner, device_id_type=pl.DeviceIdType.MESH)
    pl.semaphore_wait(barrier, len(partners))

    def remote(source, target, sem, device):
        return pltpu.make_async_remote_copy(
            src_ref=source,
            dst_ref=target,
            send_sem=send_sem.at[sem],
            recv_sem=recv_sem.at[sem],
            device_id=device,
            device_id_type=pl.DeviceIdType.MESH,
        )

    def send(source, target, sem, device):
        copy = remote(source, target, sem, device)
        copy.start()
        return copy

    def arrived(target, sem):
        remote(target, target, sem, to_core).wait_recv()

    def tell(index, device):
        pl.semaphore_signal(
            credit.at[index], inc=1, device_id=device, device_id_type=pl.DeviceIdType.MESH
        )

    def local(source, target, sem):
        copy = pltpu.make_async_copy(source, target, local_sem.at[sem])
        copy.start()
        return copy

    def columns(k):
        return pl.ds(pl.multiple_of(turn[k] * SPAN, 128), SPAN)

    def load_right(source, k, slot):
        return local(source.at[:, columns(k)], right.at[slot], slot)

    grad_load = local(grad_in, grad, 2)
    right_loads = [load_right(hidden_in, 0, 0), None]
    weight_loads, slope_loads = [], []
    for k in range(TURNS):
        weight_loads.append(local(w_down_in.at[:, columns(k)], weight.at[:, columns(k)], 3 + k))
        slope_loads.append(local(slope_in.at[:, columns(k)], wide.at[:, columns(k)], 7 + k))
    right_loads[1] = load_right(hidden_in, 1, 1)
    left_load = local(second_in, left, 11)
    middle_load = local(middle_in, middle, 12)
    totals_loads = [local(totals_in.at[turn[k]], totals.at[k], 21 + k) for k in range(TURNS)]
    sums[...] = jnp.zeros_like(sums)

    in_flight = [[] for _ in range(TURNS)]

    def place(k, where):
        return product.at[k, pl.ds(pl.multiple_of(where * UNIT, 16), UNIT)]

    def ready(k):
        for copy in in_flight[k]:
            copy.wait_send()
        in_flight[k] = []

    def produce(k, factor, chunk):
        ready(k)

        def step_part(part, _):
            rows = pl.ds(pl.multiple_of(part * 640, 640), 640)
            product[k, rows, :] = dot_tn(factor[:, rows], chunk[...]).astype(BF16)
            return 0

        lax.fori_loop(0, 2, step_part, 0)

    def ways(k):
        if k % 2 == 0:
            return to_x, to_y, plane_x, plane_y
        return to_y, to_x, plane_y, plane_x

    def stage_one(array, k):
        go, _, near, _ = ways(k)
        if array > 0:
            pl.semaphore_wait(credit.at[k], 1)
        sem = 16 * array + k
        in_flight[k].append(send(place(k, plane_xy), far_got.at[k], sem + 4, go))
        in_flight[k].append(send(place(k, near), near_got.at[k], sem, go))

    def add_to(target, sources):
        total = target[...].astype(F32)
        for source in sources:
            total = total + source[...].astype(F32)
        return total

    def stage_two(array, k):
        go, follow, _, far = ways(k)
        sem = 16 * array + k
        arrived(far_got.at[k], sem + 4)
        target = place(k, far)
        target[...] = add_to(target, [far_got.at[k]]).astype(BF16)
        if array > 0:
            pl.semaphore_wait(credit.at[4 + k], 1)
        in_flight[k].append(send(target, turn_got.at[k], sem + 8, follow))
        arrived(near_got.at[k], sem)
        target = place(k, plane)
        target[...] = add_to(target, [near_got.at[k]]).astype(BF16)
        if array < 2:
            tell(k, go)

    def stage_three(array, k):
        _, follow, _, _ = ways(k)
        sem = 16 * array + k
        arrived(turn_got.at[k], sem + 8)
        target = place(k, plane)
        total = add_to(target, [turn_got.at[k]]).astype(BF16)
        if array < 2:
            tell(4 + k, follow)
        if k == 0:
            line_own[...] = total
            return
        target[...] = total
        if array > 0:
            pl.semaphore_wait(credit.at[8 + k], 1)
        in_flight[k].append(send(target, line_got.at[k], sem + 12, to_z[(TURNS - k) % TURNS]))

    results = [down_out, up_out, attn_out]
    final_moves = []

    def final_one(array):
        for copy in final_moves:
            copy()
        final_moves.clear()
        for k in range(1, TURNS):
            arrived(line_got.at[k], 16 * array + k + 12)
        final[...] = add_to(line_own, [line_got.at[k] for k in range(1, TURNS)])
        if array < 2:
            for k in range(1, TURNS):
                tell(8 + k, to_z[k])
        rows = UNIT // 2
        keep = pl.ds(pl.multiple_of(core * rows, 16), rows)
        give = pl.ds(pl.multiple_of((1 - core) * rows, 16), rows)
        final_moves.append(send(final.at[give], final_got.at[array], 52 + array, to_core).wait_send)
        target = results[array].at[:, pl.ds(pl.multiple_of(core * SPAN, 128), SPAN)]
        final_moves.append(local(final.at[keep], target, 13).wait)

    last_moves = []

    def final_two(array):
        arrived(final_got.at[array], 52 + array)
        target = results[array].at[:, pl.ds(pl.multiple_of((1 - core) * SPAN, 128), SPAN)]
        last_moves.append(local(final_got.at[array], target, 14 + array).wait)

    grad_load.wait()
    right_loads[0].wait()
    produce(0, grad, right.at[0])
    stage_one(0, 0)
    right_loads[0] = load_right(hidden_in, 2, 0)
    pre_puts = []

    def grad_pre(k):
        weight_loads[k].wait()
        slope_loads[k].wait()

        def step_rows(step, total):
            rows = pl.ds(pl.multiple_of(step * 512, 512), 512)
            value = dot_nn(grad[rows, :], weight[:, columns(k)])
            value = value * wide[rows, columns(k)].astype(F32)
            wide[rows, columns(k)] = value.astype(BF16)
            return total + jnp.sum(value, 0, keepdims=True)

        total = lax.fori_loop(0, count // 512, step_rows, jnp.zeros((1, SPAN), F32))
        sums[8 + 2 * turn[k] + core, :, :SPAN] = total
        pre_puts.append(local(wide.at[:, columns(k)], pre_out.at[:, columns(k)], 17 + k))
        weight_loads[k] = local(w_up_in.at[:, columns(k)], weight.at[:, columns(k)], 3 + k)

    grad_pre(0)
    grad_pre(1)
    right_loads[1].wait()
    produce(1, grad, right.at[1])
    stage_one(0, 1)
    right_loads[1] = load_right(hidden_in, 3, 1)
    grad_pre(2)
    grad_pre(3)
    for load in weight_loads:
        load.wait()

    def second_part(rows):
        return dot_nt(wide[rows, :], weight[...])

    def second_other(step, _):
        rows = pl.ds(pl.multiple_of(other + step * 256, 256), 256)
        send_rows[pl.ds(pl.multiple_of(step * 256, 256), 256), :] = second_part(rows).astype(BF16)
        return 0

    lax.fori_loop(0, half // 256, second_other, 0)
    rows_sent = send(send_rows, got_rows, 48, to_core)
    stage_two(0, 0)
    right_loads[0].wait()
    produce(2, grad, right.at[0])
    stage_one(0, 2)
    right_loads[1].wait()
    produce(3, grad, right.at[1])
    stage_one(0, 3)
    tell(12, to_core)
    middle_load.wait()
    arrived(got_rows, 48)

    def norm_back_rows(values, gain, above):
        center = values - jnp.mean(values, -1, keepdims=True)
        scale = lax.rsqrt(jnp.mean(center * center, -1, keepdims=True) + EPS)
        normed = center * scale
        scaled = above * gain
        back = scaled - jnp.mean(scaled, -1, keepdims=True)
        back = (back - normed * jnp.mean(scaled * normed, -1, keepdims=True)) * scale
        return back, jnp.sum(above * normed, 0, keepdims=True), jnp.sum(above, 0, keepdims=True)

    def norm_two(step, total):
        low = pl.ds(pl.multiple_of(step * 256, 256), 256)
        rows = pl.ds(pl.multiple_of(base + step * 256, 256), 256)
        above = second_part(rows) + got_rows[low, :].astype(F32)
        back, by_gain, by_shift = norm_back_rows(middle[low, :], gain_two[...], above)
        out_grad = grad[rows, :].astype(F32)
        below = out_grad + back
        middle[low, :] = below
        grad[rows, :] = below.astype(BF16)
        by_down, by_out = jnp.sum(out_grad, 0, keepdims=True), jnp.sum(below, 0, keepdims=True)
        return (total[0] + by_down, total[1] + by_out, total[2] + by_gain, total[3] + by_shift)

    zero = jnp.zeros((1, features), F32)
    parts = lax.fori_loop(0, half // 256, norm_two, (zero,) * 4)
    for i in range(4):
        sums[i, :, :] = parts[i]
    pl.semaphore_wait(credit.at[12], 1)
    branch_sent = send(grad.at[own_rows], grad.at[own_rows], 49, to_core)
    for copy in pre_puts:
        copy.wait()
    weight_load = local(w_attn_in, weight, 3)
    joined_loads = [
        local(joined_in.at[turn[k]], wide.at[:, k * SPAN : (k + 1) * SPAN], 7 + k) for k in range(TURNS)
    ]
    pre_loads = [local(pre_out.at[:, columns(k)], right.at[k], k) for k in range(2)]
    stage_two(0, 1)
    stage_three(0, 0)
    weight_load.wait()
    arrived(grad.at[other_rows], 49)

    def heads_back(k):
        slab = pl.ds(pl.multiple_of(turn[k] * SPAN + 384, 128), 256)

        def step_rows(step, _):
            rows = pl.ds(pl.multiple_of(step * 512, 512), 512)
            grad_heads[rows, :] = dot_nn(grad[rows, :], weight[:, slab]).astype(BF16)
            return 0

        lax.fori_loop(0, count // 512, step_rows, 0)
        joined_loads[k].wait()
        totals_loads[k].wait()
        key_sum[...] = jnp.zeros_like(key_sum)
        value_sum[...] = jnp.zeros_like(value_sum)

    one_lane = (lax.broadcasted_iota(jnp.int32, (256, 48), 1) == 0).astype(F32).astype(BF16)

    def attention(k, part, total):
        low = k * SPAN

        def step_rows(step, total):
            rows = pl.ds(pl.multiple_of(step * 256, 256), 256)
            queries = wide[rows, low : low + 160]
            grads = grad_heads[rows, :]
            outs = []
            for head in range(2):
                at = head * HDIM
                query = queries[:, at : at + HDIM]
                above = grads[:, 96 + at : 96 + at + HDIM]
                key = wide[:, low + 160 + at : low + 160 + at + HDIM]
                value = wide[:, low + 320 + at : low + 320 + at + HDIM]
                scores = dot_nt(
                    jnp.concatenate([key, key_mask[:, :48]], -1),
                    jnp.concatenate([query, one_lane], -1),
                )
                probs = jnp.exp2(
                    scores * (scaling * LOG2E) - totals[k, head : head + 1, rows]
                )
                grad_probs = dot_nt(value, above)
                shared = jnp.sum(probs * grad_probs, 0, keepdims=True)
                grad_scores = (probs * (grad_probs - shared)).astype(BF16)
                value_sum[head, :, :HDIM] += dot_nn(probs.astype(BF16), above)
                key_sum[head, :, :HDIM] += dot_nn(grad_scores, query)
                outs.append(dot_tn(grad_scores, key) * scaling)
            joined = jnp.concatenate(outs, -1)
            wide[rows, low : low + 160] = joined.astype(BF16)
            return total + jnp.sum(joined, 0, keepdims=True)

        return lax.fori_loop(2 * part, 2 * part + 2, step_rows, total)

    def attention_end(k, total):
        low = k * SPAN

        def step_rows(step, value_total):
            rows = pl.ds(pl.multiple_of(step * 256, 256), 256)
            keys = [key_sum[head, rows, :HDIM] * scaling for head in range(2)]
            values = [value_sum[head, rows, :HDIM] for head in range(2)]
            joined = jnp.concatenate(keys + values, -1)
            wide[rows, low + 160 : low + 480] = joined.astype(BF16)
            return value_total + jnp.sum(joined[:, 160:], 0, keepdims=True)

        value_total = lax.fori_loop(0, count // 256, step_rows, jnp.zeros((1, 160), F32))
        sums[16 + 2 * turn[k] + core, :, :160] = total
        sums[16 + 2 * turn[k] + core, :, 160:320] = value_total

    def produce_attn(k):
        heads_load = local(heads_in.at[turn[k]], grad_heads, 4)
        ready(k)
        heads_load.wait()

        def step_part(part, _):
            rows = pl.ds(pl.multiple_of(part * 640, 640), 640)
            by_first = dot_tn(left[:, rows], wide[:, k * SPAN : k * SPAN + 480])
            by_branch = dot_tn(grad[:, rows], grad_heads[:, 96:256])
            product[k, rows, :] = jnp.concatenate([by_first, by_branch], -1).astype(BF16)
            return 0

        lax.fori_loop(0, 2, step_part, 0)

    start = jnp.zeros((1, 160), F32)
    left_load.wait()

    def up_chunk(k):
        slot = k % 2
        pre_loads[slot].wait()
        produce(k, left, right.at[slot])
        stage_one(1, k)
        if k < 2:
            pre_loads[slot] = local(pre_out.at[:, columns(k + 2)], right.at[slot], slot)

    heads_back(0)
    up_chunk(0)
    total = attention(0, 0, start)
    stage_two(0, 2)
    stage_three(0, 1)
    total = attention(0, 1, total)
    stage_two(0, 3)
    up_chunk(1)
    total = attention(0, 2, total)
    attention_end(0, total)
    stage_three(0, 2)
    stage_two(1, 0)
    heads_back(1)
    total = attention(1, 0, start)
    stage_three(0, 3)
    up_chunk(2)
    total = attention(1, 1, total)
    stage_two(1, 1)
    final_one(0)
    up_chunk(3)
    left_load = local(first_in, left, 11)
    total = attention(1, 2, total)
    attention_end(1, total)
    final_two(0)
    stage_two(1, 2)
    stage_three(1, 0)
    stage_three(1, 1)
    left_load.wait()
    produce_attn(0)
    stage_one(2, 0)
    produce_attn(1)
    stage_one(2, 1)
    heads_back(2)
    stage_two(1, 3)
    total = attention(2, 0, start)
    stage_three(1, 2)
    total = attention(2, 1, total)
    stage_two(2, 0)
    stage_three(1, 3)
    total = attention(2, 2, total)
    attention_end(2, total)
    stage_two(2, 1)
    produce_attn(2)
    stage_one(2, 2)
    final_one(1)
    heads_back(3)
    total = attention(3, 0, start)
    stage_three(2, 0)
    total = attention(3, 1, total)
    stage_three(2, 1)
    final_two(1)
    total = attention(3, 2, total)
    attention_end(3, total)
    produce_attn(3)
    stage_one(2, 3)
    branch_sent.wait_send()
    tok_load = local(tok_in, grad.at[0:half], 2)
    stage_two(2, 2)

    def first_part(rows):
        total = None
        for k in range(TURNS):
            slab = pl.ds(pl.multiple_of(turn[k] * SPAN, 128), 480)
            part = dot_nt(wide[rows, k * SPAN : k * SPAN + 480], weight[:, slab])
            total = part if total is None else total + part
        return total

    rows_sent.wait_send()

    def first_other(step, _):
        rows = pl.ds(pl.multiple_of(other + step * 256, 256), 256)
        send_rows[pl.ds(pl.multiple_of(step * 256, 256), 256), :] = first_part(rows).astype(BF16)
        return 0

    lax.fori_loop(0, half // 256, first_other, 0)
    rows_sent = send(send_rows, got_rows, 50, to_core)
    stage_three(2, 2)
    tok_load.wait()
    arrived(got_rows, 50)

    def norm_one(step, total):
        low = pl.ds(pl.multiple_of(step * 256, 256), 256)
        rows = pl.ds(pl.multiple_of(base + step * 256, 256), 256)
        above = first_part(rows) + got_rows[low, :].astype(F32)
        back, by_gain, by_shift = norm_back_rows(grad[low, :].astype(F32), gain_one[...], above)
        below = middle[low, :] + back
        grad[pl.ds(pl.multiple_of(half + step * 256, 256), 256), :] = below.astype(BF16)
        return (total[0] + by_gain, total[1] + by_shift)

    parts = lax.fori_loop(0, half // 256, norm_one, (zero,) * 2)
    for i in range(2):
        sums[4 + i, :, :] = parts[i]
    tokens_away = remote(grad.at[half:count], tokens_out, 51, to_clip)
    tokens_here = pltpu.make_async_copy(grad.at[half:count], tokens_out, local_sem.at[2])

    @pl.when(moves)
    def _():
        tokens_away.start()

    @pl.when(jnp.logical_not(moves))
    def _():
        tokens_here.start()

    def hop(index, device):
        copy = send(sums, sums_got.at[index], 55 + index, device)
        copy.wait_send()
        arrived(sums_got.at[index], 55 + index)
        sums[...] = sums[...] + sums_got[index]

    hop(0, to_core)
    hop(1, to_x)
    stage_two(2, 3)
    hop(2, to_y)
    hop(3, to_z_pair)
    hop(4, to_z[2])
    sums_put = local(sums, sums_out, 5)
    stage_three(2, 3)
    final_one(2)
    final_two(2)

    @pl.when(moves)
    def _():
        tokens_away.wait()

    @pl.when(jnp.logical_not(moves))
    def _():
        tokens_here.wait()

    sums_put.wait()
    rows_sent.wait_send()
    for wait in final_moves + last_moves:
        wait()
    for k in range(TURNS):
        ready(k)


def backward_pass(
    w_attn, w_up, w_down, tok, grad, first, second, joined, heads, middle, hidden, slope, totals, key_mask,
    gain_one, gain_two,
):
    half, features = tok.shape
    count = 2 * half
    any_space = pl.BlockSpec(memory_space=pl.ANY)
    vmem = pl.BlockSpec(memory_space=pltpu.VMEM)
    cols = TURNS * SPAN
    shapes = [
        ((half, features), BF16), ((UNIT // 2, 2 * SPAN), F32), ((UNIT // 2, 2 * SPAN), F32),
        ((UNIT // 2, 2 * SPAN), F32), ((24, 1, features), F32), ((count, cols), BF16),
    ]
    return pl.pallas_call(
        functools.partial(backward_kernel, HDIM ** (-0.5)),
        in_specs=[any_space] * 13 + [vmem] * 3,
        out_specs=[any_space] * len(shapes),
        out_shape=[jax.ShapeDtypeStruct(shape, kind) for shape, kind in shapes],
        scratch_shapes=[
            pltpu.VMEM((features, cols), BF16),
            pltpu.VMEM((count, features), BF16),
            pltpu.VMEM((count, features), BF16),
            pltpu.VMEM((count, cols), BF16),
            pltpu.VMEM((2, count, SPAN), BF16),
            pltpu.VMEM((count, 256), BF16),
            pltpu.VMEM((TURNS, 8, count), F32),
            pltpu.VMEM((half, features), F32),
            pltpu.VMEM((half, features), BF16),
            pltpu.VMEM((half, features), BF16),
            pltpu.VMEM((2, count, 128), F32),
            pltpu.VMEM((2, count, 128), F32),
            pltpu.VMEM((TURNS, features, SPAN), BF16),
            pltpu.VMEM((TURNS, UNIT, SPAN), BF16),
            pltpu.VMEM((TURNS, UNIT, SPAN), BF16),
            pltpu.VMEM((TURNS, UNIT, SPAN), BF16),
            pltpu.VMEM((TURNS, UNIT, SPAN), BF16),
            pltpu.VMEM((UNIT, SPAN), BF16),
            pltpu.VMEM((UNIT, SPAN), F32),
            pltpu.VMEM((3, UNIT // 2, SPAN), F32),
            pltpu.VMEM((24, 1, features), F32),
            pltpu.VMEM((5, 24, 1, features), F32),
            pltpu.SemaphoreType.DMA((64,)),
            pltpu.SemaphoreType.DMA((64,)),
            pltpu.SemaphoreType.DMA((32,)),
            pltpu.SemaphoreType.REGULAR((16,)),
        ],
        cost_estimate=pl.CostEstimate(
            flops=4 * count * features * 6400, bytes_accessed=90_000_000, transcendentals=30_000_000
        ),
        compiler_params=pltpu.CompilerParams(
            vmem_limit_bytes=60 << 20, collective_id=1, has_side_effects=True
        ),
        name="backward_pass",
    )(
        w_attn, w_up, w_down, tok, grad, first, second, joined, heads, middle, hidden, slope, totals,
        key_mask, gain_one, gain_two,
    )


class Links:
    def __init__(self):
        self.dp = lax.axis_size("dp")
        self.tensor = lax.axis_size("tensor")
        self.tensor_pos = lax.axis_index("tensor")
        self.half = self.tensor_pos % 2

    def pair(self, value):
        return lax.ppermute(value, "tensor", [(i, i ^ 1) for i in range(self.tensor)])

    def columns(self, shard):
        rows, _, width = shard.shape
        whole = lax.all_gather(shard, ("dp", "tensor"), axis=0)
        whole = lax.dynamic_index_in_dim(whole, self.half, 2, keepdims=False)
        whole = whole.reshape(self.dp, self.tensor, rows, width)
        return [whole[:, k].reshape(self.dp * rows, width) for k in range(self.tensor)]

    def vectors(self, value):
        whole = lax.all_gather(value, "tensor", axis=0)
        return [whole[k] for k in range(self.tensor)]

    def place(self, pieces):
        halves = (jnp.arange(2) == self.half)[None, :, None]
        return jnp.where(halves, jnp.stack(pieces)[:, None, :], 0.0)

    def gradient(self, left, rights):
        whole = jnp.stack([dot_tn(left, right).astype(BF16) for right in rights], 0)
        features, width = whole.shape[1:]
        whole = whole.reshape(self.tensor, self.dp, features // self.dp, width)
        whole = jnp.moveaxis(whole, 1, 0)[:, :, :, None, :]
        halves = (jnp.arange(2) == self.half)[None, None, None, :, None]
        whole = jnp.where(halves, whole, jnp.zeros((), BF16))
        whole = whole.reshape((self.dp * self.tensor,) + whole.shape[2:])
        return lax.psum_scatter(whole, ("dp", "tensor"), tiled=False).astype(F32)

    def merged(self, partial_of):
        got = self.pair(partial_of(1).astype(BF16))
        return partial_of(0) + got.astype(F32)


def summed(vectors, total):
    whole = total(jnp.concatenate(vectors))
    at = 0
    result = []
    for vector in vectors:
        result.append(whole[at : at + vector.shape[0]])
        at += vector.shape[0]
    return result


def halves_of(weight):
    return weight.reshape(weight.shape[0], 2, weight.shape[1] // 2)


def flat(piece):
    return piece.reshape(piece.shape[0], -1)


def local_any(
    tokens,
    lengths,
    cotangent,
    norm1_gain,
    norm1_shift,
    query_weight,
    query_bias,
    key_weight,
    value_weight,
    value_bias,
    out_weight,
    out_bias,
    norm2_gain,
    norm2_shift,
    up_weight,
    up_bias,
    down_weight,
    down_bias,
):
    links = Links()
    rows = tokens.shape[0]
    scaling = HDIM ** (-0.5)
    width = query_weight.shape[1] // 2
    heads = width // HDIM
    units = up_weight.shape[1] // 2
    count = links.tensor

    shard_attn = [query_weight, key_weight, value_weight, out_weight.T]
    w_attn = links.columns(jnp.concatenate([halves_of(w) for w in shard_attn], -1))
    w_up = jnp.concatenate(links.columns(halves_of(up_weight)), 1)
    w_down = jnp.concatenate(links.columns(halves_of(down_weight.T)), 1)
    w_qkv = [block[:, : 3 * width] for block in w_attn]
    w_out = [block[:, 3 * width :] for block in w_attn]
    small = [query_bias.reshape(2, width), value_bias.reshape(2, width), up_bias.reshape(2, units)]
    small = jnp.concatenate(small, -1)
    small = links.vectors(jnp.where(links.half == 0, small[0], small[1]))
    bias_qkv = [
        jnp.concatenate([v[:width], jnp.zeros((width,), F32), v[width : 2 * width]]) for v in small
    ]
    bias_up = jnp.concatenate([v[2 * width :] for v in small])

    place = links.tensor_pos // 2
    clip_length = jnp.sum(jnp.where(jnp.arange(lengths.shape[0]) == place, lengths, 0))
    frames = jnp.arange(rows)
    frames = jnp.concatenate([links.half * rows + frames, (1 - links.half) * rows + frames])
    visible = frames < clip_length
    mask = jnp.where(visible, 0.0, -1e30).astype(F32)

    def part_of(value, part):
        return value[part * rows : (part + 1) * rows]

    def both(value):
        return jnp.concatenate([value, links.pair(value)])

    source = tokens.astype(F32)
    first = both(norm_rows(source, norm1_gain, norm1_shift).astype(BF16))
    joined, heads_out, totals = [], [], []
    for k in range(count):
        joined.append((dot_nn(first, w_qkv[k]) + bias_qkv[k]).astype(BF16))
        mixed, total = attend(joined[k], mask[None, :], heads, scaling)
        heads_out.append(mixed)
        totals.append(total)
    heads_all = jnp.concatenate(heads_out, 1)
    w_out_all = jnp.concatenate(w_out, 1)
    branch = links.merged(lambda part: dot_nt(part_of(heads_all, part), w_out_all))
    middle = source + branch + out_bias
    second = both(norm_rows(middle, norm2_gain, norm2_shift).astype(BF16))
    hidden, slope = up_gelu(second, w_up, bias_up[None, :])
    out_own = cotangent * visible[:rows].astype(BF16)[:, None]
    out_grad = both(out_own)

    def cut(value):
        return [value[:, k * units : (k + 1) * units] for k in range(count)]

    grad_down = links.gradient(out_grad, cut(hidden))
    down_out = links.merged(lambda part: dot_nt(part_of(hidden, part), w_down))
    layer_out = (middle + down_out + down_bias).astype(BF16)
    grad_pre = (dot_nn(out_grad, w_down) * slope.astype(F32)).astype(BF16)
    grad_up = links.gradient(second, cut(grad_pre))
    grad_second = links.merged(lambda part: dot_nt(part_of(grad_pre, part), w_up))
    back_two, grad_gain_two, grad_shift_two = norm_back(middle, norm2_gain, grad_second)
    grad_middle = out_own.astype(F32) + back_two
    branch_grad = both(grad_middle.astype(BF16))
    grad_heads = [dot_nn(branch_grad, w_out[k]).astype(BF16) for k in range(count)]
    grad_out_w = links.gradient(branch_grad, heads_out)
    grad_joined, sums = [], []
    for k in range(count):
        back, sum_k = attend_back(joined[k], grad_heads[k], totals[k], mask[:, None], heads, scaling)
        grad_joined.append(back)
        sums.append(sum_k)
    grad_qkv = links.gradient(first, grad_joined)
    grad_all = jnp.concatenate(grad_joined, 1)
    w_qkv_all = jnp.concatenate(w_qkv, 1)
    grad_first = links.merged(lambda part: dot_nt(part_of(grad_all, part), w_qkv_all))
    back_one, grad_gain_one, grad_shift_one = norm_back(source, norm1_gain, grad_first)
    grad_tokens = (grad_middle + back_one).astype(BF16)

    vectors = [
        links.place([v[0] for v in cut(jnp.sum(grad_pre.astype(F32), 0)[None, :])]).reshape(-1),
        links.place([s[0, :width] for s in sums]).reshape(-1),
        links.place([s[1, :width] for s in sums]).reshape(-1),
        grad_gain_one,
        grad_shift_one,
        jnp.sum(grad_middle, 0),
        grad_gain_two,
        grad_shift_two,
        jnp.sum(out_own.astype(F32), 0),
    ]
    sum_up, sum_query, sum_value, *rest = summed(
        vectors, lambda value: lax.psum(value, ("dp", "tensor"))
    )
    sum_gain_one, sum_shift_one, sum_out, sum_gain_two, sum_shift_two, sum_down = rest

    def own(vector):
        size = vector.shape[0] // count
        return lax.dynamic_slice_in_dim(vector, links.tensor_pos * size, size, 0)

    return (
        layer_out,
        grad_tokens,
        sum_gain_one,
        sum_shift_one,
        flat(grad_qkv[:, :, :width]),
        own(sum_query),
        flat(grad_qkv[:, :, width : 2 * width]),
        flat(grad_qkv[:, :, 2 * width :]),
        own(sum_value),
        flat(grad_out_w).T,
        sum_out,
        sum_gain_two,
        sum_shift_two,
        flat(grad_up),
        own(sum_up),
        flat(grad_down).T,
        sum_down,
    )


def local_chips(
    tokens,
    lengths,
    cotangent,
    norm1_gain,
    norm1_shift,
    query_weight,
    query_bias,
    key_weight,
    value_weight,
    value_bias,
    out_weight,
    out_bias,
    norm2_gain,
    norm2_shift,
    up_weight,
    up_bias,
    down_weight,
    down_bias,
):
    dp, z = lax.axis_index("dp"), lax.axis_index("tensor")
    core, plane = dp % 2, dp // 2
    half = tokens.shape[0]
    count = 2 * half
    width, units = 160, SPAN

    def split(weight):
        return jnp.moveaxis(halves_of(weight), 1, 0)

    shards = (
        jnp.concatenate([split(w) for w in (query_weight, key_weight, value_weight, out_weight.T)], -1),
        split(up_weight),
        split(down_weight.T),
    )
    place = jnp.sum(jnp.where(jnp.arange(lengths.shape[0]) == z // 2, lengths, 0))
    mask = jnp.where(jnp.arange(count) < place, 0.0, -1e30).astype(F32)
    mask = jnp.broadcast_to(mask[None, :], (8, count))
    valid = ((z % 2) * half + jnp.arange(half) < place).astype(BF16)
    small = [query_bias.reshape(2, width), jnp.zeros((2, width), F32), value_bias.reshape(2, width)]
    small = jnp.concatenate(small + [jnp.zeros((2, width), F32)], -1)
    small = jnp.stack([small, up_bias.reshape(2, units)], 1)
    small = jnp.pad(jnp.where(core == 0, small[0], small[1]), ((0, 6), (0, 0)))
    (
        w_attn, w_up, w_down, tok, out_grad, mask, first, second, joined, heads, totals, middle, hidden,
        slope,
    ) = forward_pass(
        shards, tokens, cotangent * valid[:, None], mask, small,
        norm1_gain[None, :], norm1_shift[None, :], norm2_gain[None, :], norm2_shift[None, :],
        out_bias[None, :],
    )

    def pair(value):
        return lax.ppermute(value, "dp", [(i, i ^ 1) for i in range(8)])

    def move_rows(value):
        swaps = [
            (a * 4 + b, (a ^ 1) * 4 + (b ^ 1)) for a in range(8) for b in range(4) if a % 2 != b % 2
        ]
        moved = lax.ppermute(value, ("dp", "tensor"), swaps)
        return jnp.where(core == z % 2, value, moved)

    def part_of(value, part):
        start = (core if part == 0 else 1 - core) * half
        return lax.dynamic_slice_in_dim(value, start, half, 0)

    got = pair(dot_nt(part_of(hidden, 1), w_down).astype(BF16))
    layer_out = middle + dot_nt(part_of(hidden, 0), w_down) + got.astype(F32) + down_bias
    layer_out = move_rows(layer_out.astype(BF16))

    lane = jnp.arange(128)[None, :] == 0
    key_mask = jnp.where(lane, mask[0][:, None], 0.0).astype(BF16)
    grad_tokens, grad_down, grad_up, grad_attn, sums, _ = backward_pass(
        w_attn, w_up, w_down, tok, out_grad, first, second, joined, heads, middle, hidden, slope, totals,
        key_mask, norm1_gain[None, :], norm2_gain[None, :],
    )

    def piece(index):
        start = index * width
        both = [grad_attn[:, i * SPAN + start : i * SPAN + start + width] for i in range(2)]
        return jnp.concatenate(both, 1)

    def own(first_row, start, size):
        rows = lax.dynamic_slice_in_dim(sums[:, 0], first_row + 2 * z, 2, 0)
        return rows[:, start : start + size].reshape(-1)

    return (
        layer_out,
        grad_tokens,
        sums[4, 0],
        sums[5, 0],
        piece(0),
        own(16, 0, width),
        piece(1),
        piece(2),
        own(16, width, width),
        piece(3).T,
        sums[1, 0],
        sums[2, 0],
        sums[3, 0],
        grad_up,
        own(8, 0, units),
        grad_down.T,
        sums[0, 0],
    )


def solution(mesh):
    rows = P(("dp", "tensor"), None)
    wide, tall = P("dp", "tensor"), P("tensor", "dp")
    piece, same = P("tensor"), P()
    chips = mesh.shape["dp"] == 8 and mesh.shape["tensor"] == 4
    return jax.shard_map(
        local_chips if chips else local_any,
        mesh=mesh,
        in_specs=(
            rows, P("dp"), rows, same, same, wide, piece, wide, wide, piece, tall, same, same, same,
            wide, piece, tall, same,
        ),
        out_specs=(
            rows, rows, same, same, wide, piece, wide, wide, piece, tall, same, same, same, wide, piece,
            tall, same,
        ),
        check_vma=False,
    )
```

```python
import functools

import jax
import jax.numpy as jnp
from jax import lax
from jax.experimental import pallas as pl
from jax.experimental.pallas import tpu as pltpu
from jax.sharding import PartitionSpec as P

HDIM = 80
EPS = 1e-05
LOG2E = 1.4426950408889634
F32 = jnp.float32
BF16 = jnp.bfloat16


def norm_rows(values, norm_gain, norm_shift):
    center = values - jnp.mean(values, -1, keepdims=True)
    spread = jnp.mean(center * center, -1, keepdims=True)
    return center * lax.rsqrt(spread + EPS) * norm_gain + norm_shift


def norm_back(values, norm_gain, grad):
    center = values - jnp.mean(values, -1, keepdims=True)
    scale = lax.rsqrt(jnp.mean(center * center, -1, keepdims=True) + EPS)
    normed = center * scale
    scaled = grad * norm_gain
    back = scaled - jnp.mean(scaled, -1, keepdims=True)
    back = (back - normed * jnp.mean(scaled * normed, -1, keepdims=True)) * scale
    return back, jnp.sum(grad * normed, 0), jnp.sum(grad, 0)


def dot_nn(left, right):
    return jnp.dot(left, right, preferred_element_type=F32)


def dot_tn(left, right):
    return lax.dot_general(left, right, (((0,), (0,)), ((), ())), preferred_element_type=F32)


def dot_nt(left, right):
    return lax.dot_general(left, right, (((1,), (1,)), ((), ())), preferred_element_type=F32)


def up_kernel(rows_ref, weight_ref, bias_ref, hidden_ref, slope_ref):
    pre = dot_nn(rows_ref[...], weight_ref[...]) + bias_ref[...]
    cdf = 0.5 * lax.erf(pre * (0.5**0.5)) + 0.5
    density = jnp.exp(-0.5 * pre * pre) * 0.3989422804014327
    hidden_ref[...] = (pre * cdf).astype(BF16)
    slope_ref[...] = (cdf + pre * density).astype(BF16)


def up_gelu(rows, weight, bias):
    count, depth = rows.shape
    cols = weight.shape[1]
    block_rows, block_cols = min(512, count), min(640, cols)
    return pl.pallas_call(
        up_kernel,
        grid=(cols // block_cols, count // block_rows),
        in_specs=[
            pl.BlockSpec((block_rows, depth), lambda n, m: (m, 0)),
            pl.BlockSpec((depth, block_cols), lambda n, m: (0, n)),
            pl.BlockSpec((1, block_cols), lambda n, m: (0, n)),
        ],
        out_specs=[
            pl.BlockSpec((block_rows, block_cols), lambda n, m: (m, n)),
            pl.BlockSpec((block_rows, block_cols), lambda n, m: (m, n)),
        ],
        out_shape=[jax.ShapeDtypeStruct((count, cols), BF16)] * 2,
        cost_estimate=pl.CostEstimate(
            flops=2 * count * depth * cols, bytes_accessed=20_000_000, transcendentals=0
        ),
        compiler_params=pltpu.CompilerParams(vmem_limit_bytes=40 << 20),
        name="up_gelu",
    )(rows, weight, bias)


def attend_kernel(heads, scaling, query_ref, all_ref, mask_ref, out_ref, total_ref):
    width = heads * HDIM
    queries = query_ref[...]
    mask = mask_ref[...]
    outs, totals = [], []
    for head in range(heads):
        low = head * HDIM
        query = queries[:, low : low + HDIM]
        key = all_ref[:, width + low : width + low + HDIM]
        value = all_ref[:, 2 * width + low : 2 * width + low + HDIM]
        scores = dot_nt(query, key) * (scaling * LOG2E) + mask
        row_max = jnp.max(scores, -1, keepdims=True)
        exp_scores = jnp.exp2(scores - row_max)
        total = jnp.sum(exp_scores, -1, keepdims=True)
        mixed = dot_nn(exp_scores.astype(BF16), value)
        outs.append(mixed * (1.0 / total))
        totals.append(row_max + jnp.log2(total))
    out_ref[...] = jnp.concatenate(outs, -1).astype(BF16)
    for head in range(heads):
        wide = jnp.broadcast_to(totals[head], (totals[head].shape[0], 128))
        total_ref[head : head + 1, :] = wide.T[0:1, :]


def attend(joined, mask_row, heads, scaling):
    count, cols = joined.shape
    block_rows = min(256, count)
    width = heads * HDIM
    return pl.pallas_call(
        functools.partial(attend_kernel, heads, scaling),
        grid=(count // block_rows,),
        in_specs=[
            pl.BlockSpec((block_rows, cols), lambda m: (m, 0)),
            pl.BlockSpec((count, cols), lambda m: (0, 0)),
            pl.BlockSpec((1, count), lambda m: (0, 0)),
        ],
        out_specs=[
            pl.BlockSpec((block_rows, width), lambda m: (m, 0)),
            pl.BlockSpec((heads, block_rows), lambda m: (0, m)),
        ],
        out_shape=[
            jax.ShapeDtypeStruct((count, width), BF16),
            jax.ShapeDtypeStruct((heads, count), F32),
        ],
        cost_estimate=pl.CostEstimate(
            flops=2 * heads * count * count * 512,
            bytes_accessed=4_000_000,
            transcendentals=heads * count * count,
        ),
        compiler_params=pltpu.CompilerParams(vmem_limit_bytes=48 << 20),
        name="attend",
    )(joined, joined, mask_row)


def attend_back_kernel(
    heads, scaling, query_ref, all_ref, grad_ref, total_ref, mask_ref,
    out_ref, sums_ref, key_sum, value_sum,
):
    step = pl.program_id(0)
    steps = pl.num_programs(0)
    width = heads * HDIM
    block_rows = query_ref.shape[0]

    @pl.when(step == 0)
    def _():
        key_sum[...] = jnp.zeros_like(key_sum)
        value_sum[...] = jnp.zeros_like(value_sum)
        sums_ref[...] = jnp.zeros_like(sums_ref)

    queries = query_ref[...]
    grads = grad_ref[...]
    query_outs = []
    for head in range(heads):
        low = head * HDIM
        query = queries[:, low : low + HDIM]
        grad = grads[:, low : low + HDIM]
        key = all_ref[:, width + low : width + low + HDIM]
        value = all_ref[:, 2 * width + low : 2 * width + low + HDIM]
        scores = dot_nt(key, query) * (scaling * LOG2E) + mask_ref[...]
        probs = jnp.exp2(scores - total_ref[head : head + 1, :])
        grad_probs = dot_nt(value, grad)
        shared = jnp.sum(probs * grad_probs, 0, keepdims=True)
        grad_scores = (probs * (grad_probs - shared)).astype(BF16)
        value_sum[head, :, :HDIM] += dot_nn(probs.astype(BF16), grad)
        key_sum[head, :, :HDIM] += dot_nn(grad_scores, query)
        query_outs.append(dot_tn(grad_scores, key) * scaling)
    joined = jnp.concatenate(query_outs, -1)
    sums_ref[0:1, :width] += jnp.sum(joined, 0, keepdims=True)
    rows = pl.ds(pl.multiple_of(step * block_rows, block_rows), block_rows)
    out_ref[rows, :width] = joined.astype(BF16)

    @pl.when(step == steps - 1)
    def _():
        keys = jnp.concatenate([key_sum[head, :, :HDIM] for head in range(heads)], -1)
        values = jnp.concatenate([value_sum[head, :, :HDIM] for head in range(heads)], -1)
        sums_ref[1:2, :width] = jnp.sum(values, 0, keepdims=True)
        out_ref[:, width:] = jnp.concatenate([keys * scaling, values], -1).astype(BF16)


def attend_back(joined, grad_heads, totals, mask_col, heads, scaling):
    count, cols = joined.shape
    block_rows = min(256, count)
    width = heads * HDIM
    return pl.pallas_call(
        functools.partial(attend_back_kernel, heads, scaling),
        grid=(count // block_rows,),
        in_specs=[
            pl.BlockSpec((block_rows, cols), lambda m: (m, 0)),
            pl.BlockSpec((count, cols), lambda m: (0, 0)),
            pl.BlockSpec((block_rows, width), lambda m: (m, 0)),
            pl.BlockSpec((heads, block_rows), lambda m: (0, m)),
            pl.BlockSpec((count, 1), lambda m: (0, 0)),
        ],
        out_specs=[
            pl.BlockSpec((count, cols), lambda m: (0, 0)),
            pl.BlockSpec((8, 256), lambda m: (0, 0)),
        ],
        out_shape=[
            jax.ShapeDtypeStruct((count, cols), BF16),
            jax.ShapeDtypeStruct((8, 256), F32),
        ],
        scratch_shapes=[
            pltpu.VMEM((heads, count, 128), F32),
            pltpu.VMEM((heads, count, 128), F32),
        ],
        cost_estimate=pl.CostEstimate(
            flops=2 * heads * count * count * 1280,
            bytes_accessed=5_000_000,
            transcendentals=heads * count * count,
        ),
        compiler_params=pltpu.CompilerParams(vmem_limit_bytes=56 << 20),
        name="attend_back",
    )(joined, joined, grad_heads, totals, mask_col)


UNIT = 320
SPAN = 640
TURNS = 4


def clamp_rows(ref, start, size):
    return ref.at[pl.ds(pl.multiple_of(start, 16), size)]


def forward_kernel(
    scaling,
    attn_shard, up_shard, down_shard, tokens, cotangent, mask_in, bias_in,
    gain_one, shift_one, gain_two, shift_two, bias_out,
    w_attn_out, w_up_out, w_down, tokens_out, grad_out, mask_out, first_out, second_out, joined_out,
    heads_out, totals_out, middle_out, hidden_out, slope_out,
    w_attn, w_up, tok, first, second, joined, heads, middle, send_rows, got_rows, hidden, slope,
    mask, totals, bias, send_sem, recv_sem, local_sem,
):
    dp, z = lax.axis_index("dp"), lax.axis_index("tensor")
    core, plane = lax.rem(dp, 2), lax.div(dp, 2)
    x_bit, y_bit = lax.rem(plane, 2), lax.div(plane, 2)
    half = tok.shape[0]
    count = 2 * half
    to_x = (y_bit * 4 + (1 - x_bit) * 2 + core, z)
    to_y = ((1 - y_bit) * 4 + x_bit * 2 + core, z)
    to_core = (plane * 2 + 1 - core, z)
    to_clip = (plane * 2 + 1 - core, z + 1 - 2 * lax.rem(z, 2))
    to_z = [(dp, lax.rem(z + k, TURNS)) for k in range(TURNS)]
    moves = core != lax.rem(z, 2)
    plane_x = y_bit * 2 + 1 - x_bit
    plane_y = (1 - y_bit) * 2 + x_bit
    plane_xy = (1 - y_bit) * 2 + 1 - x_bit
    turn = [lax.rem(z + TURNS - k, TURNS) for k in range(TURNS)]

    barrier = pltpu.get_barrier_semaphore()
    partners = [to_x, to_y, to_core, to_clip] + to_z[1:]
    for partner in partners:
        pl.semaphore_signal(barrier, inc=1, device_id=partner, device_id_type=pl.DeviceIdType.MESH)
    pl.semaphore_wait(barrier, len(partners))

    def remote(source, target, sem, device):
        return pltpu.make_async_remote_copy(
            src_ref=source,
            dst_ref=target,
            send_sem=send_sem.at[sem],
            recv_sem=recv_sem.at[sem],
            device_id=device,
            device_id_type=pl.DeviceIdType.MESH,
        )

    sent = []

    def send(source, target, sem, device):
        copy = remote(source, target, sem, device)
        copy.start()
        sent.append(copy)

    def arrived(target, sem):
        remote(target, target, sem, to_core).wait_recv()

    weights = [w_attn, w_up, w_down]
    shards = [attn_shard, up_shard, down_shard]

    def block(array, k, place):
        return weights[array].at[
            pl.ds(pl.multiple_of(place * UNIT, 16), UNIT),
            pl.ds(pl.multiple_of(turn[k] * SPAN, 128), SPAN),
        ]

    def own_half(array, which):
        rows = UNIT // 2
        return weights[array].at[
            pl.ds(pl.multiple_of(plane * UNIT + which * rows, 16), rows),
            pl.ds(pl.multiple_of(z * SPAN, 128), SPAN),
        ]

    def pair_start(array):
        send(shards[array].at[1 - core], own_half(array, core), 48 + array, to_core)
        copy = pltpu.make_async_copy(
            shards[array].at[core], own_half(array, core), local_sem.at[array]
        )
        copy.start()
        return copy

    def pair_wait(array, copy):
        copy.wait()
        arrived(own_half(array, 1 - core), 48 + array)

    def go_plane(array, k):
        send(block(array, k, plane), block(array, k, plane), 16 * array + 4 + k, to_x)
        send(block(array, k, plane), block(array, k, plane), 16 * array + 8 + k, to_y)

    def go_line(array):
        for k in range(1, TURNS):
            send(block(array, 0, plane), block(array, 0, plane), 16 * array + k, to_z[k])

    def from_line(array, k):
        arrived(block(array, k, plane), 16 * array + k)
        go_plane(array, k)

    def forward_on(array, k):
        if k % 2 == 0:
            arrived(block(array, k, plane_x), 16 * array + 4 + k)
            send(block(array, k, plane_x), block(array, k, plane_x), 16 * array + 12 + k, to_y)
        else:
            arrived(block(array, k, plane_y), 16 * array + 8 + k)
            send(block(array, k, plane_y), block(array, k, plane_y), 16 * array + 12 + k, to_x)

    def complete(array, k):
        if k % 2 == 0:
            arrived(block(array, k, plane_y), 16 * array + 8 + k)
        else:
            arrived(block(array, k, plane_x), 16 * array + 4 + k)
        arrived(block(array, k, plane_xy), 16 * array + 12 + k)

    pairs = [pair_start(0)]
    tok_copy = pltpu.make_async_copy(tokens, tok, local_sem.at[3])
    mask_copy = pltpu.make_async_copy(mask_in, mask, local_sem.at[4])
    clip_tok = remote(tokens, tok, 51, to_clip)
    clip_mask = remote(mask_in, mask, 52, to_clip)
    there = grad_out.at[pl.ds(pl.multiple_of((1 - core) * half, 256), half)]
    here = grad_out.at[pl.ds(pl.multiple_of(core * half, 256), half)]
    cot_copy = pltpu.make_async_copy(cotangent, here, local_sem.at[5])
    clip_cot = remote(cotangent, there, 59, to_clip)

    @pl.when(moves)
    def _():
        clip_mask.start()
        clip_tok.start()

    @pl.when(jnp.logical_not(moves))
    def _():
        tok_copy.start()
        mask_copy.start()

    bias_copy = pltpu.make_async_copy(bias_in, bias.at[z], local_sem.at[6])
    bias_copy.start()
    for k in range(1, TURNS):
        send(bias_in, bias.at[z], 52 + k, to_z[k])
    pairs += [pair_start(1), pair_start(2)]
    pair_wait(0, pairs[0])
    go_plane(0, 0)
    go_line(0)
    pair_wait(1, pairs[1])
    go_plane(1, 0)
    pair_wait(2, pairs[2])

    @pl.when(moves)
    def _():
        clip_mask.wait()
        clip_tok.wait()

    @pl.when(jnp.logical_not(moves))
    def _():
        tok_copy.wait()
        mask_copy.wait()

    outs = []

    def put(source, target, sem):
        copy = pltpu.make_async_copy(source, target, local_sem.at[sem])
        copy.start()
        outs.append(copy)
        return copy

    put(tok, tokens_out, 7)
    put(mask, mask_out, 8)
    base = pl.multiple_of(core * half, 256)
    other = pl.multiple_of((1 - core) * half, 256)

    def norm_loop(step, _):
        rows = pl.ds(pl.multiple_of(step * 256, 256), 256)
        values = tok[rows, :].astype(F32)
        normed = norm_rows(values, gain_one[...], shift_one[...])
        first[pl.ds(pl.multiple_of(base + step * 256, 256), 256), :] = normed.astype(BF16)
        return 0

    lax.fori_loop(0, half // 256, norm_loop, 0)
    own_rows, other_rows = pl.ds(base, half), pl.ds(other, half)
    send(first.at[own_rows], first.at[own_rows], 56, to_core)
    forward_on(0, 0)
    arrived(first.at[other_rows], 56)
    put(first, first_out, 9)
    bias_copy.wait()
    for k in range(1, TURNS):
        arrived(bias.at[turn[k]], 52 + k)
    forward_on(1, 0)
    for k in range(1, TURNS):
        from_line(0, k)
    go_line(1)

    def project(k):
        complete(0, k)
        columns = pl.ds(pl.multiple_of(turn[k] * SPAN, 128), 480)

        def step_rows(step, _):
            rows = pl.ds(pl.multiple_of(step * half, half), half)
            product = dot_nn(first[rows, :], w_attn[:, columns]) + bias[turn[k], 0:1, :480]
            joined[k, rows, :480] = product.astype(BF16)
            return 0

        lax.fori_loop(0, 2, step_rows, 0)
        put(joined.at[k], joined_out.at[turn[k]], 10 + k)

    def attention(k, part):
        def step_rows(step, _):
            rows = pl.ds(pl.multiple_of(step * 256, 256), 256)
            queries = joined[k, rows, :160]
            mixes, logs = [jnp.zeros((256, 96), F32)], []
            for head in range(2):
                low = head * HDIM
                query = queries[:, low : low + HDIM]
                key = joined[k, :, 160 + low : 160 + low + HDIM]
                value = joined[k, :, 320 + low : 320 + low + HDIM]
                scores = dot_nt(query, key) * (scaling * LOG2E) + mask[0:1, :]
                row_max = jnp.max(scores, -1, keepdims=True)
                exp_scores = jnp.exp2(scores - row_max)
                total = jnp.sum(exp_scores, -1, keepdims=True)
                mixes.append(dot_nn(exp_scores.astype(BF16), value) * (1.0 / total))
                logs.append(row_max + jnp.log2(total))
            heads[k, rows, :] = jnp.concatenate(mixes, -1).astype(BF16)
            for head in range(2):
                wide = jnp.broadcast_to(logs[head], (256, 128))
                totals[k, head : head + 1, rows] = wide.T[0:1, :]
            return 0

        lax.fori_loop(3 * part, 3 * part + 3, step_rows, 0)
        if part == 1:
            put(heads.at[k], heads_out.at[turn[k]], 14 + k)
            put(totals.at[k], totals_out.at[turn[k]], 18 + k)

    project(0)
    attention(0, 0)
    forward_on(0, 1)
    attention(0, 1)
    forward_on(0, 2)
    forward_on(0, 3)
    project(1)
    attention(1, 0)
    for k in range(1, TURNS):
        from_line(1, k)
    go_plane(2, 0)
    go_line(2)

    @pl.when(moves)
    def _():
        clip_cot.start()

    @pl.when(jnp.logical_not(moves))
    def _():
        cot_copy.start()

    attention(1, 1)
    project(2)
    attention(2, 0)
    forward_on(1, 1)
    forward_on(1, 2)
    attention(2, 1)
    forward_on(1, 3)
    project(3)
    put(w_attn, w_attn_out, 22)
    attention(3, 0)
    forward_on(2, 0)
    attention(3, 1)

    def branch(rows):
        total = None
        for k in range(TURNS):
            columns = pl.ds(pl.multiple_of(turn[k] * SPAN + 384, 128), 256)
            product = dot_nt(heads[k, rows, :], w_attn[:, columns])
            total = product if total is None else total + product
        return total

    def branch_other(step, _):
        rows = pl.ds(pl.multiple_of(other + step * 256, 256), 256)
        send_rows[pl.ds(pl.multiple_of(step * 256, 256), 256), :] = branch(rows).astype(BF16)
        return 0

    lax.fori_loop(0, half // 256, branch_other, 0)
    send(send_rows, got_rows, 57, to_core)
    for k in range(1, TURNS):
        from_line(2, k)

    def branch_own(step, _):
        rows = pl.ds(pl.multiple_of(base + step * 256, 256), 256)
        low = pl.ds(pl.multiple_of(step * 256, 256), 256)
        middle[low, :] = branch(rows) + tok[low, :].astype(F32) + bias_out[...]
        return 0

    lax.fori_loop(0, half // 256, branch_own, 0)
    arrived(got_rows, 57)

    def norm_two(step, _):
        low = pl.ds(pl.multiple_of(step * 256, 256), 256)
        values = middle[low, :] + got_rows[low, :].astype(F32)
        middle[low, :] = values
        normed = norm_rows(values, gain_two[...], shift_two[...])
        second[pl.ds(pl.multiple_of(base + step * 256, 256), 256), :] = normed.astype(BF16)
        return 0

    lax.fori_loop(0, half // 256, norm_two, 0)
    send(second.at[own_rows], second.at[own_rows], 58, to_core)
    put(middle, middle_out, 23)
    forward_on(2, 1)
    arrived(second.at[other_rows], 58)
    put(second, second_out, 24)

    waits = [None, None]

    def lift(k):
        complete(1, k)
        slot = k % 2
        if waits[slot] is not None:
            for copy in waits[slot]:
                copy.wait()
        columns = pl.ds(pl.multiple_of(turn[k] * SPAN, 128), SPAN)

        def step_rows(step, _):
            rows = pl.ds(pl.multiple_of(step * 256, 256), 256)
            pre = dot_nn(second[rows, :], w_up[:, columns]) + bias[turn[k], 1:2, :]
            cdf = 0.5 * lax.erf(pre * (0.5**0.5)) + 0.5
            density = jnp.exp(-0.5 * pre * pre) * 0.3989422804014327
            hidden[slot, rows, :] = (pre * cdf).astype(BF16)
            slope[slot, rows, :] = (cdf + pre * density).astype(BF16)
            return 0

        lax.fori_loop(0, count // 256, step_rows, 0)
        waits[slot] = [
            put(hidden.at[slot], hidden_out.at[:, columns], 25 + slot),
            put(slope.at[slot], slope_out.at[:, columns], 27 + slot),
        ]
        for _ in range(2):
            outs.pop()

    lift(0)
    forward_on(2, 2)
    lift(1)
    forward_on(2, 3)
    lift(2)
    lift(3)
    put(w_up, w_up_out, 29)

    @pl.when(moves)
    def _():
        clip_cot.wait_send()
        arrived(here, 59)

    @pl.when(jnp.logical_not(moves))
    def _():
        cot_copy.wait()

    send(here, here, 60, to_core)
    for k in range(TURNS):
        complete(2, k)
    arrived(there, 60)
    for copy in outs + waits[0] + waits[1]:
        copy.wait()
    for copy in sent:
        copy.wait_send()


def forward_pass(
    shards, tokens, cotangent, mask, bias, gain_one, shift_one, gain_two, shift_two, bias_out
):
    half, features = tokens.shape
    count = 2 * half
    any_space = pl.BlockSpec(memory_space=pl.ANY)
    vmem = pl.BlockSpec(memory_space=pltpu.VMEM)
    wide = (features, TURNS * SPAN)
    shapes = [
        (wide, BF16), (wide, BF16), (wide, BF16), ((half, features), BF16), ((count, features), BF16),
        ((8, count), F32), ((count, features), BF16), ((count, features), BF16),
        ((TURNS, count, SPAN), BF16), ((TURNS, count, 256), BF16), ((TURNS, 8, count), F32),
        ((half, features), F32), ((count, TURNS * SPAN), BF16), ((count, TURNS * SPAN), BF16),
    ]
    return pl.pallas_call(
        functools.partial(forward_kernel, HDIM ** (-0.5)),
        in_specs=[any_space] * 7 + [vmem] * 5,
        out_specs=[any_space] * len(shapes),
        out_shape=[jax.ShapeDtypeStruct(shape, kind) for shape, kind in shapes],
        scratch_shapes=[
            pltpu.VMEM(wide, BF16),
            pltpu.VMEM(wide, BF16),
            pltpu.VMEM((half, features), BF16),
            pltpu.VMEM((count, features), BF16),
            pltpu.VMEM((count, features), BF16),
            pltpu.VMEM((TURNS, count, SPAN), BF16),
            pltpu.VMEM((TURNS, count, 256), BF16),
            pltpu.VMEM((half, features), F32),
            pltpu.VMEM((half, features), BF16),
            pltpu.VMEM((half, features), BF16),
            pltpu.VMEM((2, count, SPAN), BF16),
            pltpu.VMEM((2, count, SPAN), BF16),
            pltpu.VMEM((8, count), F32),
            pltpu.VMEM((TURNS, 8, count), F32),
            pltpu.VMEM((TURNS, 8, SPAN), F32),
            pltpu.SemaphoreType.DMA((64,)),
            pltpu.SemaphoreType.DMA((64,)),
            pltpu.SemaphoreType.DMA((32,)),
        ],
        cost_estimate=pl.CostEstimate(
            flops=2 * count * features * 6400, bytes_accessed=80_000_000, transcendentals=30_000_000
        ),
        compiler_params=pltpu.CompilerParams(
            vmem_limit_bytes=60 << 20, collective_id=0, has_side_effects=True
        ),
        name="forward_pass",
    )(*shards, tokens, cotangent, mask, bias, gain_one, shift_one, gain_two, shift_two, bias_out)


BACKWARD_STEPS = (
    ("load",), ("P", 0, 0), ("pre",), ("P", 0, 1), ("pre",), ("pre",), ("pre",), ("2", 0, 0), ("soth",),
    ("send", "a"), ("P", 0, 2), ("P", 0, 3), ("wait", "a"), ("ntwo",), ("send", "b"), ("3", 0, 0),
    ("2", 0, 1), ("2", 0, 2), ("P", 1, 0), ("wait", "b"), ("hb",), ("att",), ("3", 0, 1), ("2", 0, 3),
    ("att",), ("P", 1, 1), ("att",), ("3", 0, 3), ("3", 0, 2), ("aend",), ("P", 1, 2), ("hb",), ("2", 1, 0),
    ("att",), ("2", 1, 1), ("att",), ("P", 1, 3), ("2", 1, 2), ("F", 0), ("att",), ("aend",), ("3", 1, 1),
    ("3", 1, 0), ("P", 2, 0), ("2", 1, 3), ("P", 2, 1), ("hb",), ("3", 1, 2), ("att",), ("G", 0), ("att",),
    ("att",), ("3", 1, 3), ("aend",), ("P", 2, 2), ("2", 2, 1), ("hb",), ("att",), ("F", 1), ("att",),
    ("3", 2, 1), ("2", 2, 2), ("att",), ("aend",), ("3", 2, 2), ("foth",), ("send", "c"), ("P", 2, 3),
    ("tok",), ("2", 2, 0), ("wait", "c"), ("none",), ("reloc",), ("none",), ("2", 2, 3), ("reloc",),
    ("none",), ("hs", "c"), ("G", 1), ("3", 2, 0), ("hw", "c"), ("hs", "x"), ("hw", "x"), ("hs", "y"),
    ("3", 2, 3), ("hw", "y"), ("hs", "z1"), ("reloc",), ("F", 2), ("hw", "z1"), ("hs", "z2"), ("wreloc",),
    ("G", 2), ("hw", "z2"),
)


def backward_kernel(
    scaling,
    w_attn_in, w_up_in, w_down_in, tok_in, grad_in, first_in, second_in, joined_in, heads_in, middle_in,
    hidden_in, slope_in, totals_in, key_mask, gain_one, gain_two,
    tokens_out, down_out, up_out, attn_out, sums_out, pre_out,
    weight, grad, left, wide, right, grad_heads, totals, middle, send_rows, got_rows, key_sum, value_sum,
    product, near_got, far_got, turn_got, line_got, line_own, final, final_got, sums, sums_got,
    send_sem, recv_sem, local_sem, credit,
):
    dp, z = lax.axis_index("dp"), lax.axis_index("tensor")
    core, plane = lax.rem(dp, 2), lax.div(dp, 2)
    x_bit, y_bit = lax.rem(plane, 2), lax.div(plane, 2)
    half = middle.shape[0]
    count = 2 * half
    features = middle.shape[1]
    to_x = (y_bit * 4 + (1 - x_bit) * 2 + core, z)
    to_y = ((1 - y_bit) * 4 + x_bit * 2 + core, z)
    to_core = (plane * 2 + 1 - core, z)
    to_clip = (plane * 2 + 1 - core, z + 1 - 2 * lax.rem(z, 2))
    to_z = [(dp, lax.rem(z + k, TURNS)) for k in range(TURNS)]
    to_z_pair = (dp, z + 1 - 2 * lax.rem(z, 2))
    moves = core != lax.rem(z, 2)
    plane_x = y_bit * 2 + 1 - x_bit
    plane_y = (1 - y_bit) * 2 + x_bit
    plane_xy = (1 - y_bit) * 2 + 1 - x_bit
    turn = [lax.rem(z + TURNS - k, TURNS) for k in range(TURNS)]
    base = pl.multiple_of(core * half, 256)
    other = pl.multiple_of((1 - core) * half, 256)
    own_rows, other_rows = pl.ds(base, half), pl.ds(other, half)

    barrier = pltpu.get_barrier_semaphore()
    partners = [to_x, to_y, to_core, to_clip] + to_z[1:]
    for partner in partners:
        pl.semaphore_signal(barrier, inc=1, device_id=partner, device_id_type=pl.DeviceIdType.MESH)
    pl.semaphore_wait(barrier, len(partners))

    def remote(source, target, sem, device):
        return pltpu.make_async_remote_copy(
            src_ref=source,
            dst_ref=target,
            send_sem=send_sem.at[sem],
            recv_sem=recv_sem.at[sem],
            device_id=device,
            device_id_type=pl.DeviceIdType.MESH,
        )

    def send(source, target, sem, device):
        copy = remote(source, target, sem, device)
        copy.start()
        return copy

    def arrived(target, sem):
        remote(target, target, sem, to_core).wait_recv()

    def tell(index, device):
        pl.semaphore_signal(
            credit.at[index], inc=1, device_id=device, device_id_type=pl.DeviceIdType.MESH
        )

    def local(source, target, sem):
        copy = pltpu.make_async_copy(source, target, local_sem.at[sem])
        copy.start()
        return copy

    def columns(k):
        return pl.ds(pl.multiple_of(turn[k] * SPAN, 128), SPAN)

    def load_right(source, k, slot):
        return local(source.at[:, columns(k)], right.at[slot], slot)

    grad_load = local(grad_in, grad, 2)
    right_loads = [load_right(hidden_in, 0, 0), None]
    weight_loads, slope_loads = [], []
    for k in range(TURNS):
        weight_loads.append(local(w_down_in.at[:, columns(k)], weight.at[:, columns(k)], 3 + k))
        slope_loads.append(local(slope_in.at[:, columns(k)], wide.at[:, columns(k)], 7 + k))
    right_loads[1] = load_right(hidden_in, 1, 1)
    left_load = local(second_in, left, 11)
    middle_load = local(middle_in, middle, 12)
    totals_loads = [local(totals_in.at[turn[k]], totals.at[k], 21 + k) for k in range(TURNS)]
    sums[...] = jnp.zeros_like(sums)

    in_flight = [[] for _ in range(TURNS)]
    staged = [None] * TURNS
    rows_half = UNIT // 2

    def place(k, where, part=None):
        if part is None:
            return product.at[k, pl.ds(pl.multiple_of(where * UNIT, 16), UNIT)]
        start = pl.multiple_of(where * UNIT + part * rows_half, 16)
        return product.at[k, pl.ds(start, rows_half)]

    def slot(ref, k, part):
        return ref.at[k, part * rows_half : (part + 1) * rows_half]

    def sem_of(array, kind, k):
        return array * 28 + kind * 4 + k

    def ready(k):
        for copy in in_flight[k]:
            copy.wait_send()
        in_flight[k] = []

    def stage_one(array, k):
        for part, device, near in ((0, to_x, plane_x), (1, to_y, plane_y)):
            if array > 0:
                pl.semaphore_wait(credit.at[4 * part + k], 1)
            far = place(k, plane_xy, part)
            in_flight[k] += [
                send(far, slot(far_got, k, part), sem_of(array, part, k), device),
                send(place(k, near, part), slot(near_got, k, part), sem_of(array, 2 + part, k), device),
            ]

    def add_to(target, sources):
        total = target[...].astype(F32)
        for source in sources:
            total = total + source[...].astype(F32)
        return total

    def stage_two(array, k):
        for part, device, back, far in ((0, to_y, to_x, plane_y), (1, to_x, to_y, plane_x)):
            arrived(slot(far_got, k, part), sem_of(array, part, k))
            target = place(k, far, part)
            target[...] = add_to(target, [slot(far_got, k, part)]).astype(BF16)
            if array > 0:
                pl.semaphore_wait(credit.at[8 + 4 * part + k], 1)
            in_flight[k].append(send(target, slot(turn_got, k, part), sem_of(array, 4 + part, k), device))
        for part, back in ((0, to_x), (1, to_y)):
            arrived(slot(near_got, k, part), sem_of(array, 2 + part, k))
            target = place(k, plane, part)
            target[...] = add_to(target, [slot(near_got, k, part)]).astype(BF16)
            if array < 2:
                tell(4 * part + k, back)

    def stage_three(array, k):
        for part in range(2):
            arrived(slot(turn_got, k, part), sem_of(array, 4 + part, k))
        source = place(k, plane)
        total = add_to(source, [turn_got.at[k]]).astype(BF16)
        if array < 2:
            tell(8 + k, to_y)
            tell(12 + k, to_x)
        if k == 0:
            line_own[...] = total
            return
        if array < 2:
            if staged[k] is not None:
                staged[k].wait_send()
            row, col = (k - 1) % 2, (k - 1) // 2
            source = send_rows.at[
                row * UNIT : (row + 1) * UNIT, col * SPAN : (col + 1) * SPAN
            ]
        source[...] = total
        if array > 0:
            pl.semaphore_wait(credit.at[16 + k], 1)
        copy = send(source, line_got.at[k], sem_of(array, 6, k), to_z[(TURNS - k) % TURNS])
        if array < 2:
            staged[k] = copy
        else:
            in_flight[k].append(copy)

    results = [down_out, up_out, attn_out]
    final_moves = []
    last_moves = []

    def final_one(array):
        for wait in final_moves:
            wait()
        final_moves.clear()
        for k in range(1, TURNS):
            arrived(line_got.at[k], sem_of(array, 6, k))
        final[...] = add_to(line_own, [line_got.at[k] for k in range(1, TURNS)])
        if array < 2:
            for k in range(1, TURNS):
                tell(16 + k, to_z[k])
        keep = pl.ds(pl.multiple_of(core * rows_half, 16), rows_half)
        give = pl.ds(pl.multiple_of((1 - core) * rows_half, 16), rows_half)
        final_moves.append(send(final.at[give], final_got.at[array], 90 + array, to_core).wait_send)
        target = results[array].at[:, pl.ds(pl.multiple_of(core * SPAN, 128), SPAN)]
        final_moves.append(local(final.at[keep], target, 13).wait)

    def final_two(array):
        arrived(final_got.at[array], 90 + array)
        target = results[array].at[:, pl.ds(pl.multiple_of((1 - core) * SPAN, 128), SPAN)]
        last_moves.append(local(final_got.at[array], target, 14 + array).wait)

    pre_puts, pre_loads = [], [None, None]
    loads = {"left": left_load}
    exchange = {}
    start = jnp.zeros((1, 160), F32)
    att_total = [start]

    def load():
        grad_load.wait()

    def pre():
        k = len(pre_puts)
        weight_loads[k].wait()
        slope_loads[k].wait()

        def step_rows(step, total):
            rows = pl.ds(pl.multiple_of(step * 512, 512), 512)
            value = dot_nn(grad[rows, :], weight[:, columns(k)])
            value = value * wide[rows, columns(k)].astype(F32)
            wide[rows, columns(k)] = value.astype(BF16)
            return total + jnp.sum(value, 0, keepdims=True)

        total = lax.fori_loop(0, count // 512, step_rows, jnp.zeros((1, SPAN), F32))
        sums[8 + 2 * turn[k] + core, :, :SPAN] = total
        pre_puts.append(local(wide.at[:, columns(k)], pre_out.at[:, columns(k)], 17 + k))
        weight_loads[k] = local(w_up_in.at[:, columns(k)], weight.at[:, columns(k)], 3 + k)

    def second_part(rows):
        return dot_nt(wide[rows, :], weight[...])

    def soth():
        for copy in weight_loads:
            copy.wait()

        def step_rows(step, _):
            rows = pl.ds(pl.multiple_of(other + step * 256, 256), 256)
            low = pl.ds(pl.multiple_of(step * 256, 256), 256)
            send_rows[low, :] = second_part(rows).astype(BF16)
            return 0

        lax.fori_loop(0, half // 256, step_rows, 0)

    def norm_back_rows(values, gain, above):
        center = values - jnp.mean(values, -1, keepdims=True)
        scale = lax.rsqrt(jnp.mean(center * center, -1, keepdims=True) + EPS)
        normed = center * scale
        scaled = above * gain
        back = scaled - jnp.mean(scaled, -1, keepdims=True)
        back = (back - normed * jnp.mean(scaled * normed, -1, keepdims=True)) * scale
        return back, jnp.sum(above * normed, 0, keepdims=True), jnp.sum(above, 0, keepdims=True)

    zero = jnp.zeros((1, features), F32)

    def ntwo():
        middle_load.wait()

        def step_rows(step, total):
            low = pl.ds(pl.multiple_of(step * 256, 256), 256)
            rows = pl.ds(pl.multiple_of(base + step * 256, 256), 256)
            above = second_part(rows) + got_rows[low, :].astype(F32)
            back, by_gain, by_shift = norm_back_rows(middle[low, :], gain_two[...], above)
            out_grad = grad[rows, :].astype(F32)
            below = out_grad + back
            middle[low, :] = below
            grad[rows, :] = below.astype(BF16)
            by_down, by_out = jnp.sum(out_grad, 0, keepdims=True), jnp.sum(below, 0, keepdims=True)
            return (total[0] + by_down, total[1] + by_out, total[2] + by_gain, total[3] + by_shift)

        parts = lax.fori_loop(0, half // 256, step_rows, (zero,) * 4)
        for i in range(4):
            sums[i, :, :] = parts[i]
        exchange["a"].wait_send()
        for copy in pre_puts[2:]:
            copy.wait()
        loads["weight"] = local(w_attn_in, weight, 3)
        loads["joined"] = [
            local(joined_in.at[turn[k]], wide.at[:, k * SPAN : (k + 1) * SPAN], 7 + k)
            for k in range(TURNS)
        ]

    def hand(name):
        if name == "a":
            exchange[name] = send(send_rows, got_rows, 84, to_core)
        elif name == "b":
            pl.semaphore_wait(credit.at[20], 1)
            exchange[name] = send(grad.at[own_rows], grad.at[own_rows], 85, to_core)
        else:
            exchange[name] = send(send_rows, got_rows, 86, to_core)

    def take(name):
        if name == "a":
            arrived(got_rows, 84)
        elif name == "b":
            arrived(grad.at[other_rows], 85)
        else:
            arrived(got_rows, 86)
            loads["tok"].wait()

    def produce(array, k):
        ready(k)
        if array < 2:
            if array == 0:
                right_loads[k % 2].wait()
                factor = grad
            else:
                pre_loads[k % 2].wait()
                if k == 0:
                    loads["left"].wait()
                factor = left

            def step_part(part, _):
                rows = pl.ds(pl.multiple_of(part * 640, 640), 640)
                product[k, rows, :] = dot_tn(factor[:, rows], right[k % 2]).astype(BF16)
                return 0

            lax.fori_loop(0, 2, step_part, 0)
            if array == 0 and k < 2:
                right_loads[k] = load_right(hidden_in, k + 2, k)
            elif array == 0:
                pre_puts[k - 2].wait()
                pre_loads[k - 2] = load_right(pre_out, k - 2, k - 2)
                if k == 3:
                    tell(20, to_core)
            elif k < 2:
                pre_loads[k] = load_right(pre_out, k + 2, k)
            if array == 1 and k == 3:
                loads["left"] = local(first_in, left, 11)
                loads["first"] = loads["left"]
        else:
            heads_load = local(heads_in.at[turn[k]], grad_heads, 4)
            if "first" in loads:
                loads.pop("first").wait()
            heads_load.wait()

            def step_part(part, _):
                rows = pl.ds(pl.multiple_of(part * 640, 640), 640)
                by_first = dot_tn(left[:, rows], wide[:, k * SPAN : k * SPAN + 480])
                by_branch = dot_tn(grad[:, rows], grad_heads[:, 96:256])
                product[k, rows, :] = jnp.concatenate([by_first, by_branch], -1).astype(BF16)
                return 0

            lax.fori_loop(0, 2, step_part, 0)
        stage_one(array, k)

    steps_done = {"hb": 0, "att": 0, "aend": 0, "none": 0, "reloc": 0}

    def count_step(name):
        steps_done[name] += 1
        return steps_done[name] - 1

    def hb():
        k = count_step("hb")
        if k == 0:
            loads["weight"].wait()
        slab = pl.ds(pl.multiple_of(turn[k] * SPAN + 384, 128), 256)

        def step_rows(step, _):
            rows = pl.ds(pl.multiple_of(step * 512, 512), 512)
            grad_heads[rows, :] = dot_nn(grad[rows, :], weight[:, slab]).astype(BF16)
            return 0

        lax.fori_loop(0, count // 512, step_rows, 0)
        loads["joined"][k].wait()
        totals_loads[k].wait()
        key_sum[...] = jnp.zeros_like(key_sum)
        value_sum[...] = jnp.zeros_like(value_sum)
        att_total[0] = start

    one_lane = (lax.broadcasted_iota(jnp.int32, (256, 48), 1) == 0).astype(F32).astype(BF16)

    def att():
        step_at = count_step("att")
        k, part = step_at // 3, step_at % 3
        low = k * SPAN

        def step_rows(step, total):
            rows = pl.ds(pl.multiple_of(step * 256, 256), 256)
            queries = wide[rows, low : low + 160]
            grads = grad_heads[rows, :]
            outs = []
            for head in range(2):
                at = head * HDIM
                query = queries[:, at : at + HDIM]
                above = grads[:, 96 + at : 96 + at + HDIM]
                key = wide[:, low + 160 + at : low + 160 + at + HDIM]
                value = wide[:, low + 320 + at : low + 320 + at + HDIM]
                scores = dot_nt(
                    jnp.concatenate([key, key_mask[:, :48]], -1),
                    jnp.concatenate([query, one_lane], -1),
                )
                probs = jnp.exp2(scores * (scaling * LOG2E) - totals[k, head : head + 1, rows])
                grad_probs = dot_nt(value, above)
                shared = jnp.sum(probs * grad_probs, 0, keepdims=True)
                grad_scores = (probs * (grad_probs - shared)).astype(BF16)
                value_sum[head, :, :HDIM] += dot_nn(probs.astype(BF16), above)
                key_sum[head, :, :HDIM] += dot_nn(grad_scores, query)
                outs.append(dot_tn(grad_scores, key) * scaling)
            joined = jnp.concatenate(outs, -1)
            wide[rows, low : low + 160] = joined.astype(BF16)
            return total + jnp.sum(joined, 0, keepdims=True)

        att_total[0] = lax.fori_loop(2 * part, 2 * part + 2, step_rows, att_total[0])

    def aend():
        k = count_step("aend")
        low = k * SPAN

        def step_rows(step, value_total):
            rows = pl.ds(pl.multiple_of(step * 256, 256), 256)
            keys = [key_sum[head, rows, :HDIM] * scaling for head in range(2)]
            values = [value_sum[head, rows, :HDIM] for head in range(2)]
            joined = jnp.concatenate(keys + values, -1)
            wide[rows, low + 160 : low + 480] = joined.astype(BF16)
            return value_total + jnp.sum(joined[:, 160:], 0, keepdims=True)

        value_total = lax.fori_loop(0, count // 256, step_rows, start)
        sums[16 + 2 * turn[k] + core, :, :160] = att_total[0]
        sums[16 + 2 * turn[k] + core, :, 160:320] = value_total

    def first_part(rows):
        total = None
        for k in range(TURNS):
            slab = pl.ds(pl.multiple_of(turn[k] * SPAN, 128), 480)
            part = dot_nt(wide[rows, k * SPAN : k * SPAN + 480], weight[:, slab])
            total = part if total is None else total + part
        return total

    def foth():
        for copy in staged[1:]:
            copy.wait_send()

        def step_rows(step, _):
            rows = pl.ds(pl.multiple_of(other + step * 256, 256), 256)
            low = pl.ds(pl.multiple_of(step * 256, 256), 256)
            send_rows[low, :] = first_part(rows).astype(BF16)
            return 0

        lax.fori_loop(0, half // 256, step_rows, 0)

    def none():
        step = count_step("none")
        low = slice(step * 256, step * 256 + 256)
        rows = pl.ds(pl.multiple_of(base + step * 256, 256), 256)
        above = first_part(rows) + got_rows[low, :].astype(F32)
        values = got_tok[low, :].astype(F32)
        back, by_gain, by_shift = norm_back_rows(values, gain_one[...], above)
        grad[half + step * 256 : half + step * 256 + 256, :] = (middle[low, :] + back).astype(BF16)
        if step == 0:
            sums[4, :, :] = by_gain
            sums[5, :, :] = by_shift
        else:
            sums[4, :, :] += by_gain
            sums[5, :, :] += by_shift

    got_tok = grad.at[0:half]

    def tokens_move(step):
        rows = pl.ds(step * 256, 256)
        source = grad.at[half + step * 256 : half + step * 256 + 256]
        away = remote(source, tokens_out.at[rows], 87 + step, to_clip)
        here = pltpu.make_async_copy(source, tokens_out.at[rows], local_sem.at[25 + step])
        return away, here

    def reloc():
        away, here = tokens_move(count_step("reloc"))

        @pl.when(moves)
        def _():
            away.start()

        @pl.when(jnp.logical_not(moves))
        def _():
            here.start()

    def wreloc():
        for step in range(half // 256):
            away, here = tokens_move(step)

            @pl.when(moves)
            def _(away=away):
                away.wait()

            @pl.when(jnp.logical_not(moves))
            def _(here=here):
                here.wait()

    hops = {"c": (0, to_core), "x": (1, to_x), "y": (2, to_y), "z1": (3, to_z_pair), "z2": (4, to_z[2])}
    hop_copies = {}

    def hs(name):
        index, device = hops[name]
        hop_copies[name] = send(sums, sums_got.at[index], 93 + index, device)

    def hw(name):
        index, _ = hops[name]
        hop_copies[name].wait_send()
        arrived(sums_got.at[index], 93 + index)
        sums[...] = sums[...] + sums_got[index]

    def token_load():
        exchange["b"].wait_send()
        loads["tok"] = local(tok_in, grad.at[0:half], 2)

    actions = {
        "load": load, "pre": pre, "soth": soth, "ntwo": ntwo, "hb": hb, "att": att, "aend": aend,
        "foth": foth, "none": none, "reloc": reloc, "wreloc": wreloc, "send": hand, "wait": take,
        "P": produce, "2": stage_two, "3": stage_three, "F": final_one, "G": final_two, "hs": hs, "hw": hw,
        "tok": token_load,
    }
    for name, *numbers in BACKWARD_STEPS:
        actions[name](*numbers)
    sums_put = local(sums, sums_out, 5)
    exchange["c"].wait_send()
    for wait in final_moves + last_moves:
        wait()
    for k in range(TURNS):
        ready(k)
    sums_put.wait()


def backward_pass(
    w_attn, w_up, w_down, tok, grad, first, second, joined, heads, middle, hidden, slope, totals, key_mask,
    gain_one, gain_two,
):
    half, features = tok.shape
    count = 2 * half
    any_space = pl.BlockSpec(memory_space=pl.ANY)
    vmem = pl.BlockSpec(memory_space=pltpu.VMEM)
    cols = TURNS * SPAN
    shapes = [
        ((half, features), BF16), ((UNIT // 2, 2 * SPAN), F32), ((UNIT // 2, 2 * SPAN), F32),
        ((UNIT // 2, 2 * SPAN), F32), ((24, 1, features), F32), ((count, cols), BF16),
    ]
    return pl.pallas_call(
        functools.partial(backward_kernel, HDIM ** (-0.5)),
        in_specs=[any_space] * 13 + [vmem] * 3,
        out_specs=[any_space] * len(shapes),
        out_shape=[jax.ShapeDtypeStruct(shape, kind) for shape, kind in shapes],
        scratch_shapes=[
            pltpu.VMEM((features, cols), BF16),
            pltpu.VMEM((count, features), BF16),
            pltpu.VMEM((count, features), BF16),
            pltpu.VMEM((count, cols), BF16),
            pltpu.VMEM((2, count, SPAN), BF16),
            pltpu.VMEM((count, 256), BF16),
            pltpu.VMEM((TURNS, 8, count), F32),
            pltpu.VMEM((half, features), F32),
            pltpu.VMEM((half, features), BF16),
            pltpu.VMEM((half, features), BF16),
            pltpu.VMEM((2, count, 128), F32),
            pltpu.VMEM((2, count, 128), F32),
            pltpu.VMEM((TURNS, features, SPAN), BF16),
            pltpu.VMEM((TURNS, UNIT, SPAN), BF16),
            pltpu.VMEM((TURNS, UNIT, SPAN), BF16),
            pltpu.VMEM((TURNS, UNIT, SPAN), BF16),
            pltpu.VMEM((TURNS, UNIT, SPAN), BF16),
            pltpu.VMEM((UNIT, SPAN), BF16),
            pltpu.VMEM((UNIT, SPAN), F32),
            pltpu.VMEM((3, UNIT // 2, SPAN), F32),
            pltpu.VMEM((24, 1, features), F32),
            pltpu.VMEM((5, 24, 1, features), F32),
            pltpu.SemaphoreType.DMA((100,)),
            pltpu.SemaphoreType.DMA((100,)),
            pltpu.SemaphoreType.DMA((32,)),
            pltpu.SemaphoreType.REGULAR((24,)),
        ],
        cost_estimate=pl.CostEstimate(
            flops=4 * count * features * 6400, bytes_accessed=90_000_000, transcendentals=30_000_000
        ),
        compiler_params=pltpu.CompilerParams(
            vmem_limit_bytes=60 << 20, collective_id=1, has_side_effects=True
        ),
        name="backward_pass",
    )(
        w_attn, w_up, w_down, tok, grad, first, second, joined, heads, middle, hidden, slope, totals,
        key_mask, gain_one, gain_two,
    )


class Links:
    def __init__(self):
        self.dp = lax.axis_size("dp")
        self.tensor = lax.axis_size("tensor")
        self.tensor_pos = lax.axis_index("tensor")
        self.half = self.tensor_pos % 2

    def pair(self, value):
        return lax.ppermute(value, "tensor", [(i, i ^ 1) for i in range(self.tensor)])

    def columns(self, shard):
        rows, _, width = shard.shape
        whole = lax.all_gather(shard, ("dp", "tensor"), axis=0)
        whole = lax.dynamic_index_in_dim(whole, self.half, 2, keepdims=False)
        whole = whole.reshape(self.dp, self.tensor, rows, width)
        return [whole[:, k].reshape(self.dp * rows, width) for k in range(self.tensor)]

    def vectors(self, value):
        whole = lax.all_gather(value, "tensor", axis=0)
        return [whole[k] for k in range(self.tensor)]

    def place(self, pieces):
        halves = (jnp.arange(2) == self.half)[None, :, None]
        return jnp.where(halves, jnp.stack(pieces)[:, None, :], 0.0)

    def gradient(self, left, rights):
        whole = jnp.stack([dot_tn(left, right).astype(BF16) for right in rights], 0)
        features, width = whole.shape[1:]
        whole = whole.reshape(self.tensor, self.dp, features // self.dp, width)
        whole = jnp.moveaxis(whole, 1, 0)[:, :, :, None, :]
        halves = (jnp.arange(2) == self.half)[None, None, None, :, None]
        whole = jnp.where(halves, whole, jnp.zeros((), BF16))
        whole = whole.reshape((self.dp * self.tensor,) + whole.shape[2:])
        return lax.psum_scatter(whole, ("dp", "tensor"), tiled=False).astype(F32)

    def merged(self, partial_of):
        got = self.pair(partial_of(1).astype(BF16))
        return partial_of(0) + got.astype(F32)


def summed(vectors, total):
    whole = total(jnp.concatenate(vectors))
    at = 0
    result = []
    for vector in vectors:
        result.append(whole[at : at + vector.shape[0]])
        at += vector.shape[0]
    return result


def halves_of(weight):
    return weight.reshape(weight.shape[0], 2, weight.shape[1] // 2)


def flat(piece):
    return piece.reshape(piece.shape[0], -1)


def local_any(
    tokens,
    lengths,
    cotangent,
    norm1_gain,
    norm1_shift,
    query_weight,
    query_bias,
    key_weight,
    value_weight,
    value_bias,
    out_weight,
    out_bias,
    norm2_gain,
    norm2_shift,
    up_weight,
    up_bias,
    down_weight,
    down_bias,
):
    links = Links()
    rows = tokens.shape[0]
    scaling = HDIM ** (-0.5)
    width = query_weight.shape[1] // 2
    heads = width // HDIM
    units = up_weight.shape[1] // 2
    count = links.tensor

    shard_attn = [query_weight, key_weight, value_weight, out_weight.T]
    w_attn = links.columns(jnp.concatenate([halves_of(w) for w in shard_attn], -1))
    w_up = jnp.concatenate(links.columns(halves_of(up_weight)), 1)
    w_down = jnp.concatenate(links.columns(halves_of(down_weight.T)), 1)
    w_qkv = [block[:, : 3 * width] for block in w_attn]
    w_out = [block[:, 3 * width :] for block in w_attn]
    small = [query_bias.reshape(2, width), value_bias.reshape(2, width), up_bias.reshape(2, units)]
    small = jnp.concatenate(small, -1)
    small = links.vectors(jnp.where(links.half == 0, small[0], small[1]))
    bias_qkv = [
        jnp.concatenate([v[:width], jnp.zeros((width,), F32), v[width : 2 * width]]) for v in small
    ]
    bias_up = jnp.concatenate([v[2 * width :] for v in small])

    place = links.tensor_pos // 2
    clip_length = jnp.sum(jnp.where(jnp.arange(lengths.shape[0]) == place, lengths, 0))
    frames = jnp.arange(rows)
    frames = jnp.concatenate([links.half * rows + frames, (1 - links.half) * rows + frames])
    visible = frames < clip_length
    mask = jnp.where(visible, 0.0, -1e30).astype(F32)

    def part_of(value, part):
        return value[part * rows : (part + 1) * rows]

    def both(value):
        return jnp.concatenate([value, links.pair(value)])

    source = tokens.astype(F32)
    first = both(norm_rows(source, norm1_gain, norm1_shift).astype(BF16))
    joined, heads_out, totals = [], [], []
    for k in range(count):
        joined.append((dot_nn(first, w_qkv[k]) + bias_qkv[k]).astype(BF16))
        mixed, total = attend(joined[k], mask[None, :], heads, scaling)
        heads_out.append(mixed)
        totals.append(total)
    heads_all = jnp.concatenate(heads_out, 1)
    w_out_all = jnp.concatenate(w_out, 1)
    branch = links.merged(lambda part: dot_nt(part_of(heads_all, part), w_out_all))
    middle = source + branch + out_bias
    second = both(norm_rows(middle, norm2_gain, norm2_shift).astype(BF16))
    hidden, slope = up_gelu(second, w_up, bias_up[None, :])
    out_own = cotangent * visible[:rows].astype(BF16)[:, None]
    out_grad = both(out_own)

    def cut(value):
        return [value[:, k * units : (k + 1) * units] for k in range(count)]

    grad_down = links.gradient(out_grad, cut(hidden))
    down_out = links.merged(lambda part: dot_nt(part_of(hidden, part), w_down))
    layer_out = (middle + down_out + down_bias).astype(BF16)
    grad_pre = (dot_nn(out_grad, w_down) * slope.astype(F32)).astype(BF16)
    grad_up = links.gradient(second, cut(grad_pre))
    grad_second = links.merged(lambda part: dot_nt(part_of(grad_pre, part), w_up))
    back_two, grad_gain_two, grad_shift_two = norm_back(middle, norm2_gain, grad_second)
    grad_middle = out_own.astype(F32) + back_two
    branch_grad = both(grad_middle.astype(BF16))
    grad_heads = [dot_nn(branch_grad, w_out[k]).astype(BF16) for k in range(count)]
    grad_out_w = links.gradient(branch_grad, heads_out)
    grad_joined, sums = [], []
    for k in range(count):
        back, sum_k = attend_back(joined[k], grad_heads[k], totals[k], mask[:, None], heads, scaling)
        grad_joined.append(back)
        sums.append(sum_k)
    grad_qkv = links.gradient(first, grad_joined)
    grad_all = jnp.concatenate(grad_joined, 1)
    w_qkv_all = jnp.concatenate(w_qkv, 1)
    grad_first = links.merged(lambda part: dot_nt(part_of(grad_all, part), w_qkv_all))
    back_one, grad_gain_one, grad_shift_one = norm_back(source, norm1_gain, grad_first)
    grad_tokens = (grad_middle + back_one).astype(BF16)

    vectors = [
        links.place([v[0] for v in cut(jnp.sum(grad_pre.astype(F32), 0)[None, :])]).reshape(-1),
        links.place([s[0, :width] for s in sums]).reshape(-1),
        links.place([s[1, :width] for s in sums]).reshape(-1),
        grad_gain_one,
        grad_shift_one,
        jnp.sum(grad_middle, 0),
        grad_gain_two,
        grad_shift_two,
        jnp.sum(out_own.astype(F32), 0),
    ]
    sum_up, sum_query, sum_value, *rest = summed(
        vectors, lambda value: lax.psum(value, ("dp", "tensor"))
    )
    sum_gain_one, sum_shift_one, sum_out, sum_gain_two, sum_shift_two, sum_down = rest

    def own(vector):
        size = vector.shape[0] // count
        return lax.dynamic_slice_in_dim(vector, links.tensor_pos * size, size, 0)

    return (
        layer_out,
        grad_tokens,
        sum_gain_one,
        sum_shift_one,
        flat(grad_qkv[:, :, :width]),
        own(sum_query),
        flat(grad_qkv[:, :, width : 2 * width]),
        flat(grad_qkv[:, :, 2 * width :]),
        own(sum_value),
        flat(grad_out_w).T,
        sum_out,
        sum_gain_two,
        sum_shift_two,
        flat(grad_up),
        own(sum_up),
        flat(grad_down).T,
        sum_down,
    )


def local_chips(
    tokens,
    lengths,
    cotangent,
    norm1_gain,
    norm1_shift,
    query_weight,
    query_bias,
    key_weight,
    value_weight,
    value_bias,
    out_weight,
    out_bias,
    norm2_gain,
    norm2_shift,
    up_weight,
    up_bias,
    down_weight,
    down_bias,
):
    dp, z = lax.axis_index("dp"), lax.axis_index("tensor")
    core, plane = dp % 2, dp // 2
    half = tokens.shape[0]
    count = 2 * half
    width, units = 160, SPAN

    def split(weight):
        return jnp.moveaxis(halves_of(weight), 1, 0)

    shards = (
        jnp.concatenate([split(w) for w in (query_weight, key_weight, value_weight, out_weight.T)], -1),
        split(up_weight),
        split(down_weight.T),
    )
    place = jnp.sum(jnp.where(jnp.arange(lengths.shape[0]) == z // 2, lengths, 0))
    mask = jnp.where(jnp.arange(count) < place, 0.0, -1e30).astype(F32)
    mask = jnp.broadcast_to(mask[None, :], (8, count))
    valid = ((z % 2) * half + jnp.arange(half) < place).astype(BF16)
    small = [query_bias.reshape(2, width), jnp.zeros((2, width), F32), value_bias.reshape(2, width)]
    small = jnp.concatenate(small + [jnp.zeros((2, width), F32)], -1)
    small = jnp.stack([small, up_bias.reshape(2, units)], 1)
    small = jnp.pad(jnp.where(core == 0, small[0], small[1]), ((0, 6), (0, 0)))
    (
        w_attn, w_up, w_down, tok, out_grad, mask, first, second, joined, heads, totals, middle, hidden,
        slope,
    ) = forward_pass(
        shards, tokens, cotangent * valid[:, None], mask, small,
        norm1_gain[None, :], norm1_shift[None, :], norm2_gain[None, :], norm2_shift[None, :],
        out_bias[None, :],
    )

    def pair(value):
        return lax.ppermute(value, "dp", [(i, i ^ 1) for i in range(8)])

    def move_rows(value):
        swaps = [
            (a * 4 + b, (a ^ 1) * 4 + (b ^ 1)) for a in range(8) for b in range(4) if a % 2 != b % 2
        ]
        moved = lax.ppermute(value, ("dp", "tensor"), swaps)
        return jnp.where(core == z % 2, value, moved)

    def part_of(value, part):
        start = (core if part == 0 else 1 - core) * half
        return lax.dynamic_slice_in_dim(value, start, half, 0)

    got = pair(dot_nt(part_of(hidden, 1), w_down).astype(BF16))
    layer_out = middle + dot_nt(part_of(hidden, 0), w_down) + got.astype(F32) + down_bias
    layer_out = move_rows(layer_out.astype(BF16))

    lane = jnp.arange(128)[None, :] == 0
    key_mask = jnp.where(lane, mask[0][:, None], 0.0).astype(BF16)
    grad_tokens, grad_down, grad_up, grad_attn, sums, _ = backward_pass(
        w_attn, w_up, w_down, tok, out_grad, first, second, joined, heads, middle, hidden, slope, totals,
        key_mask, norm1_gain[None, :], norm2_gain[None, :],
    )

    def piece(index):
        start = index * width
        both = [grad_attn[:, i * SPAN + start : i * SPAN + start + width] for i in range(2)]
        return jnp.concatenate(both, 1)

    def own(first_row, start, size):
        rows = lax.dynamic_slice_in_dim(sums[:, 0], first_row + 2 * z, 2, 0)
        return rows[:, start : start + size].reshape(-1)

    return (
        layer_out,
        grad_tokens,
        sums[4, 0],
        sums[5, 0],
        piece(0),
        own(16, 0, width),
        piece(1),
        piece(2),
        own(16, width, width),
        piece(3).T,
        sums[1, 0],
        sums[2, 0],
        sums[3, 0],
        grad_up,
        own(8, 0, units),
        grad_down.T,
        sums[0, 0],
    )


def solution(mesh):
    rows = P(("dp", "tensor"), None)
    wide, tall = P("dp", "tensor"), P("tensor", "dp")
    piece, same = P("tensor"), P()
    chips = mesh.shape["dp"] == 8 and mesh.shape["tensor"] == 4
    return jax.shard_map(
        local_chips if chips else local_any,
        mesh=mesh,
        in_specs=(
            rows, P("dp"), rows, same, same, wide, piece, wide, wide, piece, tall, same, same, same,
            wide, piece, tall, same,
        ),
        out_specs=(
            rows, rows, same, same, wide, piece, wide, wide, piece, tall, same, same, same, wide, piece,
            tall, same,
        ),
        check_vma=False,
    )
```

```python
import functools

import jax
import jax.numpy as jnp
from jax import lax
from jax.experimental import pallas as pl
from jax.experimental.pallas import tpu as pltpu
from jax.sharding import PartitionSpec as P

HDIM = 80
EPS = 1e-05
LOG2E = 1.4426950408889634
F32 = jnp.float32
BF16 = jnp.bfloat16


def norm_rows(values, norm_gain, norm_shift):
    center = values - jnp.mean(values, -1, keepdims=True)
    spread = jnp.mean(center * center, -1, keepdims=True)
    return center * lax.rsqrt(spread + EPS) * norm_gain + norm_shift


def norm_back(values, norm_gain, grad):
    center = values - jnp.mean(values, -1, keepdims=True)
    scale = lax.rsqrt(jnp.mean(center * center, -1, keepdims=True) + EPS)
    normed = center * scale
    scaled = grad * norm_gain
    back = scaled - jnp.mean(scaled, -1, keepdims=True)
    back = (back - normed * jnp.mean(scaled * normed, -1, keepdims=True)) * scale
    return back, jnp.sum(grad * normed, 0), jnp.sum(grad, 0)


def dot_nn(left, right):
    return jnp.dot(left, right, preferred_element_type=F32)


def dot_tn(left, right):
    return lax.dot_general(left, right, (((0,), (0,)), ((), ())), preferred_element_type=F32)


def dot_nt(left, right):
    return lax.dot_general(left, right, (((1,), (1,)), ((), ())), preferred_element_type=F32)


def up_kernel(rows_ref, weight_ref, bias_ref, hidden_ref, slope_ref):
    pre = dot_nn(rows_ref[...], weight_ref[...]) + bias_ref[...]
    cdf = 0.5 * lax.erf(pre * (0.5**0.5)) + 0.5
    density = jnp.exp(-0.5 * pre * pre) * 0.3989422804014327
    hidden_ref[...] = (pre * cdf).astype(BF16)
    slope_ref[...] = (cdf + pre * density).astype(BF16)


def up_gelu(rows, weight, bias):
    count, depth = rows.shape
    cols = weight.shape[1]
    block_rows, block_cols = min(512, count), min(640, cols)
    return pl.pallas_call(
        up_kernel,
        grid=(cols // block_cols, count // block_rows),
        in_specs=[
            pl.BlockSpec((block_rows, depth), lambda n, m: (m, 0)),
            pl.BlockSpec((depth, block_cols), lambda n, m: (0, n)),
            pl.BlockSpec((1, block_cols), lambda n, m: (0, n)),
        ],
        out_specs=[
            pl.BlockSpec((block_rows, block_cols), lambda n, m: (m, n)),
            pl.BlockSpec((block_rows, block_cols), lambda n, m: (m, n)),
        ],
        out_shape=[jax.ShapeDtypeStruct((count, cols), BF16)] * 2,
        cost_estimate=pl.CostEstimate(
            flops=2 * count * depth * cols, bytes_accessed=20_000_000, transcendentals=0
        ),
        compiler_params=pltpu.CompilerParams(vmem_limit_bytes=40 << 20),
        name="up_gelu",
    )(rows, weight, bias)


def attend_kernel(heads, scaling, query_ref, all_ref, mask_ref, out_ref, total_ref):
    width = heads * HDIM
    queries = query_ref[...]
    mask = mask_ref[...]
    outs, totals = [], []
    for head in range(heads):
        low = head * HDIM
        query = queries[:, low : low + HDIM]
        key = all_ref[:, width + low : width + low + HDIM]
        value = all_ref[:, 2 * width + low : 2 * width + low + HDIM]
        scores = dot_nt(query, key) * (scaling * LOG2E) + mask
        row_max = jnp.max(scores, -1, keepdims=True)
        exp_scores = jnp.exp2(scores - row_max)
        total = jnp.sum(exp_scores, -1, keepdims=True)
        mixed = dot_nn(exp_scores.astype(BF16), value)
        outs.append(mixed * (1.0 / total))
        totals.append(row_max + jnp.log2(total))
    out_ref[...] = jnp.concatenate(outs, -1).astype(BF16)
    for head in range(heads):
        wide = jnp.broadcast_to(totals[head], (totals[head].shape[0], 128))
        total_ref[head : head + 1, :] = wide.T[0:1, :]


def attend(joined, mask_row, heads, scaling):
    count, cols = joined.shape
    block_rows = min(256, count)
    width = heads * HDIM
    return pl.pallas_call(
        functools.partial(attend_kernel, heads, scaling),
        grid=(count // block_rows,),
        in_specs=[
            pl.BlockSpec((block_rows, cols), lambda m: (m, 0)),
            pl.BlockSpec((count, cols), lambda m: (0, 0)),
            pl.BlockSpec((1, count), lambda m: (0, 0)),
        ],
        out_specs=[
            pl.BlockSpec((block_rows, width), lambda m: (m, 0)),
            pl.BlockSpec((heads, block_rows), lambda m: (0, m)),
        ],
        out_shape=[
            jax.ShapeDtypeStruct((count, width), BF16),
            jax.ShapeDtypeStruct((heads, count), F32),
        ],
        cost_estimate=pl.CostEstimate(
            flops=2 * heads * count * count * 512,
            bytes_accessed=4_000_000,
            transcendentals=heads * count * count,
        ),
        compiler_params=pltpu.CompilerParams(vmem_limit_bytes=48 << 20),
        name="attend",
    )(joined, joined, mask_row)


def attend_back_kernel(
    heads, scaling, query_ref, all_ref, grad_ref, total_ref, mask_ref,
    out_ref, sums_ref, key_sum, value_sum,
):
    step = pl.program_id(0)
    steps = pl.num_programs(0)
    width = heads * HDIM
    block_rows = query_ref.shape[0]

    @pl.when(step == 0)
    def _():
        key_sum[...] = jnp.zeros_like(key_sum)
        value_sum[...] = jnp.zeros_like(value_sum)
        sums_ref[...] = jnp.zeros_like(sums_ref)

    queries = query_ref[...]
    grads = grad_ref[...]
    query_outs = []
    for head in range(heads):
        low = head * HDIM
        query = queries[:, low : low + HDIM]
        grad = grads[:, low : low + HDIM]
        key = all_ref[:, width + low : width + low + HDIM]
        value = all_ref[:, 2 * width + low : 2 * width + low + HDIM]
        scores = dot_nt(key, query) * (scaling * LOG2E) + mask_ref[...]
        probs = jnp.exp2(scores - total_ref[head : head + 1, :])
        grad_probs = dot_nt(value, grad)
        shared = jnp.sum(probs * grad_probs, 0, keepdims=True)
        grad_scores = (probs * (grad_probs - shared)).astype(BF16)
        value_sum[head, :, :HDIM] += dot_nn(probs.astype(BF16), grad)
        key_sum[head, :, :HDIM] += dot_nn(grad_scores, query)
        query_outs.append(dot_tn(grad_scores, key) * scaling)
    joined = jnp.concatenate(query_outs, -1)
    sums_ref[0:1, :width] += jnp.sum(joined, 0, keepdims=True)
    rows = pl.ds(pl.multiple_of(step * block_rows, block_rows), block_rows)
    out_ref[rows, :width] = joined.astype(BF16)

    @pl.when(step == steps - 1)
    def _():
        keys = jnp.concatenate([key_sum[head, :, :HDIM] for head in range(heads)], -1)
        values = jnp.concatenate([value_sum[head, :, :HDIM] for head in range(heads)], -1)
        sums_ref[1:2, :width] = jnp.sum(values, 0, keepdims=True)
        out_ref[:, width:] = jnp.concatenate([keys * scaling, values], -1).astype(BF16)


def attend_back(joined, grad_heads, totals, mask_col, heads, scaling):
    count, cols = joined.shape
    block_rows = min(256, count)
    width = heads * HDIM
    return pl.pallas_call(
        functools.partial(attend_back_kernel, heads, scaling),
        grid=(count // block_rows,),
        in_specs=[
            pl.BlockSpec((block_rows, cols), lambda m: (m, 0)),
            pl.BlockSpec((count, cols), lambda m: (0, 0)),
            pl.BlockSpec((block_rows, width), lambda m: (m, 0)),
            pl.BlockSpec((heads, block_rows), lambda m: (0, m)),
            pl.BlockSpec((count, 1), lambda m: (0, 0)),
        ],
        out_specs=[
            pl.BlockSpec((count, cols), lambda m: (0, 0)),
            pl.BlockSpec((8, 256), lambda m: (0, 0)),
        ],
        out_shape=[
            jax.ShapeDtypeStruct((count, cols), BF16),
            jax.ShapeDtypeStruct((8, 256), F32),
        ],
        scratch_shapes=[
            pltpu.VMEM((heads, count, 128), F32),
            pltpu.VMEM((heads, count, 128), F32),
        ],
        cost_estimate=pl.CostEstimate(
            flops=2 * heads * count * count * 1280,
            bytes_accessed=5_000_000,
            transcendentals=heads * count * count,
        ),
        compiler_params=pltpu.CompilerParams(vmem_limit_bytes=56 << 20),
        name="attend_back",
    )(joined, joined, grad_heads, totals, mask_col)


UNIT = 320
SPAN = 640
TURNS = 4


def clamp_rows(ref, start, size):
    return ref.at[pl.ds(pl.multiple_of(start, 16), size)]


FORWARD_STEPS = (
    ("pr", 0), ("tok",), ("pr", 1), ("zz", 0), ("pp", 0, 0), ("pp", 1, 0), ("pr", 2), ("fw", 0, 0),
    ("fw", 1, 0), ("tokw",), ("pp", 2, 0), ("norm",), ("send", "a"), ("wait", "a"), ("pp", 0, 1), ("proj",),
    ("fw", 2, 0), ("att",), ("att",), ("fw", 0, 1), ("zz", 1), ("pp", 0, 2), ("pp", 0, 3), ("proj",),
    ("att",), ("att",), ("zz", 2), ("fw", 0, 2), ("fw", 0, 3), ("pp", 1, 1), ("cot",), ("pp", 1, 2),
    ("proj",), ("att",), ("att",), ("pp", 1, 3), ("proj",), ("att",), ("pp", 2, 1), ("att",), ("fw", 1, 3),
    ("fw", 1, 2), ("both",), ("send", "b"), ("bown",), ("wait", "b"), ("fw", 1, 1), ("ntwo",),
    ("send", "c"), ("fw", 2, 1), ("pp", 2, 2), ("wait", "c"), ("pp", 2, 3), ("lift",), ("lift",), ("lift",),
    ("lift",), ("down",), ("fw", 2, 2), ("fw", 2, 3), ("cotx",), ("down",), ("down",), ("cotw",), ("down",),
)


def forward_kernel(
    scaling,
    lengths, attn_shard, up_shard, down_shard, tokens, cotangent, bias_in,
    gain_one, shift_one, gain_two, shift_two, bias_out, bias_down,
    w_attn_out, w_up_out, w_down, tokens_out, grad_out, mask_out, first_out, second_out, joined_out,
    heads_out, totals_out, middle_out, hidden_out, slope_out, layer_own_out, layer_other_out,
    w_attn, w_up, tok, first, second, joined, heads, middle, send_rows, got_rows, layer_other, slope,
    mask_own, mask, totals, bias, params, send_sem, recv_sem, local_sem,
):
    dp, z = lax.axis_index("dp"), lax.axis_index("tensor")
    core, plane = lax.rem(dp, 2), lax.div(dp, 2)
    x_bit, y_bit = lax.rem(plane, 2), lax.div(plane, 2)
    half = tok.shape[0]
    count = 2 * half
    to_x = (y_bit * 4 + (1 - x_bit) * 2 + core, z)
    to_y = ((1 - y_bit) * 4 + x_bit * 2 + core, z)
    to_core = (plane * 2 + 1 - core, z)
    to_clip = (plane * 2 + 1 - core, z + 1 - 2 * lax.rem(z, 2))
    to_z = [(dp, lax.rem(z + k, TURNS)) for k in range(TURNS)]
    moves = core != lax.rem(z, 2)
    plane_x = y_bit * 2 + 1 - x_bit
    plane_y = (1 - y_bit) * 2 + x_bit
    plane_xy = (1 - y_bit) * 2 + 1 - x_bit
    turn = [lax.rem(z + TURNS - k, TURNS) for k in range(TURNS)]
    base = pl.multiple_of(core * half, 256)
    other = pl.multiple_of((1 - core) * half, 256)
    own_rows, other_rows = pl.ds(base, half), pl.ds(other, half)

    barrier = pltpu.get_barrier_semaphore()
    partners = [to_x, to_y, to_core, to_clip] + to_z[1:]
    for partner in partners:
        pl.semaphore_signal(barrier, inc=1, device_id=partner, device_id_type=pl.DeviceIdType.MESH)
    pl.semaphore_wait(barrier, len(partners))

    def remote(source, target, sem, device):
        return pltpu.make_async_remote_copy(
            src_ref=source,
            dst_ref=target,
            send_sem=send_sem.at[sem],
            recv_sem=recv_sem.at[sem],
            device_id=device,
            device_id_type=pl.DeviceIdType.MESH,
        )

    sent = {}

    def send(source, target, sem, device):
        copy = remote(source, target, sem, device)
        copy.start()
        sent[sem] = copy
        return copy

    def arrived(target, sem):
        remote(target, target, sem, to_core).wait_recv()

    outs = {}

    def put(source, target, sem):
        copy = pltpu.make_async_copy(source, target, local_sem.at[sem])
        copy.start()
        outs[sem] = copy

    def done(sem):
        outs.pop(sem).wait()

    weights = [w_attn, w_up, w_down]
    shards = [attn_shard, up_shard, down_shard]
    rows_half = UNIT // 2

    def columns(k):
        return pl.ds(pl.multiple_of(turn[k] * SPAN, 128), SPAN)

    def block(array, k, where, part=None):
        if part is None:
            rows = pl.ds(pl.multiple_of(where * UNIT, 16), UNIT)
        else:
            rows = pl.ds(pl.multiple_of(where * UNIT + part * rows_half, 16), rows_half)
        return weights[array].at[rows, columns(k)]

    def own_piece(array, which):
        rows = pl.ds(pl.multiple_of(plane * UNIT + which * rows_half, 16), rows_half)
        return weights[array].at[rows, columns(0)]

    def shard_half(array, which):
        return shards[array].at[:, pl.ds(pl.multiple_of(which * SPAN, 128), SPAN)]

    pairs = [None] * 3

    def pair_start(array):
        send(shard_half(array, 1 - core), own_piece(array, core), 72 + array, to_core)
        copy = pltpu.make_async_copy(
            shard_half(array, core), own_piece(array, core), local_sem.at[array]
        )
        copy.start()
        pairs[array] = copy

    def pair_wait(array):
        if pairs[array] is not None:
            pairs[array].wait()
            arrived(own_piece(array, 1 - core), 72 + array)
            pairs[array] = None

    def sem_of(array, kind, k):
        return array * 24 + kind * 4 + k

    def plane_send(array, k):
        if k == 0:
            pair_wait(array)
        else:
            arrived(block(array, k, plane), sem_of(array, 0, k))
        source = block(array, k, plane)
        send(source, source, sem_of(array, 1, k), to_x)
        send(source, source, sem_of(array, 2, k), to_y)

    def line_send(array):
        pair_wait(array)
        source = block(array, 0, plane)
        for k in range(1, TURNS):
            send(source, source, sem_of(array, 0, k), to_z[k])

    def forward_on(array, k):
        arrived(block(array, k, plane_x), sem_of(array, 1, k))
        source = block(array, k, plane_x, 0)
        send(source, source, sem_of(array, 3, k), to_y)
        arrived(block(array, k, plane_y), sem_of(array, 2, k))
        source = block(array, k, plane_y, 1)
        send(source, source, sem_of(array, 4, k), to_x)

    def complete(array, k):
        for part in range(2):
            arrived(block(array, k, plane_xy, part), sem_of(array, 3 + part, k))

    there = grad_out.at[other_rows]
    here = grad_out.at[own_rows]
    length = lengths[lax.div(z, 2)]
    frames = lax.broadcasted_iota(jnp.int32, mask_own.shape, 1)
    mask_own[...] = jnp.where(frames < length, 0.0, -1e30).astype(F32)
    tok_copy = pltpu.make_async_copy(tokens, tok, local_sem.at[3])
    mask_copy = pltpu.make_async_copy(mask_own, mask, local_sem.at[4])
    clip_tok = remote(tokens, tok, 75, to_clip)
    clip_mask = remote(mask_own, mask, 76, to_clip)
    cot_copy = pltpu.make_async_copy(send_rows, here, local_sem.at[5])
    clip_cot = remote(send_rows, there, 77, to_clip)
    bias_copy = pltpu.make_async_copy(bias_in, bias.at[z], local_sem.at[6])
    exchange = {}
    for i, vector in enumerate((gain_one, shift_one, gain_two, shift_two, bias_out, bias_down)):
        params[i : i + 1, :] = vector[...][None, :]

    def tok_start():
        @pl.when(moves)
        def _():
            clip_mask.start()
            clip_tok.start()

        @pl.when(jnp.logical_not(moves))
        def _():
            tok_copy.start()
            mask_copy.start()

        bias_copy.start()
        for k in range(1, TURNS):
            send(bias_in, bias.at[z], 77 + k, to_z[k])
        put(cotangent, send_rows, 7)

    def tok_wait():
        @pl.when(moves)
        def _():
            clip_mask.wait()
            clip_tok.wait()

        @pl.when(jnp.logical_not(moves))
        def _():
            tok_copy.wait()
            mask_copy.wait()

        put(tok, tokens_out, 8)
        put(mask, mask_out, 9)

    def cot_start():
        done(7)

        def step_rows(step, _):
            rows = pl.ds(pl.multiple_of(step * 256, 256), 256)
            at = lax.broadcasted_iota(jnp.int32, (256, send_rows.shape[1]), 0)
            at = at + (lax.rem(z, 2) * half + step * 256)
            values = jnp.where(at < length, send_rows[rows, :].astype(F32), 0.0)
            send_rows[rows, :] = values.astype(BF16)
            return 0

        lax.fori_loop(0, half // 256, step_rows, 0)

        @pl.when(moves)
        def _():
            clip_cot.start()

        @pl.when(jnp.logical_not(moves))
        def _():
            cot_copy.start()

    def cot_pair():
        @pl.when(moves)
        def _():
            arrived(here, 77)

        send(here, here, 81, to_core)

    def cot_wait():
        arrived(there, 81)

    def norm():
        def step_rows(step, _):
            rows = pl.ds(pl.multiple_of(step * 256, 256), 256)
            values = tok[rows, :].astype(F32)
            normed = norm_rows(values, params[0:1, :], params[1:2, :])
            first[pl.ds(pl.multiple_of(base + step * 256, 256), 256), :] = normed.astype(BF16)
            return 0

        lax.fori_loop(0, half // 256, step_rows, 0)

    def hand(name):
        if name == "a":
            exchange[name] = send(first.at[own_rows], first.at[own_rows], 82, to_core)
        elif name == "b":
            exchange[name] = send(send_rows, got_rows, 83, to_core)
        else:
            exchange[name] = send(second.at[own_rows], second.at[own_rows], 84, to_core)

    def take(name):
        if name == "a":
            arrived(first.at[other_rows], 82)
            put(first, first_out, 10)
            bias_copy.wait()
            for k in range(1, TURNS):
                arrived(bias.at[turn[k]], 77 + k)
        elif name == "b":
            arrived(got_rows, 83)
        else:
            arrived(second.at[other_rows], 84)
            put(second, second_out, 11)

    steps_done = {"proj": 0, "att": 0, "lift": 0, "down": 0}

    def count_step(name):
        steps_done[name] += 1
        return steps_done[name] - 1

    def proj():
        k = count_step("proj")
        complete(0, k)
        slab = pl.ds(pl.multiple_of(turn[k] * SPAN, 128), 480)

        def step_rows(step, _):
            rows = pl.ds(pl.multiple_of(step * half, half), half)
            product = dot_nn(first[rows, :], w_attn[:, slab]) + bias[turn[k], 0:1, :480]
            joined[k, rows, :480] = product.astype(BF16)
            return 0

        lax.fori_loop(0, 2, step_rows, 0)
        put(joined.at[k], joined_out.at[turn[k]], 12 + k)
        if k == TURNS - 1:
            put(w_attn, w_attn_out, 24)

    def att():
        step_at = count_step("att")
        k, part = step_at // 2, step_at % 2

        def step_rows(step, _):
            rows = pl.ds(pl.multiple_of(step * 256, 256), 256)
            queries = joined[k, rows, :160]
            mixes, logs = [jnp.zeros((256, 96), F32)], []
            for head in range(2):
                low = head * HDIM
                query = queries[:, low : low + HDIM]
                key = joined[k, :, 160 + low : 160 + low + HDIM]
                value = joined[k, :, 320 + low : 320 + low + HDIM]
                scores = dot_nt(query, key) * (scaling * LOG2E) + mask[0:1, :]
                row_max = jnp.max(scores, -1, keepdims=True)
                exp_scores = jnp.exp2(scores - row_max)
                total = jnp.sum(exp_scores, -1, keepdims=True)
                mixes.append(dot_nn(exp_scores.astype(BF16), value) * (1.0 / total))
                logs.append(row_max + jnp.log2(total))
            heads[k, rows, :] = jnp.concatenate(mixes, -1).astype(BF16)
            for head in range(2):
                wide = jnp.broadcast_to(logs[head], (256, 128))
                totals[k, head : head + 1, rows] = wide.T[0:1, :]
            return 0

        lax.fori_loop(3 * part, 3 * part + 3, step_rows, 0)
        if part == 1:
            put(heads.at[k], heads_out.at[turn[k]], 16 + k)
            put(totals.at[k], totals_out.at[turn[k]], 20 + k)

    def branch(rows):
        total = None
        for k in range(TURNS):
            slab = pl.ds(pl.multiple_of(turn[k] * SPAN + 384, 128), 256)
            product = dot_nt(heads[k, rows, :], w_attn[:, slab])
            total = product if total is None else total + product
        return total

    def both():
        @pl.when(moves)
        def _():
            clip_cot.wait_send()

        @pl.when(jnp.logical_not(moves))
        def _():
            cot_copy.wait()

        def step_rows(step, _):
            rows = pl.ds(pl.multiple_of(other + step * 256, 256), 256)
            low = pl.ds(pl.multiple_of(step * 256, 256), 256)
            send_rows[low, :] = branch(rows).astype(BF16)
            return 0

        lax.fori_loop(0, half // 256, step_rows, 0)

    def bown():
        def step_rows(step, _):
            rows = pl.ds(pl.multiple_of(base + step * 256, 256), 256)
            low = pl.ds(pl.multiple_of(step * 256, 256), 256)
            middle[low, :] = branch(rows) + tok[low, :].astype(F32) + params[4:5, :]
            return 0

        lax.fori_loop(0, half // 256, step_rows, 0)

    def ntwo():
        def step_rows(step, _):
            low = pl.ds(pl.multiple_of(step * 256, 256), 256)
            values = middle[low, :] + got_rows[low, :].astype(F32)
            middle[low, :] = values
            normed = norm_rows(values, params[2:3, :], params[3:4, :])
            second[pl.ds(pl.multiple_of(base + step * 256, 256), 256), :] = normed.astype(BF16)
            return 0

        lax.fori_loop(0, half // 256, step_rows, 0)
        put(middle, middle_out, 25)

    def lift():
        k = count_step("lift")
        complete(1, k)
        if k == 0:
            for sem in range(12, 16):
                done(sem)
        if k >= 2:
            done(28 + k % 2)

        def step_rows(step, _):
            rows = pl.ds(pl.multiple_of(step * 256, 256), 256)
            pre = dot_nn(second[rows, :], w_up[:, columns(k)]) + bias[turn[k], 1:2, :]
            cdf = 0.5 * lax.erf(pre * (0.5**0.5)) + 0.5
            density = jnp.exp(-0.5 * pre * pre) * 0.3989422804014327
            joined[k, rows, :] = (pre * cdf).astype(BF16)
            slope[k % 2, rows, :] = (cdf + pre * density).astype(BF16)
            return 0

        lax.fori_loop(0, count // 256, step_rows, 0)
        put(joined.at[k], hidden_out.at[:, columns(k)], 12 + k)
        put(slope.at[k % 2], slope_out.at[:, columns(k)], 28 + k % 2)
        if k == TURNS - 1:
            put(w_up, w_up_out, 30)

    def down():
        k = count_step("down")
        complete(2, k)
        if k == 0:
            done(24)
            done(25)
            for sem in [83] + [sem for sem in sent if sem < 24]:
                sent.pop(sem).wait_send()
        slab = pltpu.make_async_copy(w_down.at[:, columns(k)], w_attn.at[:, columns(k)], local_sem.at[31])
        slab.start()
        slab.wait()

        def step_rows(step, _):
            low = pl.ds(pl.multiple_of(step * 256, 256), 256)
            own = pl.ds(pl.multiple_of(base + step * 256, 256), 256)
            away = pl.ds(pl.multiple_of(other + step * 256, 256), 256)
            mine = dot_nt(joined[k, own, :], w_attn[:, columns(k)])
            yours = dot_nt(joined[k, away, :], w_attn[:, columns(k)])
            if k == 0:
                mine = mine + params[5:6, :]
                layer_other[low, :] = yours
            elif k < TURNS - 1:
                layer_other[low, :] += yours
            else:
                send_rows[low, :] = (layer_other[low, :] + yours).astype(BF16)
            middle[low, :] += mine
            return 0

        lax.fori_loop(0, half // 256, step_rows, 0)
        if k == TURNS - 1:
            put(middle, layer_own_out, 26)
            put(send_rows, layer_other_out, 27)

    actions = {
        "pr": pair_start, "pp": plane_send, "zz": line_send, "fw": forward_on, "tok": tok_start,
        "tokw": tok_wait, "cot": cot_start, "cotx": cot_pair, "cotw": cot_wait, "norm": norm, "send": hand,
        "wait": take, "proj": proj, "att": att, "both": both, "bown": bown, "ntwo": ntwo, "lift": lift,
        "down": down,
    }
    for name, *numbers in FORWARD_STEPS:
        actions[name](*numbers)
    for sem in sorted(outs):
        outs[sem].wait()
    for copy in sent.values():
        copy.wait_send()


def forward_pass(lengths, shards, tokens, cotangent, bias, vectors):
    half, features = tokens.shape
    count = 2 * half
    any_space = pl.BlockSpec(memory_space=pl.ANY)
    vmem = pl.BlockSpec(memory_space=pltpu.VMEM)
    smem = pl.BlockSpec(memory_space=pltpu.SMEM)
    wide = (features, TURNS * SPAN)
    shapes = [
        (wide, BF16), (wide, BF16), (wide, BF16), ((half, features), BF16), ((count, features), BF16),
        ((8, count), F32), ((count, features), BF16), ((count, features), BF16),
        ((TURNS, count, SPAN), BF16), ((TURNS, count, 256), BF16), ((TURNS, 8, count), F32),
        ((half, features), F32), ((count, TURNS * SPAN), BF16), ((count, TURNS * SPAN), BF16),
        ((half, features), F32), ((half, features), BF16),
    ]
    return pl.pallas_call(
        functools.partial(forward_kernel, HDIM ** (-0.5)),
        in_specs=[smem] + [any_space] * 6 + [vmem] * 6,
        out_specs=[any_space] * len(shapes),
        out_shape=[jax.ShapeDtypeStruct(shape, kind) for shape, kind in shapes],
        scratch_shapes=[
            pltpu.VMEM(wide, BF16),
            pltpu.VMEM(wide, BF16),
            pltpu.VMEM((half, features), BF16),
            pltpu.VMEM((count, features), BF16),
            pltpu.VMEM((count, features), BF16),
            pltpu.VMEM((TURNS, count, SPAN), BF16),
            pltpu.VMEM((TURNS, count, 256), BF16),
            pltpu.VMEM((half, features), F32),
            pltpu.VMEM((half, features), BF16),
            pltpu.VMEM((half, features), BF16),
            pltpu.VMEM((half, features), F32),
            pltpu.VMEM((2, count, SPAN), BF16),
            pltpu.VMEM((8, count), F32),
            pltpu.VMEM((8, count), F32),
            pltpu.VMEM((TURNS, 8, count), F32),
            pltpu.VMEM((TURNS, 8, SPAN), F32),
            pltpu.VMEM((8, features), F32),
            pltpu.SemaphoreType.DMA((88,)),
            pltpu.SemaphoreType.DMA((88,)),
            pltpu.SemaphoreType.DMA((32,)),
        ],
        cost_estimate=pl.CostEstimate(
            flops=2 * count * features * 9000, bytes_accessed=90_000_000, transcendentals=30_000_000
        ),
        compiler_params=pltpu.CompilerParams(
            vmem_limit_bytes=60 << 20, collective_id=0, has_side_effects=True
        ),
        name="forward_pass",
    )(lengths, *shards, tokens, cotangent, bias, *vectors)


BACKWARD_STEPS = (
    ("load",), ("P", 0, 0), ("pre",), ("layer", 0), ("P", 0, 1), ("pre",), ("layer", 1), ("pre",),
    ("layer", 2), ("pre",), ("2", 0, 0), ("soth",), ("send", "a"), ("P", 0, 2), ("P", 0, 3), ("wait", "a"),
    ("ntwo",), ("send", "b"), ("3", 0, 0), ("2", 0, 1), ("2", 0, 2), ("P", 1, 0), ("wait", "b"), ("hb",),
    ("att",), ("3", 0, 1), ("2", 0, 3), ("att",), ("P", 1, 1), ("att",), ("3", 0, 3), ("3", 0, 2),
    ("aend",), ("P", 1, 2), ("hb",), ("2", 1, 0), ("att",), ("2", 1, 1), ("att",), ("P", 1, 3), ("2", 1, 2),
    ("F", 0), ("att",), ("aend",), ("3", 1, 1), ("3", 1, 0), ("P", 2, 0), ("2", 1, 3), ("P", 2, 1), ("hb",),
    ("3", 1, 2), ("att",), ("G", 0), ("att",), ("att",), ("3", 1, 3), ("aend",), ("P", 2, 2), ("2", 2, 1),
    ("hb",), ("att",), ("F", 1), ("att",), ("3", 2, 1), ("2", 2, 2), ("att",), ("aend",), ("3", 2, 2),
    ("foth",), ("send", "c"), ("P", 2, 3), ("tok",), ("2", 2, 0), ("wait", "c"), ("none",), ("reloc",),
    ("none",), ("2", 2, 3), ("reloc",), ("none",), ("hs", "c"), ("G", 1), ("3", 2, 0), ("hw", "c"),
    ("hs", "x"), ("hw", "x"), ("hs", "y"), ("3", 2, 3), ("hw", "y"), ("hs", "z1"), ("reloc",), ("F", 2),
    ("hw", "z1"), ("hs", "z2"), ("wreloc",), ("G", 2), ("hw", "z2"), ("layer", 3),
)


def backward_kernel(
    scaling,
    w_attn_in, w_up_in, w_down_in, tok_in, grad_in, first_in, second_in, joined_in, heads_in, middle_in,
    hidden_in, slope_in, totals_in, layer_own_in, layer_other_in, key_mask, gain_one, gain_two,
    tokens_out, down_out, up_out, attn_out, sums_out, pre_out, layer_out, layer_got, layer_low,
    weight, grad, left, wide, right, grad_heads, totals, middle, send_rows, got_rows, key_sum, value_sum,
    product, near_got, far_got, turn_got, line_got, line_own, final, final_got, sums, sums_got,
    send_sem, recv_sem, local_sem, credit,
):
    dp, z = lax.axis_index("dp"), lax.axis_index("tensor")
    core, plane = lax.rem(dp, 2), lax.div(dp, 2)
    x_bit, y_bit = lax.rem(plane, 2), lax.div(plane, 2)
    half = middle.shape[0]
    count = 2 * half
    features = middle.shape[1]
    to_x = (y_bit * 4 + (1 - x_bit) * 2 + core, z)
    to_y = ((1 - y_bit) * 4 + x_bit * 2 + core, z)
    to_core = (plane * 2 + 1 - core, z)
    to_clip = (plane * 2 + 1 - core, z + 1 - 2 * lax.rem(z, 2))
    to_z = [(dp, lax.rem(z + k, TURNS)) for k in range(TURNS)]
    to_z_pair = (dp, z + 1 - 2 * lax.rem(z, 2))
    moves = core != lax.rem(z, 2)
    plane_x = y_bit * 2 + 1 - x_bit
    plane_y = (1 - y_bit) * 2 + x_bit
    plane_xy = (1 - y_bit) * 2 + 1 - x_bit
    turn = [lax.rem(z + TURNS - k, TURNS) for k in range(TURNS)]
    base = pl.multiple_of(core * half, 256)
    other = pl.multiple_of((1 - core) * half, 256)
    own_rows, other_rows = pl.ds(base, half), pl.ds(other, half)

    barrier = pltpu.get_barrier_semaphore()
    partners = [to_x, to_y, to_core, to_clip] + to_z[1:]
    for partner in partners:
        pl.semaphore_signal(barrier, inc=1, device_id=partner, device_id_type=pl.DeviceIdType.MESH)
    pl.semaphore_wait(barrier, len(partners))

    def remote(source, target, sem, device):
        return pltpu.make_async_remote_copy(
            src_ref=source,
            dst_ref=target,
            send_sem=send_sem.at[sem],
            recv_sem=recv_sem.at[sem],
            device_id=device,
            device_id_type=pl.DeviceIdType.MESH,
        )

    def send(source, target, sem, device):
        copy = remote(source, target, sem, device)
        copy.start()
        return copy

    def arrived(target, sem):
        remote(target, target, sem, to_core).wait_recv()

    def tell(index, device):
        pl.semaphore_signal(
            credit.at[index], inc=1, device_id=device, device_id_type=pl.DeviceIdType.MESH
        )

    def local(source, target, sem):
        copy = pltpu.make_async_copy(source, target, local_sem.at[sem])
        copy.start()
        return copy

    def columns(k):
        return pl.ds(pl.multiple_of(turn[k] * SPAN, 128), SPAN)

    def load_right(source, k, slot):
        return local(source.at[:, columns(k)], right.at[slot], slot)

    grad_load = local(grad_in, grad, 2)
    right_loads = [load_right(hidden_in, 0, 0), None]
    weight_loads, slope_loads = [], []
    for k in range(TURNS):
        weight_loads.append(local(w_down_in.at[:, columns(k)], weight.at[:, columns(k)], 3 + k))
        slope_loads.append(local(slope_in.at[:, columns(k)], wide.at[:, columns(k)], 7 + k))
    right_loads[1] = load_right(hidden_in, 1, 1)
    left_load = local(second_in, left, 11)
    layer_sent = send(layer_other_in, layer_got, 98, to_core)
    layer_load = local(layer_own_in, middle, 12)
    totals_loads = [local(totals_in.at[turn[k]], totals.at[k], 21 + k) for k in range(TURNS)]
    sums[...] = jnp.zeros_like(sums)

    in_flight = [[] for _ in range(TURNS)]
    staged = [None] * TURNS
    rows_half = UNIT // 2

    def place(k, where, part=None):
        if part is None:
            return product.at[k, pl.ds(pl.multiple_of(where * UNIT, 16), UNIT)]
        start = pl.multiple_of(where * UNIT + part * rows_half, 16)
        return product.at[k, pl.ds(start, rows_half)]

    def slot(ref, k, part):
        return ref.at[k, part * rows_half : (part + 1) * rows_half]

    def sem_of(array, kind, k):
        return array * 28 + kind * 4 + k

    def ready(k):
        for copy in in_flight[k]:
            copy.wait_send()
        in_flight[k] = []

    def stage_one(array, k):
        for part, device, near in ((0, to_x, plane_x), (1, to_y, plane_y)):
            if array > 0:
                pl.semaphore_wait(credit.at[4 * part + k], 1)
            far = place(k, plane_xy, part)
            in_flight[k] += [
                send(far, slot(far_got, k, part), sem_of(array, part, k), device),
                send(place(k, near, part), slot(near_got, k, part), sem_of(array, 2 + part, k), device),
            ]

    def add_to(target, sources):
        total = target[...].astype(F32)
        for source in sources:
            total = total + source[...].astype(F32)
        return total

    def stage_two(array, k):
        for part, device, back, far in ((0, to_y, to_x, plane_y), (1, to_x, to_y, plane_x)):
            arrived(slot(far_got, k, part), sem_of(array, part, k))
            target = place(k, far, part)
            target[...] = add_to(target, [slot(far_got, k, part)]).astype(BF16)
            if array > 0:
                pl.semaphore_wait(credit.at[8 + 4 * part + k], 1)
            in_flight[k].append(send(target, slot(turn_got, k, part), sem_of(array, 4 + part, k), device))
        for part, back in ((0, to_x), (1, to_y)):
            arrived(slot(near_got, k, part), sem_of(array, 2 + part, k))
            target = place(k, plane, part)
            target[...] = add_to(target, [slot(near_got, k, part)]).astype(BF16)
            if array < 2:
                tell(4 * part + k, back)

    def stage_three(array, k):
        for part in range(2):
            arrived(slot(turn_got, k, part), sem_of(array, 4 + part, k))
        source = place(k, plane)
        total = add_to(source, [turn_got.at[k]]).astype(BF16)
        if array < 2:
            tell(8 + k, to_y)
            tell(12 + k, to_x)
        if k == 0:
            line_own[...] = total
            return
        if array < 2:
            if staged[k] is not None:
                staged[k].wait_send()
            row, col = (k - 1) % 2, (k - 1) // 2
            source = send_rows.at[
                row * UNIT : (row + 1) * UNIT, col * SPAN : (col + 1) * SPAN
            ]
        source[...] = total
        if array > 0:
            pl.semaphore_wait(credit.at[16 + k], 1)
        copy = send(source, line_got.at[k], sem_of(array, 6, k), to_z[(TURNS - k) % TURNS])
        if array < 2:
            staged[k] = copy
        else:
            in_flight[k].append(copy)

    results = [down_out, up_out, attn_out]
    final_moves = []
    last_moves = []

    def final_one(array):
        for wait in final_moves:
            wait()
        final_moves.clear()
        for k in range(1, TURNS):
            arrived(line_got.at[k], sem_of(array, 6, k))
        final[...] = add_to(line_own, [line_got.at[k] for k in range(1, TURNS)])
        if array < 2:
            for k in range(1, TURNS):
                tell(16 + k, to_z[k])
        keep = pl.ds(pl.multiple_of(core * rows_half, 16), rows_half)
        give = pl.ds(pl.multiple_of((1 - core) * rows_half, 16), rows_half)
        final_moves.append(send(final.at[give], final_got.at[array], 90 + array, to_core).wait_send)
        target = results[array].at[:, pl.ds(pl.multiple_of(core * SPAN, 128), SPAN)]
        final_moves.append(local(final.at[keep], target, 13).wait)

    def final_two(array):
        arrived(final_got.at[array], 90 + array)
        target = results[array].at[:, pl.ds(pl.multiple_of((1 - core) * SPAN, 128), SPAN)]
        last_moves.append(local(final_got.at[array], target, 14 + array).wait)

    pre_puts, pre_loads = [], [None, None]
    loads = {"left": left_load}
    exchange = {}
    start = jnp.zeros((1, 160), F32)
    att_total = [start]

    def load():
        grad_load.wait()

    def pre():
        k = len(pre_puts)
        weight_loads[k].wait()
        slope_loads[k].wait()

        def step_rows(step, total):
            rows = pl.ds(pl.multiple_of(step * 512, 512), 512)
            value = dot_nn(grad[rows, :], weight[:, columns(k)])
            value = value * wide[rows, columns(k)].astype(F32)
            wide[rows, columns(k)] = value.astype(BF16)
            return total + jnp.sum(value, 0, keepdims=True)

        total = lax.fori_loop(0, count // 512, step_rows, jnp.zeros((1, SPAN), F32))
        sums[8 + 2 * turn[k] + core, :, :SPAN] = total
        pre_puts.append(local(wide.at[:, columns(k)], pre_out.at[:, columns(k)], 17 + k))
        weight_loads[k] = local(w_up_in.at[:, columns(k)], weight.at[:, columns(k)], 3 + k)

    def second_part(rows):
        return dot_nt(wide[rows, :], weight[...])

    def soth():
        for copy in weight_loads:
            copy.wait()

        def step_rows(step, _):
            rows = pl.ds(pl.multiple_of(other + step * 256, 256), 256)
            low = pl.ds(pl.multiple_of(step * 256, 256), 256)
            send_rows[low, :] = second_part(rows).astype(BF16)
            return 0

        lax.fori_loop(0, half // 256, step_rows, 0)

    def norm_back_rows(values, gain, above):
        center = values - jnp.mean(values, -1, keepdims=True)
        scale = lax.rsqrt(jnp.mean(center * center, -1, keepdims=True) + EPS)
        normed = center * scale
        scaled = above * gain
        back = scaled - jnp.mean(scaled, -1, keepdims=True)
        back = (back - normed * jnp.mean(scaled * normed, -1, keepdims=True)) * scale
        return back, jnp.sum(above * normed, 0, keepdims=True), jnp.sum(above, 0, keepdims=True)

    zero = jnp.zeros((1, features), F32)

    def ntwo():
        loads["middle"].wait()

        def step_rows(step, total):
            low = pl.ds(pl.multiple_of(step * 256, 256), 256)
            rows = pl.ds(pl.multiple_of(base + step * 256, 256), 256)
            above = second_part(rows) + got_rows[low, :].astype(F32)
            back, by_gain, by_shift = norm_back_rows(middle[low, :], gain_two[...][None, :], above)
            out_grad = grad[rows, :].astype(F32)
            below = out_grad + back
            middle[low, :] = below
            grad[rows, :] = below.astype(BF16)
            by_down, by_out = jnp.sum(out_grad, 0, keepdims=True), jnp.sum(below, 0, keepdims=True)
            return (total[0] + by_down, total[1] + by_out, total[2] + by_gain, total[3] + by_shift)

        parts = lax.fori_loop(0, half // 256, step_rows, (zero,) * 4)
        for i in range(4):
            sums[i, :, :] = parts[i]
        exchange["a"].wait_send()
        for copy in pre_puts[2:]:
            copy.wait()
        loads["weight"] = local(w_attn_in, weight, 3)
        loads["joined"] = [
            local(joined_in.at[turn[k]], wide.at[:, k * SPAN : (k + 1) * SPAN], 7 + k)
            for k in range(TURNS)
        ]

    def hand(name):
        if name == "a":
            exchange[name] = send(send_rows, got_rows, 84, to_core)
        elif name == "b":
            pl.semaphore_wait(credit.at[20], 1)
            exchange[name] = send(grad.at[own_rows], grad.at[own_rows], 85, to_core)
        else:
            exchange[name] = send(send_rows, got_rows, 86, to_core)

    def take(name):
        if name == "a":
            arrived(got_rows, 84)
        elif name == "b":
            arrived(grad.at[other_rows], 85)
        else:
            arrived(got_rows, 86)
            loads["tok"].wait()

    def produce(array, k):
        ready(k)
        if array < 2:
            if array == 0:
                right_loads[k % 2].wait()
                factor = grad
            else:
                pre_loads[k % 2].wait()
                if k == 0:
                    loads["left"].wait()
                factor = left

            def step_part(part, _):
                rows = pl.ds(pl.multiple_of(part * 640, 640), 640)
                product[k, rows, :] = dot_tn(factor[:, rows], right[k % 2]).astype(BF16)
                return 0

            lax.fori_loop(0, 2, step_part, 0)
            if array == 0 and k < 2:
                right_loads[k] = load_right(hidden_in, k + 2, k)
            elif array == 0:
                pre_puts[k - 2].wait()
                pre_loads[k - 2] = load_right(pre_out, k - 2, k - 2)
                if k == 3:
                    tell(20, to_core)
            elif k < 2:
                pre_loads[k] = load_right(pre_out, k + 2, k)
            if array == 1 and k == 3:
                loads["left"] = local(first_in, left, 11)
                loads["first"] = loads["left"]
        else:
            heads_load = local(heads_in.at[turn[k]], grad_heads, 4)
            if "first" in loads:
                loads.pop("first").wait()
            heads_load.wait()

            def step_part(part, _):
                rows = pl.ds(pl.multiple_of(part * 640, 640), 640)
                by_first = dot_tn(left[:, rows], wide[:, k * SPAN : k * SPAN + 480])
                by_branch = dot_tn(grad[:, rows], grad_heads[:, 96:256])
                product[k, rows, :] = jnp.concatenate([by_first, by_branch], -1).astype(BF16)
                return 0

            lax.fori_loop(0, 2, step_part, 0)
        stage_one(array, k)

    steps_done = {"hb": 0, "att": 0, "aend": 0, "none": 0, "reloc": 0}

    def count_step(name):
        steps_done[name] += 1
        return steps_done[name] - 1

    def hb():
        k = count_step("hb")
        if k == 0:
            loads["weight"].wait()
        slab = pl.ds(pl.multiple_of(turn[k] * SPAN + 384, 128), 256)

        def step_rows(step, _):
            rows = pl.ds(pl.multiple_of(step * 512, 512), 512)
            grad_heads[rows, :] = dot_nn(grad[rows, :], weight[:, slab]).astype(BF16)
            return 0

        lax.fori_loop(0, count // 512, step_rows, 0)
        loads["joined"][k].wait()
        totals_loads[k].wait()
        key_sum[...] = jnp.zeros_like(key_sum)
        value_sum[...] = jnp.zeros_like(value_sum)
        att_total[0] = start

    one_lane = (lax.broadcasted_iota(jnp.int32, (256, 48), 1) == 0).astype(F32).astype(BF16)

    def att():
        step_at = count_step("att")
        k, part = step_at // 3, step_at % 3
        low = k * SPAN

        def step_rows(step, total):
            rows = pl.ds(pl.multiple_of(step * 256, 256), 256)
            queries = wide[rows, low : low + 160]
            grads = grad_heads[rows, :]
            outs = []
            for head in range(2):
                at = head * HDIM
                query = queries[:, at : at + HDIM]
                above = grads[:, 96 + at : 96 + at + HDIM]
                key = wide[:, low + 160 + at : low + 160 + at + HDIM]
                value = wide[:, low + 320 + at : low + 320 + at + HDIM]
                scores = dot_nt(
                    jnp.concatenate([key, key_mask[:, :48]], -1),
                    jnp.concatenate([query, one_lane], -1),
                )
                probs = jnp.exp2(scores * (scaling * LOG2E) - totals[k, head : head + 1, rows])
                grad_probs = dot_nt(value, above)
                shared = jnp.sum(probs * grad_probs, 0, keepdims=True)
                grad_scores = (probs * (grad_probs - shared)).astype(BF16)
                value_sum[head, :, :HDIM] += dot_nn(probs.astype(BF16), above)
                key_sum[head, :, :HDIM] += dot_nn(grad_scores, query)
                outs.append(dot_tn(grad_scores, key) * scaling)
            joined = jnp.concatenate(outs, -1)
            wide[rows, low : low + 160] = joined.astype(BF16)
            return total + jnp.sum(joined, 0, keepdims=True)

        att_total[0] = lax.fori_loop(2 * part, 2 * part + 2, step_rows, att_total[0])

    def aend():
        k = count_step("aend")
        low = k * SPAN

        def step_rows(step, value_total):
            rows = pl.ds(pl.multiple_of(step * 256, 256), 256)
            keys = [key_sum[head, rows, :HDIM] * scaling for head in range(2)]
            values = [value_sum[head, rows, :HDIM] for head in range(2)]
            joined = jnp.concatenate(keys + values, -1)
            wide[rows, low + 160 : low + 480] = joined.astype(BF16)
            return value_total + jnp.sum(joined[:, 160:], 0, keepdims=True)

        value_total = lax.fori_loop(0, count // 256, step_rows, start)
        sums[16 + 2 * turn[k] + core, :, :160] = att_total[0]
        sums[16 + 2 * turn[k] + core, :, 160:320] = value_total

    def first_part(rows):
        total = None
        for k in range(TURNS):
            slab = pl.ds(pl.multiple_of(turn[k] * SPAN, 128), 480)
            part = dot_nt(wide[rows, k * SPAN : k * SPAN + 480], weight[:, slab])
            total = part if total is None else total + part
        return total

    def foth():
        for copy in staged[1:]:
            copy.wait_send()

        def step_rows(step, _):
            rows = pl.ds(pl.multiple_of(other + step * 256, 256), 256)
            low = pl.ds(pl.multiple_of(step * 256, 256), 256)
            send_rows[low, :] = first_part(rows).astype(BF16)
            return 0

        lax.fori_loop(0, half // 256, step_rows, 0)

    def none():
        step = count_step("none")
        low = slice(step * 256, step * 256 + 256)
        rows = pl.ds(pl.multiple_of(base + step * 256, 256), 256)
        above = first_part(rows) + got_rows[low, :].astype(F32)
        values = got_tok[low, :].astype(F32)
        back, by_gain, by_shift = norm_back_rows(values, gain_one[...][None, :], above)
        grad[half + step * 256 : half + step * 256 + 256, :] = (middle[low, :] + back).astype(BF16)
        if step == 0:
            sums[4, :, :] = by_gain
            sums[5, :, :] = by_shift
        else:
            sums[4, :, :] += by_gain
            sums[5, :, :] += by_shift

    got_tok = grad.at[0:half]

    def tokens_move(step):
        rows = pl.ds(step * 256, 256)
        source = grad.at[half + step * 256 : half + step * 256 + 256]
        away = remote(source, tokens_out.at[rows], 87 + step, to_clip)
        here = pltpu.make_async_copy(source, tokens_out.at[rows], local_sem.at[25 + step])
        return away, here

    def reloc():
        away, here = tokens_move(count_step("reloc"))

        @pl.when(moves)
        def _():
            away.start()

        @pl.when(jnp.logical_not(moves))
        def _():
            here.start()

    def wreloc():
        for step in range(half // 256):
            away, here = tokens_move(step)

            @pl.when(moves)
            def _(away=away):
                away.wait()

            @pl.when(jnp.logical_not(moves))
            def _(here=here):
                here.wait()

    hops = {"c": (0, to_core), "x": (1, to_x), "y": (2, to_y), "z1": (3, to_z_pair), "z2": (4, to_z[2])}
    hop_copies = {}

    def hs(name):
        index, device = hops[name]
        hop_copies[name] = send(sums, sums_got.at[index], 93 + index, device)

    def hw(name):
        index, _ = hops[name]
        hop_copies[name].wait_send()
        arrived(sums_got.at[index], 93 + index)
        sums[...] = sums[...] + sums_got[index]

    layer_away = remote(layer_low, layer_out, 99, to_clip)
    layer_here = pltpu.make_async_copy(layer_low, layer_out, local_sem.at[30])

    def layer(stage):
        if stage == 0:
            arrived(layer_got, 98)
            loads["layer"] = local(layer_got, send_rows, 28)
        elif stage == 1:
            layer_load.wait()
            loads["layer"].wait()

            def step_rows(step, _):
                rows = pl.ds(pl.multiple_of(step * 256, 256), 256)
                send_rows[rows, :] = (middle[rows, :] + send_rows[rows, :].astype(F32)).astype(BF16)
                return 0

            lax.fori_loop(0, half // 256, step_rows, 0)
            loads["layer"] = local(send_rows, layer_low, 29)
            loads["middle"] = local(middle_in, middle, 12)
        elif stage == 2:
            loads["layer"].wait()

            @pl.when(moves)
            def _():
                layer_away.start()

            @pl.when(jnp.logical_not(moves))
            def _():
                layer_here.start()
        else:
            layer_sent.wait_send()

            @pl.when(moves)
            def _():
                layer_away.wait()

            @pl.when(jnp.logical_not(moves))
            def _():
                layer_here.wait()

    def token_load():
        exchange["b"].wait_send()
        loads["tok"] = local(tok_in, grad.at[0:half], 2)

    actions = {
        "load": load, "pre": pre, "soth": soth, "ntwo": ntwo, "hb": hb, "att": att, "aend": aend,
        "foth": foth, "none": none, "reloc": reloc, "wreloc": wreloc, "send": hand, "wait": take,
        "P": produce, "2": stage_two, "3": stage_three, "F": final_one, "G": final_two, "hs": hs, "hw": hw,
        "tok": token_load, "layer": layer,
    }
    for name, *numbers in BACKWARD_STEPS:
        actions[name](*numbers)
    sums_put = local(sums, sums_out, 5)
    exchange["c"].wait_send()
    for wait in final_moves + last_moves:
        wait()
    for k in range(TURNS):
        ready(k)
    sums_put.wait()


def backward_pass(
    w_attn, w_up, w_down, tok, grad, first, second, joined, heads, middle, hidden, slope, totals, layer_own,
    layer_other, key_mask, gain_one, gain_two,
):
    half, features = tok.shape
    count = 2 * half
    any_space = pl.BlockSpec(memory_space=pl.ANY)
    vmem = pl.BlockSpec(memory_space=pltpu.VMEM)
    cols = TURNS * SPAN
    shapes = [
        ((half, features), BF16), ((UNIT // 2, 2 * SPAN), F32), ((UNIT // 2, 2 * SPAN), F32),
        ((UNIT // 2, 2 * SPAN), F32), ((24, 1, features), F32), ((count, cols), BF16),
        ((half, features), BF16), ((half, features), BF16), ((half, features), BF16),
    ]
    return pl.pallas_call(
        functools.partial(backward_kernel, HDIM ** (-0.5)),
        in_specs=[any_space] * 15 + [vmem] * 3,
        out_specs=[any_space] * len(shapes),
        out_shape=[jax.ShapeDtypeStruct(shape, kind) for shape, kind in shapes],
        scratch_shapes=[
            pltpu.VMEM((features, cols), BF16),
            pltpu.VMEM((count, features), BF16),
            pltpu.VMEM((count, features), BF16),
            pltpu.VMEM((count, cols), BF16),
            pltpu.VMEM((2, count, SPAN), BF16),
            pltpu.VMEM((count, 256), BF16),
            pltpu.VMEM((TURNS, 8, count), F32),
            pltpu.VMEM((half, features), F32),
            pltpu.VMEM((half, features), BF16),
            pltpu.VMEM((half, features), BF16),
            pltpu.VMEM((2, count, 128), F32),
            pltpu.VMEM((2, count, 128), F32),
            pltpu.VMEM((TURNS, features, SPAN), BF16),
            pltpu.VMEM((TURNS, UNIT, SPAN), BF16),
            pltpu.VMEM((TURNS, UNIT, SPAN), BF16),
            pltpu.VMEM((TURNS, UNIT, SPAN), BF16),
            pltpu.VMEM((TURNS, UNIT, SPAN), BF16),
            pltpu.VMEM((UNIT, SPAN), BF16),
            pltpu.VMEM((UNIT, SPAN), F32),
            pltpu.VMEM((3, UNIT // 2, SPAN), F32),
            pltpu.VMEM((24, 1, features), F32),
            pltpu.VMEM((5, 24, 1, features), F32),
            pltpu.SemaphoreType.DMA((100,)),
            pltpu.SemaphoreType.DMA((100,)),
            pltpu.SemaphoreType.DMA((32,)),
            pltpu.SemaphoreType.REGULAR((24,)),
        ],
        cost_estimate=pl.CostEstimate(
            flops=4 * count * features * 6400, bytes_accessed=90_000_000, transcendentals=30_000_000
        ),
        compiler_params=pltpu.CompilerParams(
            vmem_limit_bytes=60 << 20, collective_id=1, has_side_effects=True
        ),
        name="backward_pass",
    )(
        w_attn, w_up, w_down, tok, grad, first, second, joined, heads, middle, hidden, slope, totals,
        layer_own, layer_other, key_mask, gain_one, gain_two,
    )


class Links:
    def __init__(self):
        self.dp = lax.axis_size("dp")
        self.tensor = lax.axis_size("tensor")
        self.tensor_pos = lax.axis_index("tensor")
        self.half = self.tensor_pos % 2

    def pair(self, value):
        return lax.ppermute(value, "tensor", [(i, i ^ 1) for i in range(self.tensor)])

    def columns(self, shard):
        rows, _, width = shard.shape
        whole = lax.all_gather(shard, ("dp", "tensor"), axis=0)
        whole = lax.dynamic_index_in_dim(whole, self.half, 2, keepdims=False)
        whole = whole.reshape(self.dp, self.tensor, rows, width)
        return [whole[:, k].reshape(self.dp * rows, width) for k in range(self.tensor)]

    def vectors(self, value):
        whole = lax.all_gather(value, "tensor", axis=0)
        return [whole[k] for k in range(self.tensor)]

    def place(self, pieces):
        halves = (jnp.arange(2) == self.half)[None, :, None]
        return jnp.where(halves, jnp.stack(pieces)[:, None, :], 0.0)

    def gradient(self, left, rights):
        whole = jnp.stack([dot_tn(left, right).astype(BF16) for right in rights], 0)
        features, width = whole.shape[1:]
        whole = whole.reshape(self.tensor, self.dp, features // self.dp, width)
        whole = jnp.moveaxis(whole, 1, 0)[:, :, :, None, :]
        halves = (jnp.arange(2) == self.half)[None, None, None, :, None]
        whole = jnp.where(halves, whole, jnp.zeros((), BF16))
        whole = whole.reshape((self.dp * self.tensor,) + whole.shape[2:])
        return lax.psum_scatter(whole, ("dp", "tensor"), tiled=False).astype(F32)

    def merged(self, partial_of):
        got = self.pair(partial_of(1).astype(BF16))
        return partial_of(0) + got.astype(F32)


def summed(vectors, total):
    whole = total(jnp.concatenate(vectors))
    at = 0
    result = []
    for vector in vectors:
        result.append(whole[at : at + vector.shape[0]])
        at += vector.shape[0]
    return result


def halves_of(weight):
    return weight.reshape(weight.shape[0], 2, weight.shape[1] // 2)


def flat(piece):
    return piece.reshape(piece.shape[0], -1)


def local_any(
    tokens,
    lengths,
    cotangent,
    norm1_gain,
    norm1_shift,
    query_weight,
    query_bias,
    key_weight,
    value_weight,
    value_bias,
    out_weight,
    out_bias,
    norm2_gain,
    norm2_shift,
    up_weight,
    up_bias,
    down_weight,
    down_bias,
):
    links = Links()
    rows = tokens.shape[0]
    scaling = HDIM ** (-0.5)
    width = query_weight.shape[1] // 2
    heads = width // HDIM
    units = up_weight.shape[1] // 2
    count = links.tensor

    shard_attn = [query_weight, key_weight, value_weight, out_weight.T]
    w_attn = links.columns(jnp.concatenate([halves_of(w) for w in shard_attn], -1))
    w_up = jnp.concatenate(links.columns(halves_of(up_weight)), 1)
    w_down = jnp.concatenate(links.columns(halves_of(down_weight.T)), 1)
    w_qkv = [block[:, : 3 * width] for block in w_attn]
    w_out = [block[:, 3 * width :] for block in w_attn]
    small = [query_bias.reshape(2, width), value_bias.reshape(2, width), up_bias.reshape(2, units)]
    small = jnp.concatenate(small, -1)
    small = links.vectors(jnp.where(links.half == 0, small[0], small[1]))
    bias_qkv = [
        jnp.concatenate([v[:width], jnp.zeros((width,), F32), v[width : 2 * width]]) for v in small
    ]
    bias_up = jnp.concatenate([v[2 * width :] for v in small])

    place = links.tensor_pos // 2
    clip_length = jnp.sum(jnp.where(jnp.arange(lengths.shape[0]) == place, lengths, 0))
    frames = jnp.arange(rows)
    frames = jnp.concatenate([links.half * rows + frames, (1 - links.half) * rows + frames])
    visible = frames < clip_length
    mask = jnp.where(visible, 0.0, -1e30).astype(F32)

    def part_of(value, part):
        return value[part * rows : (part + 1) * rows]

    def both(value):
        return jnp.concatenate([value, links.pair(value)])

    source = tokens.astype(F32)
    first = both(norm_rows(source, norm1_gain, norm1_shift).astype(BF16))
    joined, heads_out, totals = [], [], []
    for k in range(count):
        joined.append((dot_nn(first, w_qkv[k]) + bias_qkv[k]).astype(BF16))
        mixed, total = attend(joined[k], mask[None, :], heads, scaling)
        heads_out.append(mixed)
        totals.append(total)
    heads_all = jnp.concatenate(heads_out, 1)
    w_out_all = jnp.concatenate(w_out, 1)
    branch = links.merged(lambda part: dot_nt(part_of(heads_all, part), w_out_all))
    middle = source + branch + out_bias
    second = both(norm_rows(middle, norm2_gain, norm2_shift).astype(BF16))
    hidden, slope = up_gelu(second, w_up, bias_up[None, :])
    out_own = cotangent * visible[:rows].astype(BF16)[:, None]
    out_grad = both(out_own)

    def cut(value):
        return [value[:, k * units : (k + 1) * units] for k in range(count)]

    grad_down = links.gradient(out_grad, cut(hidden))
    down_out = links.merged(lambda part: dot_nt(part_of(hidden, part), w_down))
    layer_out = (middle + down_out + down_bias).astype(BF16)
    grad_pre = (dot_nn(out_grad, w_down) * slope.astype(F32)).astype(BF16)
    grad_up = links.gradient(second, cut(grad_pre))
    grad_second = links.merged(lambda part: dot_nt(part_of(grad_pre, part), w_up))
    back_two, grad_gain_two, grad_shift_two = norm_back(middle, norm2_gain, grad_second)
    grad_middle = out_own.astype(F32) + back_two
    branch_grad = both(grad_middle.astype(BF16))
    grad_heads = [dot_nn(branch_grad, w_out[k]).astype(BF16) for k in range(count)]
    grad_out_w = links.gradient(branch_grad, heads_out)
    grad_joined, sums = [], []
    for k in range(count):
        back, sum_k = attend_back(joined[k], grad_heads[k], totals[k], mask[:, None], heads, scaling)
        grad_joined.append(back)
        sums.append(sum_k)
    grad_qkv = links.gradient(first, grad_joined)
    grad_all = jnp.concatenate(grad_joined, 1)
    w_qkv_all = jnp.concatenate(w_qkv, 1)
    grad_first = links.merged(lambda part: dot_nt(part_of(grad_all, part), w_qkv_all))
    back_one, grad_gain_one, grad_shift_one = norm_back(source, norm1_gain, grad_first)
    grad_tokens = (grad_middle + back_one).astype(BF16)

    vectors = [
        links.place([v[0] for v in cut(jnp.sum(grad_pre.astype(F32), 0)[None, :])]).reshape(-1),
        links.place([s[0, :width] for s in sums]).reshape(-1),
        links.place([s[1, :width] for s in sums]).reshape(-1),
        grad_gain_one,
        grad_shift_one,
        jnp.sum(grad_middle, 0),
        grad_gain_two,
        grad_shift_two,
        jnp.sum(out_own.astype(F32), 0),
    ]
    sum_up, sum_query, sum_value, *rest = summed(
        vectors, lambda value: lax.psum(value, ("dp", "tensor"))
    )
    sum_gain_one, sum_shift_one, sum_out, sum_gain_two, sum_shift_two, sum_down = rest

    def own(vector):
        size = vector.shape[0] // count
        return lax.dynamic_slice_in_dim(vector, links.tensor_pos * size, size, 0)

    return (
        layer_out,
        grad_tokens,
        sum_gain_one,
        sum_shift_one,
        flat(grad_qkv[:, :, :width]),
        own(sum_query),
        flat(grad_qkv[:, :, width : 2 * width]),
        flat(grad_qkv[:, :, 2 * width :]),
        own(sum_value),
        flat(grad_out_w).T,
        sum_out,
        sum_gain_two,
        sum_shift_two,
        flat(grad_up),
        own(sum_up),
        flat(grad_down).T,
        sum_down,
    )


def local_chips(
    tokens,
    lengths,
    cotangent,
    norm1_gain,
    norm1_shift,
    query_weight,
    query_bias,
    key_weight,
    value_weight,
    value_bias,
    out_weight,
    out_bias,
    norm2_gain,
    norm2_shift,
    up_weight,
    up_bias,
    down_weight,
    down_bias,
):
    core, z = lax.axis_index("dp") % 2, lax.axis_index("tensor")
    width, units = 160, SPAN
    parts = (query_weight, key_weight, value_weight, out_weight.T)
    shards = (
        jnp.concatenate([w[:, i * width : (i + 1) * width] for i in range(2) for w in parts], 1),
        up_weight,
        down_weight.T,
    )

    def half_of(vector):
        size = vector.shape[0] // 2
        return jnp.where(core == 0, vector[:size], vector[size:])

    gap = jnp.zeros((width,), F32)
    small = [half_of(query_bias), gap, half_of(value_bias), gap, half_of(up_bias)]
    small = jnp.concatenate(small + [jnp.zeros((6 * SPAN,), F32)]).reshape(8, SPAN)
    vectors = (norm1_gain, norm1_shift, norm2_gain, norm2_shift, out_bias, down_bias)
    (
        w_attn, w_up, w_down, tok, out_grad, mask, first, second, joined, heads, totals, middle, hidden,
        slope, layer_own, layer_other,
    ) = forward_pass(lengths, shards, tokens, cotangent, small, vectors)
    lane = jnp.arange(128)[None, :] == 0
    key_mask = jnp.where(lane, mask[0][:, None], 0.0).astype(BF16)
    grad_tokens, grad_down, grad_up, grad_attn, sums, _, layer_out, _, _ = backward_pass(
        w_attn, w_up, w_down, tok, out_grad, first, second, joined, heads, middle, hidden, slope, totals,
        layer_own, layer_other, key_mask, norm1_gain, norm2_gain,
    )

    def piece(index):
        start = index * width
        both = [grad_attn[:, i * SPAN + start : i * SPAN + start + width] for i in range(2)]
        return jnp.concatenate(both, 1)

    def own(first_row, start, size):
        rows = lax.dynamic_slice_in_dim(sums[:, 0], first_row + 2 * z, 2, 0)
        return rows[:, start : start + size].reshape(-1)

    return (
        layer_out,
        grad_tokens,
        sums[4, 0],
        sums[5, 0],
        piece(0),
        own(16, 0, width),
        piece(1),
        piece(2),
        own(16, width, width),
        piece(3).T,
        sums[1, 0],
        sums[2, 0],
        sums[3, 0],
        grad_up,
        own(8, 0, units),
        grad_down.T,
        sums[0, 0],
    )


def solution(mesh):
    rows = P(("dp", "tensor"), None)
    wide, tall = P("dp", "tensor"), P("tensor", "dp")
    piece, same = P("tensor"), P()
    chips = mesh.shape["dp"] == 8 and mesh.shape["tensor"] == 4
    return jax.shard_map(
        local_chips if chips else local_any,
        mesh=mesh,
        in_specs=(
            rows, P("dp"), rows, same, same, wide, piece, wide, wide, piece, tall, same, same, same,
            wide, piece, tall, same,
        ),
        out_specs=(
            rows, rows, same, same, wide, piece, wide, wide, piece, tall, same, same, same, wide, piece,
            tall, same,
        ),
        check_vma=False,
    )
```

```python
import functools

import jax
import jax.numpy as jnp
from jax import lax
from jax.experimental import pallas as pl
from jax.experimental.pallas import tpu as pltpu
from jax.sharding import PartitionSpec as P

HDIM = 80
EPS = 1e-05
LOG2E = 1.4426950408889634
F32 = jnp.float32
BF16 = jnp.bfloat16


def norm_rows(values, norm_gain, norm_shift):
    center = values - jnp.mean(values, -1, keepdims=True)
    spread = jnp.mean(center * center, -1, keepdims=True)
    return center * lax.rsqrt(spread + EPS) * norm_gain + norm_shift


def norm_back(values, norm_gain, grad):
    center = values - jnp.mean(values, -1, keepdims=True)
    scale = lax.rsqrt(jnp.mean(center * center, -1, keepdims=True) + EPS)
    normed = center * scale
    scaled = grad * norm_gain
    back = scaled - jnp.mean(scaled, -1, keepdims=True)
    back = (back - normed * jnp.mean(scaled * normed, -1, keepdims=True)) * scale
    return back, jnp.sum(grad * normed, 0), jnp.sum(grad, 0)


def dot_nn(left, right):
    return jnp.dot(left, right, preferred_element_type=F32)


def dot_tn(left, right):
    return lax.dot_general(left, right, (((0,), (0,)), ((), ())), preferred_element_type=F32)


def dot_nt(left, right):
    return lax.dot_general(left, right, (((1,), (1,)), ((), ())), preferred_element_type=F32)


def up_kernel(rows_ref, weight_ref, bias_ref, hidden_ref, slope_ref):
    pre = dot_nn(rows_ref[...], weight_ref[...]) + bias_ref[...]
    cdf = 0.5 * lax.erf(pre * (0.5**0.5)) + 0.5
    density = jnp.exp(-0.5 * pre * pre) * 0.3989422804014327
    hidden_ref[...] = (pre * cdf).astype(BF16)
    slope_ref[...] = (cdf + pre * density).astype(BF16)


def up_gelu(rows, weight, bias):
    count, depth = rows.shape
    cols = weight.shape[1]
    block_rows, block_cols = min(512, count), min(640, cols)
    return pl.pallas_call(
        up_kernel,
        grid=(cols // block_cols, count // block_rows),
        in_specs=[
            pl.BlockSpec((block_rows, depth), lambda n, m: (m, 0)),
            pl.BlockSpec((depth, block_cols), lambda n, m: (0, n)),
            pl.BlockSpec((1, block_cols), lambda n, m: (0, n)),
        ],
        out_specs=[
            pl.BlockSpec((block_rows, block_cols), lambda n, m: (m, n)),
            pl.BlockSpec((block_rows, block_cols), lambda n, m: (m, n)),
        ],
        out_shape=[jax.ShapeDtypeStruct((count, cols), BF16)] * 2,
        cost_estimate=pl.CostEstimate(
            flops=2 * count * depth * cols, bytes_accessed=20_000_000, transcendentals=0
        ),
        compiler_params=pltpu.CompilerParams(vmem_limit_bytes=40 << 20),
        name="up_gelu",
    )(rows, weight, bias)


def attend_kernel(heads, scaling, query_ref, all_ref, mask_ref, out_ref, total_ref):
    width = heads * HDIM
    queries = query_ref[...]
    mask = mask_ref[...]
    outs, totals = [], []
    for head in range(heads):
        low = head * HDIM
        query = queries[:, low : low + HDIM]
        key = all_ref[:, width + low : width + low + HDIM]
        value = all_ref[:, 2 * width + low : 2 * width + low + HDIM]
        scores = dot_nt(query, key) * (scaling * LOG2E) + mask
        row_max = jnp.max(scores, -1, keepdims=True)
        exp_scores = jnp.exp2(scores - row_max)
        total = jnp.sum(exp_scores, -1, keepdims=True)
        mixed = dot_nn(exp_scores.astype(BF16), value)
        outs.append(mixed * (1.0 / total))
        totals.append(row_max + jnp.log2(total))
    out_ref[...] = jnp.concatenate(outs, -1).astype(BF16)
    for head in range(heads):
        wide = jnp.broadcast_to(totals[head], (totals[head].shape[0], 128))
        total_ref[head : head + 1, :] = wide.T[0:1, :]


def attend(joined, mask_row, heads, scaling):
    count, cols = joined.shape
    block_rows = min(256, count)
    width = heads * HDIM
    return pl.pallas_call(
        functools.partial(attend_kernel, heads, scaling),
        grid=(count // block_rows,),
        in_specs=[
            pl.BlockSpec((block_rows, cols), lambda m: (m, 0)),
            pl.BlockSpec((count, cols), lambda m: (0, 0)),
            pl.BlockSpec((1, count), lambda m: (0, 0)),
        ],
        out_specs=[
            pl.BlockSpec((block_rows, width), lambda m: (m, 0)),
            pl.BlockSpec((heads, block_rows), lambda m: (0, m)),
        ],
        out_shape=[
            jax.ShapeDtypeStruct((count, width), BF16),
            jax.ShapeDtypeStruct((heads, count), F32),
        ],
        cost_estimate=pl.CostEstimate(
            flops=2 * heads * count * count * 512,
            bytes_accessed=4_000_000,
            transcendentals=heads * count * count,
        ),
        compiler_params=pltpu.CompilerParams(vmem_limit_bytes=48 << 20),
        name="attend",
    )(joined, joined, mask_row)


def attend_back_kernel(
    heads, scaling, query_ref, all_ref, grad_ref, total_ref, mask_ref,
    out_ref, sums_ref, key_sum, value_sum,
):
    step = pl.program_id(0)
    steps = pl.num_programs(0)
    width = heads * HDIM
    block_rows = query_ref.shape[0]

    @pl.when(step == 0)
    def _():
        key_sum[...] = jnp.zeros_like(key_sum)
        value_sum[...] = jnp.zeros_like(value_sum)
        sums_ref[...] = jnp.zeros_like(sums_ref)

    queries = query_ref[...]
    grads = grad_ref[...]
    query_outs = []
    for head in range(heads):
        low = head * HDIM
        query = queries[:, low : low + HDIM]
        grad = grads[:, low : low + HDIM]
        key = all_ref[:, width + low : width + low + HDIM]
        value = all_ref[:, 2 * width + low : 2 * width + low + HDIM]
        scores = dot_nt(key, query) * (scaling * LOG2E) + mask_ref[...]
        probs = jnp.exp2(scores - total_ref[head : head + 1, :])
        grad_probs = dot_nt(value, grad)
        shared = jnp.sum(probs * grad_probs, 0, keepdims=True)
        grad_scores = (probs * (grad_probs - shared)).astype(BF16)
        value_sum[head, :, :HDIM] += dot_nn(probs.astype(BF16), grad)
        key_sum[head, :, :HDIM] += dot_nn(grad_scores, query)
        query_outs.append(dot_tn(grad_scores, key) * scaling)
    joined = jnp.concatenate(query_outs, -1)
    sums_ref[0:1, :width] += jnp.sum(joined, 0, keepdims=True)
    rows = pl.ds(pl.multiple_of(step * block_rows, block_rows), block_rows)
    out_ref[rows, :width] = joined.astype(BF16)

    @pl.when(step == steps - 1)
    def _():
        keys = jnp.concatenate([key_sum[head, :, :HDIM] for head in range(heads)], -1)
        values = jnp.concatenate([value_sum[head, :, :HDIM] for head in range(heads)], -1)
        sums_ref[1:2, :width] = jnp.sum(values, 0, keepdims=True)
        out_ref[:, width:] = jnp.concatenate([keys * scaling, values], -1).astype(BF16)


def attend_back(joined, grad_heads, totals, mask_col, heads, scaling):
    count, cols = joined.shape
    block_rows = min(256, count)
    width = heads * HDIM
    return pl.pallas_call(
        functools.partial(attend_back_kernel, heads, scaling),
        grid=(count // block_rows,),
        in_specs=[
            pl.BlockSpec((block_rows, cols), lambda m: (m, 0)),
            pl.BlockSpec((count, cols), lambda m: (0, 0)),
            pl.BlockSpec((block_rows, width), lambda m: (m, 0)),
            pl.BlockSpec((heads, block_rows), lambda m: (0, m)),
            pl.BlockSpec((count, 1), lambda m: (0, 0)),
        ],
        out_specs=[
            pl.BlockSpec((count, cols), lambda m: (0, 0)),
            pl.BlockSpec((8, 256), lambda m: (0, 0)),
        ],
        out_shape=[
            jax.ShapeDtypeStruct((count, cols), BF16),
            jax.ShapeDtypeStruct((8, 256), F32),
        ],
        scratch_shapes=[
            pltpu.VMEM((heads, count, 128), F32),
            pltpu.VMEM((heads, count, 128), F32),
        ],
        cost_estimate=pl.CostEstimate(
            flops=2 * heads * count * count * 1280,
            bytes_accessed=5_000_000,
            transcendentals=heads * count * count,
        ),
        compiler_params=pltpu.CompilerParams(vmem_limit_bytes=56 << 20),
        name="attend_back",
    )(joined, joined, grad_heads, totals, mask_col)


UNIT = 320
SPAN = 640
TURNS = 4


def clamp_rows(ref, start, size):
    return ref.at[pl.ds(pl.multiple_of(start, 16), size)]


FORWARD_STEPS = (
    ("pr", 0), ("tok",), ("pr", 1), ("zz", 0), ("pp", 0, 0), ("pp", 1, 0), ("pr", 2), ("fw", 0, 0),
    ("fw", 1, 0), ("tokw",), ("pp", 2, 0), ("norm",), ("send", "a"), ("wait", "a"), ("pp", 0, 1), ("proj",),
    ("fw", 2, 0), ("att",), ("att",), ("fw", 0, 1), ("zz", 1), ("pp", 0, 2), ("pp", 0, 3), ("proj",),
    ("att",), ("att",), ("zz", 2), ("fw", 0, 2), ("fw", 0, 3), ("pp", 1, 1), ("cot",), ("pp", 1, 2),
    ("proj",), ("att",), ("att",), ("pp", 1, 3), ("proj",), ("att",), ("pp", 2, 1), ("att",), ("fw", 1, 3),
    ("fw", 1, 2), ("both",), ("send", "b"), ("bown",), ("wait", "b"), ("fw", 1, 1), ("ntwo",),
    ("send", "c"), ("fw", 2, 1), ("pp", 2, 2), ("wait", "c"), ("pp", 2, 3), ("lift",), ("lift",), ("lift",),
    ("lift",), ("down",), ("fw", 2, 2), ("fw", 2, 3), ("cotx",), ("down",), ("down",), ("cotw",), ("down",),
)


def forward_kernel(
    scaling,
    lengths, up_shard, down_shard, tokens, cotangent, query_weight, key_weight, value_weight, out_weight,
    query_bias, value_bias, up_bias, gain_one, shift_one, gain_two, shift_two, bias_out, bias_down,
    w_attn_out, w_up_out, w_down, tokens_out, grad_out, mask_out, first_out, second_out, joined_out,
    heads_out, totals_out, middle_out, hidden_out, slope_out, layer_own_out, layer_other_out,
    w_attn, w_up, tok, first, second, joined, heads, middle, send_rows, got_rows, layer_other, slope,
    mask_own, mask, totals, bias, params, attn_shard, bias_in, send_sem, recv_sem, local_sem,
):
    dp, z = lax.axis_index("dp"), lax.axis_index("tensor")
    core, plane = lax.rem(dp, 2), lax.div(dp, 2)
    x_bit, y_bit = lax.rem(plane, 2), lax.div(plane, 2)
    half = tok.shape[0]
    count = 2 * half
    to_x = (y_bit * 4 + (1 - x_bit) * 2 + core, z)
    to_y = ((1 - y_bit) * 4 + x_bit * 2 + core, z)
    to_core = (plane * 2 + 1 - core, z)
    to_clip = (plane * 2 + 1 - core, z + 1 - 2 * lax.rem(z, 2))
    to_z = [(dp, lax.rem(z + k, TURNS)) for k in range(TURNS)]
    moves = core != lax.rem(z, 2)
    plane_x = y_bit * 2 + 1 - x_bit
    plane_y = (1 - y_bit) * 2 + x_bit
    plane_xy = (1 - y_bit) * 2 + 1 - x_bit
    turn = [lax.rem(z + TURNS - k, TURNS) for k in range(TURNS)]
    base = pl.multiple_of(core * half, 256)
    other = pl.multiple_of((1 - core) * half, 256)
    own_rows, other_rows = pl.ds(base, half), pl.ds(other, half)

    barrier = pltpu.get_barrier_semaphore()
    partners = [to_x, to_y, to_core, to_clip] + to_z[1:]
    for partner in partners:
        pl.semaphore_signal(barrier, inc=1, device_id=partner, device_id_type=pl.DeviceIdType.MESH)
    width = UNIT // 2
    parts = [query_weight[...], key_weight[...], value_weight[...], out_weight[...]]
    pieces = [part[:, i * width : (i + 1) * width] for i in range(2) for part in parts]
    attn_shard[...] = jnp.concatenate(pieces, -1)

    def half_of(vector):
        row = vector[...][None, :]
        size = row.shape[1] // 2
        return jnp.where(core == 0, row[:, :size], row[:, size:])

    gap = jnp.zeros((1, width), F32)
    bias_in[...] = jnp.zeros_like(bias_in)
    bias_in[0:1, :] = jnp.concatenate([half_of(query_bias), gap, half_of(value_bias), gap], -1)
    bias_in[1:2, :] = half_of(up_bias)

    pl.semaphore_wait(barrier, len(partners))

    def remote(source, target, sem, device):
        return pltpu.make_async_remote_copy(
            src_ref=source,
            dst_ref=target,
            send_sem=send_sem.at[sem],
            recv_sem=recv_sem.at[sem],
            device_id=device,
            device_id_type=pl.DeviceIdType.MESH,
        )

    sent = {}

    def send(source, target, sem, device):
        copy = remote(source, target, sem, device)
        copy.start()
        sent[sem] = copy
        return copy

    def arrived(target, sem):
        remote(target, target, sem, to_core).wait_recv()

    outs = {}

    def put(source, target, sem):
        copy = pltpu.make_async_copy(source, target, local_sem.at[sem])
        copy.start()
        outs[sem] = copy

    def done(sem):
        outs.pop(sem).wait()

    weights = [w_attn, w_up, w_down]
    shards = [attn_shard, up_shard, down_shard]
    rows_half = UNIT // 2

    def columns(k):
        return pl.ds(pl.multiple_of(turn[k] * SPAN, 128), SPAN)

    def block(array, k, where, part=None):
        if part is None:
            rows = pl.ds(pl.multiple_of(where * UNIT, 16), UNIT)
        else:
            rows = pl.ds(pl.multiple_of(where * UNIT + part * rows_half, 16), rows_half)
        return weights[array].at[rows, columns(k)]

    def own_piece(array, which):
        rows = pl.ds(pl.multiple_of(plane * UNIT + which * rows_half, 16), rows_half)
        return weights[array].at[rows, columns(0)]

    def shard_half(array, which):
        return shards[array].at[:, pl.ds(pl.multiple_of(which * SPAN, 128), SPAN)]

    pairs = [None] * 3

    def pair_start(array):
        send(shard_half(array, 1 - core), own_piece(array, core), 72 + array, to_core)
        copy = pltpu.make_async_copy(
            shard_half(array, core), own_piece(array, core), local_sem.at[array]
        )
        copy.start()
        pairs[array] = copy

    def pair_wait(array):
        if pairs[array] is not None:
            pairs[array].wait()
            arrived(own_piece(array, 1 - core), 72 + array)
            pairs[array] = None

    def sem_of(array, kind, k):
        return array * 24 + kind * 4 + k

    def plane_send(array, k):
        if k == 0:
            pair_wait(array)
        else:
            arrived(block(array, k, plane), sem_of(array, 0, k))
        source = block(array, k, plane)
        send(source, source, sem_of(array, 1, k), to_x)
        send(source, source, sem_of(array, 2, k), to_y)

    def line_send(array):
        pair_wait(array)
        source = block(array, 0, plane)
        for k in range(1, TURNS):
            send(source, source, sem_of(array, 0, k), to_z[k])

    def forward_on(array, k):
        arrived(block(array, k, plane_x), sem_of(array, 1, k))
        source = block(array, k, plane_x, 0)
        send(source, source, sem_of(array, 3, k), to_y)
        arrived(block(array, k, plane_y), sem_of(array, 2, k))
        source = block(array, k, plane_y, 1)
        send(source, source, sem_of(array, 4, k), to_x)

    def complete(array, k):
        for part in range(2):
            arrived(block(array, k, plane_xy, part), sem_of(array, 3 + part, k))

    there = grad_out.at[other_rows]
    here = grad_out.at[own_rows]
    length = lengths[lax.div(z, 2)]
    frames = lax.broadcasted_iota(jnp.int32, mask_own.shape, 1)
    mask_own[...] = jnp.where(frames < length, 0.0, -1e30).astype(F32)
    tok_copy = pltpu.make_async_copy(tokens, tok, local_sem.at[3])
    mask_copy = pltpu.make_async_copy(mask_own, mask, local_sem.at[4])
    clip_tok = remote(tokens, tok, 75, to_clip)
    clip_mask = remote(mask_own, mask, 76, to_clip)
    cot_copy = pltpu.make_async_copy(send_rows, here, local_sem.at[5])
    clip_cot = remote(send_rows, there, 77, to_clip)
    bias_copy = pltpu.make_async_copy(bias_in, bias.at[z], local_sem.at[6])
    exchange = {}
    for i, vector in enumerate((gain_one, shift_one, gain_two, shift_two, bias_out, bias_down)):
        params[i : i + 1, :] = vector[...][None, :]

    def tok_start():
        @pl.when(moves)
        def _():
            clip_mask.start()
            clip_tok.start()

        @pl.when(jnp.logical_not(moves))
        def _():
            tok_copy.start()
            mask_copy.start()

        bias_copy.start()
        for k in range(1, TURNS):
            send(bias_in, bias.at[z], 77 + k, to_z[k])
        put(cotangent, send_rows, 7)

    def tok_wait():
        @pl.when(moves)
        def _():
            clip_mask.wait()
            clip_tok.wait()

        @pl.when(jnp.logical_not(moves))
        def _():
            tok_copy.wait()
            mask_copy.wait()

        put(tok, tokens_out, 8)
        put(mask, mask_out, 9)

    def cot_start():
        done(7)

        def step_rows(step, _):
            rows = pl.ds(pl.multiple_of(step * 256, 256), 256)
            at = lax.broadcasted_iota(jnp.int32, (256, send_rows.shape[1]), 0)
            at = at + (lax.rem(z, 2) * half + step * 256)
            values = jnp.where(at < length, send_rows[rows, :].astype(F32), 0.0)
            send_rows[rows, :] = values.astype(BF16)
            return 0

        lax.fori_loop(0, half // 256, step_rows, 0)

        @pl.when(moves)
        def _():
            clip_cot.start()

        @pl.when(jnp.logical_not(moves))
        def _():
            cot_copy.start()

    def cot_pair():
        @pl.when(moves)
        def _():
            arrived(here, 77)

        send(here, here, 81, to_core)

    def cot_wait():
        arrived(there, 81)

    def norm():
        def step_rows(step, _):
            rows = pl.ds(pl.multiple_of(step * 256, 256), 256)
            values = tok[rows, :].astype(F32)
            normed = norm_rows(values, params[0:1, :], params[1:2, :])
            first[pl.ds(pl.multiple_of(base + step * 256, 256), 256), :] = normed.astype(BF16)
            return 0

        lax.fori_loop(0, half // 256, step_rows, 0)

    def hand(name):
        if name == "a":
            exchange[name] = send(first.at[own_rows], first.at[own_rows], 82, to_core)
        elif name == "b":
            exchange[name] = send(send_rows, got_rows, 83, to_core)
        else:
            exchange[name] = send(second.at[own_rows], second.at[own_rows], 84, to_core)

    def take(name):
        if name == "a":
            arrived(first.at[other_rows], 82)
            put(first, first_out, 10)
            bias_copy.wait()
            for k in range(1, TURNS):
                arrived(bias.at[turn[k]], 77 + k)
        elif name == "b":
            arrived(got_rows, 83)
        else:
            arrived(second.at[other_rows], 84)
            put(second, second_out, 11)

    steps_done = {"proj": 0, "att": 0, "lift": 0, "down": 0}

    def count_step(name):
        steps_done[name] += 1
        return steps_done[name] - 1

    def proj():
        k = count_step("proj")
        complete(0, k)
        slab = pl.ds(pl.multiple_of(turn[k] * SPAN, 128), 480)

        def step_rows(step, _):
            rows = pl.ds(pl.multiple_of(step * half, half), half)
            product = dot_nn(first[rows, :], w_attn[:, slab]) + bias[turn[k], 0:1, :480]
            joined[k, rows, :480] = product.astype(BF16)
            return 0

        lax.fori_loop(0, 2, step_rows, 0)
        put(joined.at[k], joined_out.at[turn[k]], 12 + k)
        if k == TURNS - 1:
            put(w_attn, w_attn_out, 24)

    def att():
        step_at = count_step("att")
        k, part = step_at // 2, step_at % 2

        def step_rows(step, _):
            rows = pl.ds(pl.multiple_of(step * 256, 256), 256)
            queries = joined[k, rows, :160]
            mixes, logs = [jnp.zeros((256, 96), F32)], []
            for head in range(2):
                low = head * HDIM
                query = queries[:, low : low + HDIM]
                key = joined[k, :, 160 + low : 160 + low + HDIM]
                value = joined[k, :, 320 + low : 320 + low + HDIM]
                scores = dot_nt(query, key) * (scaling * LOG2E) + mask[0:1, :]
                row_max = jnp.max(scores, -1, keepdims=True)
                exp_scores = jnp.exp2(scores - row_max)
                total = jnp.sum(exp_scores, -1, keepdims=True)
                mixes.append(dot_nn(exp_scores.astype(BF16), value) * (1.0 / total))
                logs.append(row_max + jnp.log2(total))
            heads[k, rows, :] = jnp.concatenate(mixes, -1).astype(BF16)
            for head in range(2):
                wide = jnp.broadcast_to(logs[head], (256, 128))
                totals[k, head : head + 1, rows] = wide.T[0:1, :]
            return 0

        lax.fori_loop(3 * part, 3 * part + 3, step_rows, 0)
        if part == 1:
            put(heads.at[k], heads_out.at[turn[k]], 16 + k)
            put(totals.at[k], totals_out.at[turn[k]], 20 + k)

    def branch(rows):
        total = None
        for k in range(TURNS):
            slab = pl.ds(pl.multiple_of(turn[k] * SPAN + 384, 128), 256)
            product = dot_nt(heads[k, rows, :], w_attn[:, slab])
            total = product if total is None else total + product
        return total

    def both():
        @pl.when(moves)
        def _():
            clip_cot.wait_send()

        @pl.when(jnp.logical_not(moves))
        def _():
            cot_copy.wait()

        def step_rows(step, _):
            rows = pl.ds(pl.multiple_of(other + step * 256, 256), 256)
            low = pl.ds(pl.multiple_of(step * 256, 256), 256)
            send_rows[low, :] = branch(rows).astype(BF16)
            return 0

        lax.fori_loop(0, half // 256, step_rows, 0)

    def bown():
        def step_rows(step, _):
            rows = pl.ds(pl.multiple_of(base + step * 256, 256), 256)
            low = pl.ds(pl.multiple_of(step * 256, 256), 256)
            middle[low, :] = branch(rows) + tok[low, :].astype(F32) + params[4:5, :]
            return 0

        lax.fori_loop(0, half // 256, step_rows, 0)

    def ntwo():
        def step_rows(step, _):
            low = pl.ds(pl.multiple_of(step * 256, 256), 256)
            values = middle[low, :] + got_rows[low, :].astype(F32)
            middle[low, :] = values
            normed = norm_rows(values, params[2:3, :], params[3:4, :])
            second[pl.ds(pl.multiple_of(base + step * 256, 256), 256), :] = normed.astype(BF16)
            return 0

        lax.fori_loop(0, half // 256, step_rows, 0)
        put(middle, middle_out, 25)

    def lift():
        k = count_step("lift")
        complete(1, k)
        if k == 0:
            for sem in range(12, 16):
                done(sem)
        if k >= 2:
            done(28 + k % 2)

        def step_rows(step, _):
            rows = pl.ds(pl.multiple_of(step * 256, 256), 256)
            pre = dot_nn(second[rows, :], w_up[:, columns(k)]) + bias[turn[k], 1:2, :]
            cdf = 0.5 * lax.erf(pre * (0.5**0.5)) + 0.5
            density = jnp.exp(-0.5 * pre * pre) * 0.3989422804014327
            joined[k, rows, :] = (pre * cdf).astype(BF16)
            slope[k % 2, rows, :] = (cdf + pre * density).astype(BF16)
            return 0

        lax.fori_loop(0, count // 256, step_rows, 0)
        put(joined.at[k], hidden_out.at[:, columns(k)], 12 + k)
        put(slope.at[k % 2], slope_out.at[:, columns(k)], 28 + k % 2)
        if k == TURNS - 1:
            put(w_up, w_up_out, 30)

    def down():
        k = count_step("down")
        complete(2, k)
        if k == 0:
            done(24)
            done(25)
            for sem in [83] + [sem for sem in sent if sem < 24]:
                sent.pop(sem).wait_send()
        slab = pltpu.make_async_copy(w_down.at[:, columns(k)], w_attn.at[:, columns(k)], local_sem.at[31])
        slab.start()
        slab.wait()

        def step_rows(step, _):
            low = pl.ds(pl.multiple_of(step * 256, 256), 256)
            own = pl.ds(pl.multiple_of(base + step * 256, 256), 256)
            away = pl.ds(pl.multiple_of(other + step * 256, 256), 256)
            mine = dot_nt(joined[k, own, :], w_attn[:, columns(k)])
            yours = dot_nt(joined[k, away, :], w_attn[:, columns(k)])
            if k == 0:
                mine = mine + params[5:6, :]
                layer_other[low, :] = yours
            elif k < TURNS - 1:
                layer_other[low, :] += yours
            else:
                send_rows[low, :] = (layer_other[low, :] + yours).astype(BF16)
            middle[low, :] += mine
            return 0

        lax.fori_loop(0, half // 256, step_rows, 0)
        if k == TURNS - 1:
            put(middle, layer_own_out, 26)
            put(send_rows, layer_other_out, 27)

    actions = {
        "pr": pair_start, "pp": plane_send, "zz": line_send, "fw": forward_on, "tok": tok_start,
        "tokw": tok_wait, "cot": cot_start, "cotx": cot_pair, "cotw": cot_wait, "norm": norm, "send": hand,
        "wait": take, "proj": proj, "att": att, "both": both, "bown": bown, "ntwo": ntwo, "lift": lift,
        "down": down,
    }
    for name, *numbers in FORWARD_STEPS:
        actions[name](*numbers)
    for sem in sorted(outs):
        outs[sem].wait()
    for copy in sent.values():
        copy.wait_send()


def forward_pass(lengths, shards, tokens, cotangent, weights, vectors):
    half, features = tokens.shape
    count = 2 * half
    any_space = pl.BlockSpec(memory_space=pl.ANY)
    vmem = pl.BlockSpec(memory_space=pltpu.VMEM)
    smem = pl.BlockSpec(memory_space=pltpu.SMEM)
    wide = (features, TURNS * SPAN)
    shapes = [
        (wide, BF16), (wide, BF16), (wide, BF16), ((half, features), BF16), ((count, features), BF16),
        ((8, count), F32), ((count, features), BF16), ((count, features), BF16),
        ((TURNS, count, SPAN), BF16), ((TURNS, count, 256), BF16), ((TURNS, 8, count), F32),
        ((half, features), F32), ((count, TURNS * SPAN), BF16), ((count, TURNS * SPAN), BF16),
        ((half, features), F32), ((half, features), BF16),
    ]
    return pl.pallas_call(
        functools.partial(forward_kernel, HDIM ** (-0.5)),
        in_specs=[smem] + [any_space] * 4 + [vmem] * 13,
        out_specs=[any_space] * len(shapes),
        out_shape=[jax.ShapeDtypeStruct(shape, kind) for shape, kind in shapes],
        scratch_shapes=[
            pltpu.VMEM(wide, BF16),
            pltpu.VMEM(wide, BF16),
            pltpu.VMEM((half, features), BF16),
            pltpu.VMEM((count, features), BF16),
            pltpu.VMEM((count, features), BF16),
            pltpu.VMEM((TURNS, count, SPAN), BF16),
            pltpu.VMEM((TURNS, count, 256), BF16),
            pltpu.VMEM((half, features), F32),
            pltpu.VMEM((half, features), BF16),
            pltpu.VMEM((half, features), BF16),
            pltpu.VMEM((half, features), F32),
            pltpu.VMEM((2, count, SPAN), BF16),
            pltpu.VMEM((8, count), F32),
            pltpu.VMEM((8, count), F32),
            pltpu.VMEM((TURNS, 8, count), F32),
            pltpu.VMEM((TURNS, 8, SPAN), F32),
            pltpu.VMEM((8, features), F32),
            pltpu.VMEM((UNIT // 2, 2 * SPAN), BF16),
            pltpu.VMEM((8, SPAN), F32),
            pltpu.SemaphoreType.DMA((88,)),
            pltpu.SemaphoreType.DMA((88,)),
            pltpu.SemaphoreType.DMA((32,)),
        ],
        cost_estimate=pl.CostEstimate(
            flops=2 * count * features * 9000, bytes_accessed=90_000_000, transcendentals=30_000_000
        ),
        compiler_params=pltpu.CompilerParams(
            vmem_limit_bytes=60 << 20, collective_id=0, has_side_effects=True
        ),
        name="forward_pass",
    )(lengths, *shards, tokens, cotangent, *weights, *vectors)


BACKWARD_STEPS = (
    ("load",), ("P", 0, 0), ("pre",), ("layer", 0), ("P", 0, 1), ("pre",), ("layer", 1), ("pre",),
    ("layer", 2), ("pre",), ("2", 0, 0), ("soth",), ("send", "a"), ("P", 0, 2), ("P", 0, 3), ("wait", "a"),
    ("ntwo",), ("send", "b"), ("3", 0, 0), ("2", 0, 1), ("2", 0, 2), ("P", 1, 0), ("wait", "b"), ("hb",),
    ("att",), ("3", 0, 1), ("2", 0, 3), ("att",), ("P", 1, 1), ("att",), ("3", 0, 3), ("3", 0, 2),
    ("aend",), ("P", 1, 2), ("hb",), ("2", 1, 0), ("att",), ("2", 1, 1), ("att",), ("P", 1, 3), ("2", 1, 2),
    ("F", 0), ("att",), ("aend",), ("3", 1, 1), ("3", 1, 0), ("P", 2, 0), ("2", 1, 3), ("P", 2, 1), ("hb",),
    ("3", 1, 2), ("att",), ("G", 0), ("att",), ("att",), ("3", 1, 3), ("aend",), ("P", 2, 2), ("2", 2, 1),
    ("hb",), ("att",), ("F", 1), ("att",), ("3", 2, 1), ("2", 2, 2), ("att",), ("aend",), ("3", 2, 2),
    ("foth",), ("send", "c"), ("P", 2, 3), ("tok",), ("2", 2, 0), ("wait", "c"), ("none",), ("reloc",),
    ("none",), ("2", 2, 3), ("reloc",), ("none",), ("hs", "c"), ("G", 1), ("3", 2, 0), ("hw", "c"),
    ("hs", "x"), ("hw", "x"), ("hs", "y"), ("3", 2, 3), ("hw", "y"), ("hs", "z1"), ("reloc",), ("F", 2),
    ("hw", "z1"), ("hs", "z2"), ("wreloc",), ("G", 2), ("hw", "z2"), ("layer", 3),
)


def backward_kernel(
    scaling,
    w_attn_in, w_up_in, w_down_in, tok_in, grad_in, first_in, second_in, joined_in, heads_in, middle_in,
    hidden_in, slope_in, totals_in, layer_own_in, layer_other_in, key_mask, gain_one, gain_two,
    tokens_out, down_out, up_out, attn_out, sums_out, pre_out, layer_out, layer_got, layer_low,
    weight, grad, left, wide, right, grad_heads, totals, middle, send_rows, got_rows, key_sum, value_sum,
    product, near_got, far_got, turn_got, line_got, line_own, final, final_got, sums, sums_got,
    send_sem, recv_sem, local_sem, credit,
):
    dp, z = lax.axis_index("dp"), lax.axis_index("tensor")
    core, plane = lax.rem(dp, 2), lax.div(dp, 2)
    x_bit, y_bit = lax.rem(plane, 2), lax.div(plane, 2)
    half = middle.shape[0]
    count = 2 * half
    features = middle.shape[1]
    to_x = (y_bit * 4 + (1 - x_bit) * 2 + core, z)
    to_y = ((1 - y_bit) * 4 + x_bit * 2 + core, z)
    to_core = (plane * 2 + 1 - core, z)
    to_clip = (plane * 2 + 1 - core, z + 1 - 2 * lax.rem(z, 2))
    to_z = [(dp, lax.rem(z + k, TURNS)) for k in range(TURNS)]
    to_z_pair = (dp, z + 1 - 2 * lax.rem(z, 2))
    moves = core != lax.rem(z, 2)
    plane_x = y_bit * 2 + 1 - x_bit
    plane_y = (1 - y_bit) * 2 + x_bit
    plane_xy = (1 - y_bit) * 2 + 1 - x_bit
    turn = [lax.rem(z + TURNS - k, TURNS) for k in range(TURNS)]
    base = pl.multiple_of(core * half, 256)
    other = pl.multiple_of((1 - core) * half, 256)
    own_rows, other_rows = pl.ds(base, half), pl.ds(other, half)

    barrier = pltpu.get_barrier_semaphore()
    partners = [to_x, to_y, to_core, to_clip] + to_z[1:]
    for partner in partners:
        pl.semaphore_signal(barrier, inc=1, device_id=partner, device_id_type=pl.DeviceIdType.MESH)
    pl.semaphore_wait(barrier, len(partners))

    def remote(source, target, sem, device):
        return pltpu.make_async_remote_copy(
            src_ref=source,
            dst_ref=target,
            send_sem=send_sem.at[sem],
            recv_sem=recv_sem.at[sem],
            device_id=device,
            device_id_type=pl.DeviceIdType.MESH,
        )

    def send(source, target, sem, device):
        copy = remote(source, target, sem, device)
        copy.start()
        return copy

    def arrived(target, sem):
        remote(target, target, sem, to_core).wait_recv()

    def tell(index, device):
        pl.semaphore_signal(
            credit.at[index], inc=1, device_id=device, device_id_type=pl.DeviceIdType.MESH
        )

    def local(source, target, sem):
        copy = pltpu.make_async_copy(source, target, local_sem.at[sem])
        copy.start()
        return copy

    def columns(k):
        return pl.ds(pl.multiple_of(turn[k] * SPAN, 128), SPAN)

    def load_right(source, k, slot):
        return local(source.at[:, columns(k)], right.at[slot], slot)

    grad_load = local(grad_in, grad, 2)
    right_loads = [load_right(hidden_in, 0, 0), None]
    weight_loads, slope_loads = [], []
    for k in range(TURNS):
        weight_loads.append(local(w_down_in.at[:, columns(k)], weight.at[:, columns(k)], 3 + k))
        slope_loads.append(local(slope_in.at[:, columns(k)], wide.at[:, columns(k)], 7 + k))
    right_loads[1] = load_right(hidden_in, 1, 1)
    left_load = local(second_in, left, 11)
    layer_sent = send(layer_other_in, layer_got, 98, to_core)
    layer_load = local(layer_own_in, middle, 12)
    totals_loads = [local(totals_in.at[turn[k]], totals.at[k], 21 + k) for k in range(TURNS)]
    sums[...] = jnp.zeros_like(sums)

    in_flight = [[] for _ in range(TURNS)]
    staged = [None] * TURNS
    rows_half = UNIT // 2

    def place(k, where, part=None):
        if part is None:
            return product.at[k, pl.ds(pl.multiple_of(where * UNIT, 16), UNIT)]
        start = pl.multiple_of(where * UNIT + part * rows_half, 16)
        return product.at[k, pl.ds(start, rows_half)]

    def slot(ref, k, part):
        return ref.at[k, part * rows_half : (part + 1) * rows_half]

    def sem_of(array, kind, k):
        return array * 28 + kind * 4 + k

    def ready(k):
        for copy in in_flight[k]:
            copy.wait_send()
        in_flight[k] = []

    def stage_one(array, k):
        for part, device, near in ((0, to_x, plane_x), (1, to_y, plane_y)):
            if array > 0:
                pl.semaphore_wait(credit.at[4 * part + k], 1)
            far = place(k, plane_xy, part)
            in_flight[k] += [
                send(far, slot(far_got, k, part), sem_of(array, part, k), device),
                send(place(k, near, part), slot(near_got, k, part), sem_of(array, 2 + part, k), device),
            ]

    def add_to(target, sources):
        total = target[...].astype(F32)
        for source in sources:
            total = total + source[...].astype(F32)
        return total

    def stage_two(array, k):
        for part, device, back, far in ((0, to_y, to_x, plane_y), (1, to_x, to_y, plane_x)):
            arrived(slot(far_got, k, part), sem_of(array, part, k))
            target = place(k, far, part)
            target[...] = add_to(target, [slot(far_got, k, part)]).astype(BF16)
            if array > 0:
                pl.semaphore_wait(credit.at[8 + 4 * part + k], 1)
            in_flight[k].append(send(target, slot(turn_got, k, part), sem_of(array, 4 + part, k), device))
        for part, back in ((0, to_x), (1, to_y)):
            arrived(slot(near_got, k, part), sem_of(array, 2 + part, k))
            target = place(k, plane, part)
            target[...] = add_to(target, [slot(near_got, k, part)]).astype(BF16)
            if array < 2:
                tell(4 * part + k, back)

    def stage_three(array, k):
        for part in range(2):
            arrived(slot(turn_got, k, part), sem_of(array, 4 + part, k))
        source = place(k, plane)
        total = add_to(source, [turn_got.at[k]]).astype(BF16)
        if array < 2:
            tell(8 + k, to_y)
            tell(12 + k, to_x)
        if k == 0:
            line_own[...] = total
            return
        if array < 2:
            if staged[k] is not None:
                staged[k].wait_send()
            row, col = (k - 1) % 2, (k - 1) // 2
            source = send_rows.at[
                row * UNIT : (row + 1) * UNIT, col * SPAN : (col + 1) * SPAN
            ]
        source[...] = total
        if array > 0:
            pl.semaphore_wait(credit.at[16 + k], 1)
        copy = send(source, line_got.at[k], sem_of(array, 6, k), to_z[(TURNS - k) % TURNS])
        if array < 2:
            staged[k] = copy
        else:
            in_flight[k].append(copy)

    results = [down_out, up_out, attn_out]
    final_moves = []
    last_moves = []

    def final_one(array):
        for wait in final_moves:
            wait()
        final_moves.clear()
        for k in range(1, TURNS):
            arrived(line_got.at[k], sem_of(array, 6, k))
        final[...] = add_to(line_own, [line_got.at[k] for k in range(1, TURNS)])
        if array < 2:
            for k in range(1, TURNS):
                tell(16 + k, to_z[k])
        keep = pl.ds(pl.multiple_of(core * rows_half, 16), rows_half)
        give = pl.ds(pl.multiple_of((1 - core) * rows_half, 16), rows_half)
        final_moves.append(send(final.at[give], final_got.at[array], 90 + array, to_core).wait_send)
        target = results[array].at[:, pl.ds(pl.multiple_of(core * SPAN, 128), SPAN)]
        final_moves.append(local(final.at[keep], target, 13).wait)

    def final_two(array):
        arrived(final_got.at[array], 90 + array)
        target = results[array].at[:, pl.ds(pl.multiple_of((1 - core) * SPAN, 128), SPAN)]
        last_moves.append(local(final_got.at[array], target, 14 + array).wait)

    pre_puts, pre_loads = [], [None, None]
    loads = {"left": left_load}
    exchange = {}
    start = jnp.zeros((1, 160), F32)
    att_total = [start]

    def load():
        grad_load.wait()

    def pre():
        k = len(pre_puts)
        weight_loads[k].wait()
        slope_loads[k].wait()

        def step_rows(step, total):
            rows = pl.ds(pl.multiple_of(step * 512, 512), 512)
            value = dot_nn(grad[rows, :], weight[:, columns(k)])
            value = value * wide[rows, columns(k)].astype(F32)
            wide[rows, columns(k)] = value.astype(BF16)
            return total + jnp.sum(value, 0, keepdims=True)

        total = lax.fori_loop(0, count // 512, step_rows, jnp.zeros((1, SPAN), F32))
        sums[8 + 2 * turn[k] + core, :, :SPAN] = total
        pre_puts.append(local(wide.at[:, columns(k)], pre_out.at[:, columns(k)], 17 + k))
        weight_loads[k] = local(w_up_in.at[:, columns(k)], weight.at[:, columns(k)], 3 + k)

    def second_part(rows):
        return dot_nt(wide[rows, :], weight[...])

    def soth():
        for copy in weight_loads:
            copy.wait()

        def step_rows(step, _):
            rows = pl.ds(pl.multiple_of(other + step * 256, 256), 256)
            low = pl.ds(pl.multiple_of(step * 256, 256), 256)
            send_rows[low, :] = second_part(rows).astype(BF16)
            return 0

        lax.fori_loop(0, half // 256, step_rows, 0)

    def norm_back_rows(values, gain, above):
        center = values - jnp.mean(values, -1, keepdims=True)
        scale = lax.rsqrt(jnp.mean(center * center, -1, keepdims=True) + EPS)
        normed = center * scale
        scaled = above * gain
        back = scaled - jnp.mean(scaled, -1, keepdims=True)
        back = (back - normed * jnp.mean(scaled * normed, -1, keepdims=True)) * scale
        return back, jnp.sum(above * normed, 0, keepdims=True), jnp.sum(above, 0, keepdims=True)

    zero = jnp.zeros((1, features), F32)

    def ntwo():
        loads["middle"].wait()

        def step_rows(step, total):
            low = pl.ds(pl.multiple_of(step * 256, 256), 256)
            rows = pl.ds(pl.multiple_of(base + step * 256, 256), 256)
            above = second_part(rows) + got_rows[low, :].astype(F32)
            back, by_gain, by_shift = norm_back_rows(middle[low, :], gain_two[...][None, :], above)
            out_grad = grad[rows, :].astype(F32)
            below = out_grad + back
            middle[low, :] = below
            grad[rows, :] = below.astype(BF16)
            by_down, by_out = jnp.sum(out_grad, 0, keepdims=True), jnp.sum(below, 0, keepdims=True)
            return (total[0] + by_down, total[1] + by_out, total[2] + by_gain, total[3] + by_shift)

        parts = lax.fori_loop(0, half // 256, step_rows, (zero,) * 4)
        for i in range(4):
            sums[i, :, :] = parts[i]
        exchange["a"].wait_send()
        for copy in pre_puts[2:]:
            copy.wait()
        loads["weight"] = local(w_attn_in, weight, 3)
        loads["joined"] = [
            local(joined_in.at[turn[k]], wide.at[:, k * SPAN : (k + 1) * SPAN], 7 + k)
            for k in range(TURNS)
        ]

    def hand(name):
        if name == "a":
            exchange[name] = send(send_rows, got_rows, 84, to_core)
        elif name == "b":
            pl.semaphore_wait(credit.at[20], 1)
            exchange[name] = send(grad.at[own_rows], grad.at[own_rows], 85, to_core)
        else:
            exchange[name] = send(send_rows, got_rows, 86, to_core)

    def take(name):
        if name == "a":
            arrived(got_rows, 84)
        elif name == "b":
            arrived(grad.at[other_rows], 85)
        else:
            arrived(got_rows, 86)
            loads["tok"].wait()

    def produce(array, k):
        ready(k)
        if array < 2:
            if array == 0:
                right_loads[k % 2].wait()
                factor = grad
            else:
                pre_loads[k % 2].wait()
                if k == 0:
                    loads["left"].wait()
                factor = left

            def step_part(part, _):
                rows = pl.ds(pl.multiple_of(part * 640, 640), 640)
                product[k, rows, :] = dot_tn(factor[:, rows], right[k % 2]).astype(BF16)
                return 0

            lax.fori_loop(0, 2, step_part, 0)
            if array == 0 and k < 2:
                right_loads[k] = load_right(hidden_in, k + 2, k)
            elif array == 0:
                pre_puts[k - 2].wait()
                pre_loads[k - 2] = load_right(pre_out, k - 2, k - 2)
                if k == 3:
                    tell(20, to_core)
            elif k < 2:
                pre_loads[k] = load_right(pre_out, k + 2, k)
            if array == 1 and k == 3:
                loads["left"] = local(first_in, left, 11)
                loads["first"] = loads["left"]
        else:
            heads_load = local(heads_in.at[turn[k]], grad_heads, 4)
            if "first" in loads:
                loads.pop("first").wait()
            heads_load.wait()

            def step_part(part, _):
                rows = pl.ds(pl.multiple_of(part * 640, 640), 640)
                by_first = dot_tn(left[:, rows], wide[:, k * SPAN : k * SPAN + 480])
                by_branch = dot_tn(grad[:, rows], grad_heads[:, 96:256])
                product[k, rows, :] = jnp.concatenate([by_first, by_branch], -1).astype(BF16)
                return 0

            lax.fori_loop(0, 2, step_part, 0)
        stage_one(array, k)

    steps_done = {"hb": 0, "att": 0, "aend": 0, "none": 0, "reloc": 0}

    def count_step(name):
        steps_done[name] += 1
        return steps_done[name] - 1

    def hb():
        k = count_step("hb")
        if k == 0:
            loads["weight"].wait()
        slab = pl.ds(pl.multiple_of(turn[k] * SPAN + 384, 128), 256)

        def step_rows(step, _):
            rows = pl.ds(pl.multiple_of(step * 512, 512), 512)
            grad_heads[rows, :] = dot_nn(grad[rows, :], weight[:, slab]).astype(BF16)
            return 0

        lax.fori_loop(0, count // 512, step_rows, 0)
        loads["joined"][k].wait()
        totals_loads[k].wait()
        key_sum[...] = jnp.zeros_like(key_sum)
        value_sum[...] = jnp.zeros_like(value_sum)
        att_total[0] = start

    one_lane = (lax.broadcasted_iota(jnp.int32, (256, 48), 1) == 0).astype(F32).astype(BF16)

    def att():
        step_at = count_step("att")
        k, part = step_at // 3, step_at % 3
        low = k * SPAN

        def step_rows(step, total):
            rows = pl.ds(pl.multiple_of(step * 256, 256), 256)
            queries = wide[rows, low : low + 160]
            grads = grad_heads[rows, :]
            outs = []
            for head in range(2):
                at = head * HDIM
                query = queries[:, at : at + HDIM]
                above = grads[:, 96 + at : 96 + at + HDIM]
                key = wide[:, low + 160 + at : low + 160 + at + HDIM]
                value = wide[:, low + 320 + at : low + 320 + at + HDIM]
                scores = dot_nt(
                    jnp.concatenate([key, key_mask[:, :48]], -1),
                    jnp.concatenate([query, one_lane], -1),
                )
                probs = jnp.exp2(scores * (scaling * LOG2E) - totals[k, head : head + 1, rows])
                grad_probs = dot_nt(value, above)
                shared = jnp.sum(probs * grad_probs, 0, keepdims=True)
                grad_scores = (probs * (grad_probs - shared)).astype(BF16)
                value_sum[head, :, :HDIM] += dot_nn(probs.astype(BF16), above)
                key_sum[head, :, :HDIM] += dot_nn(grad_scores, query)
                outs.append(dot_tn(grad_scores, key) * scaling)
            joined = jnp.concatenate(outs, -1)
            wide[rows, low : low + 160] = joined.astype(BF16)
            return total + jnp.sum(joined, 0, keepdims=True)

        att_total[0] = lax.fori_loop(2 * part, 2 * part + 2, step_rows, att_total[0])

    def aend():
        k = count_step("aend")
        low = k * SPAN

        def step_rows(step, value_total):
            rows = pl.ds(pl.multiple_of(step * 256, 256), 256)
            keys = [key_sum[head, rows, :HDIM] * scaling for head in range(2)]
            values = [value_sum[head, rows, :HDIM] for head in range(2)]
            joined = jnp.concatenate(keys + values, -1)
            wide[rows, low + 160 : low + 480] = joined.astype(BF16)
            return value_total + jnp.sum(joined[:, 160:], 0, keepdims=True)

        value_total = lax.fori_loop(0, count // 256, step_rows, start)
        sums[16 + 2 * turn[k] + core, :, :160] = att_total[0]
        sums[16 + 2 * turn[k] + core, :, 160:320] = value_total

    def first_part(rows):
        total = None
        for k in range(TURNS):
            slab = pl.ds(pl.multiple_of(turn[k] * SPAN, 128), 480)
            part = dot_nt(wide[rows, k * SPAN : k * SPAN + 480], weight[:, slab])
            total = part if total is None else total + part
        return total

    def foth():
        for copy in staged[1:]:
            copy.wait_send()

        def step_rows(step, _):
            rows = pl.ds(pl.multiple_of(other + step * 256, 256), 256)
            low = pl.ds(pl.multiple_of(step * 256, 256), 256)
            send_rows[low, :] = first_part(rows).astype(BF16)
            return 0

        lax.fori_loop(0, half // 256, step_rows, 0)

    def none():
        step = count_step("none")
        low = slice(step * 256, step * 256 + 256)
        rows = pl.ds(pl.multiple_of(base + step * 256, 256), 256)
        above = first_part(rows) + got_rows[low, :].astype(F32)
        values = got_tok[low, :].astype(F32)
        back, by_gain, by_shift = norm_back_rows(values, gain_one[...][None, :], above)
        grad[half + step * 256 : half + step * 256 + 256, :] = (middle[low, :] + back).astype(BF16)
        if step == 0:
            sums[4, :, :] = by_gain
            sums[5, :, :] = by_shift
        else:
            sums[4, :, :] += by_gain
            sums[5, :, :] += by_shift

    got_tok = grad.at[0:half]

    def tokens_move(step):
        rows = pl.ds(step * 256, 256)
        source = grad.at[half + step * 256 : half + step * 256 + 256]
        away = remote(source, tokens_out.at[rows], 87 + step, to_clip)
        here = pltpu.make_async_copy(source, tokens_out.at[rows], local_sem.at[25 + step])
        return away, here

    def reloc():
        away, here = tokens_move(count_step("reloc"))

        @pl.when(moves)
        def _():
            away.start()

        @pl.when(jnp.logical_not(moves))
        def _():
            here.start()

    def wreloc():
        for step in range(half // 256):
            away, here = tokens_move(step)

            @pl.when(moves)
            def _(away=away):
                away.wait()

            @pl.when(jnp.logical_not(moves))
            def _(here=here):
                here.wait()

    hops = {"c": (0, to_core), "x": (1, to_x), "y": (2, to_y), "z1": (3, to_z_pair), "z2": (4, to_z[2])}
    hop_copies = {}

    def hs(name):
        index, device = hops[name]
        hop_copies[name] = send(sums, sums_got.at[index], 93 + index, device)

    def hw(name):
        index, _ = hops[name]
        hop_copies[name].wait_send()
        arrived(sums_got.at[index], 93 + index)
        sums[...] = sums[...] + sums_got[index]

    layer_away = remote(layer_low, layer_out, 99, to_clip)
    layer_here = pltpu.make_async_copy(layer_low, layer_out, local_sem.at[30])

    def layer(stage):
        if stage == 0:
            arrived(layer_got, 98)
            loads["layer"] = local(layer_got, send_rows, 28)
        elif stage == 1:
            layer_load.wait()
            loads["layer"].wait()

            def step_rows(step, _):
                rows = pl.ds(pl.multiple_of(step * 256, 256), 256)
                send_rows[rows, :] = (middle[rows, :] + send_rows[rows, :].astype(F32)).astype(BF16)
                return 0

            lax.fori_loop(0, half // 256, step_rows, 0)
            loads["layer"] = local(send_rows, layer_low, 29)
            loads["middle"] = local(middle_in, middle, 12)
        elif stage == 2:
            loads["layer"].wait()

            @pl.when(moves)
            def _():
                layer_away.start()

            @pl.when(jnp.logical_not(moves))
            def _():
                layer_here.start()
        else:
            layer_sent.wait_send()

            @pl.when(moves)
            def _():
                layer_away.wait()

            @pl.when(jnp.logical_not(moves))
            def _():
                layer_here.wait()

    def token_load():
        exchange["b"].wait_send()
        loads["tok"] = local(tok_in, grad.at[0:half], 2)

    actions = {
        "load": load, "pre": pre, "soth": soth, "ntwo": ntwo, "hb": hb, "att": att, "aend": aend,
        "foth": foth, "none": none, "reloc": reloc, "wreloc": wreloc, "send": hand, "wait": take,
        "P": produce, "2": stage_two, "3": stage_three, "F": final_one, "G": final_two, "hs": hs, "hw": hw,
        "tok": token_load, "layer": layer,
    }
    for name, *numbers in BACKWARD_STEPS:
        actions[name](*numbers)
    sums_put = local(sums, sums_out, 5)
    exchange["c"].wait_send()
    for wait in final_moves + last_moves:
        wait()
    for k in range(TURNS):
        ready(k)
    sums_put.wait()


def backward_pass(
    w_attn, w_up, w_down, tok, grad, first, second, joined, heads, middle, hidden, slope, totals, layer_own,
    layer_other, key_mask, gain_one, gain_two,
):
    half, features = tok.shape
    count = 2 * half
    any_space = pl.BlockSpec(memory_space=pl.ANY)
    vmem = pl.BlockSpec(memory_space=pltpu.VMEM)
    cols = TURNS * SPAN
    shapes = [
        ((half, features), BF16), ((UNIT // 2, 2 * SPAN), F32), ((UNIT // 2, 2 * SPAN), F32),
        ((UNIT // 2, 2 * SPAN), F32), ((24, 1, features), F32), ((count, cols), BF16),
        ((half, features), BF16), ((half, features), BF16), ((half, features), BF16),
    ]
    return pl.pallas_call(
        functools.partial(backward_kernel, HDIM ** (-0.5)),
        in_specs=[any_space] * 15 + [vmem] * 3,
        out_specs=[any_space] * len(shapes),
        out_shape=[jax.ShapeDtypeStruct(shape, kind) for shape, kind in shapes],
        scratch_shapes=[
            pltpu.VMEM((features, cols), BF16),
            pltpu.VMEM((count, features), BF16),
            pltpu.VMEM((count, features), BF16),
            pltpu.VMEM((count, cols), BF16),
            pltpu.VMEM((2, count, SPAN), BF16),
            pltpu.VMEM((count, 256), BF16),
            pltpu.VMEM((TURNS, 8, count), F32),
            pltpu.VMEM((half, features), F32),
            pltpu.VMEM((half, features), BF16),
            pltpu.VMEM((half, features), BF16),
            pltpu.VMEM((2, count, 128), F32),
            pltpu.VMEM((2, count, 128), F32),
            pltpu.VMEM((TURNS, features, SPAN), BF16),
            pltpu.VMEM((TURNS, UNIT, SPAN), BF16),
            pltpu.VMEM((TURNS, UNIT, SPAN), BF16),
            pltpu.VMEM((TURNS, UNIT, SPAN), BF16),
            pltpu.VMEM((TURNS, UNIT, SPAN), BF16),
            pltpu.VMEM((UNIT, SPAN), BF16),
            pltpu.VMEM((UNIT, SPAN), F32),
            pltpu.VMEM((3, UNIT // 2, SPAN), F32),
            pltpu.VMEM((24, 1, features), F32),
            pltpu.VMEM((5, 24, 1, features), F32),
            pltpu.SemaphoreType.DMA((100,)),
            pltpu.SemaphoreType.DMA((100,)),
            pltpu.SemaphoreType.DMA((32,)),
            pltpu.SemaphoreType.REGULAR((24,)),
        ],
        cost_estimate=pl.CostEstimate(
            flops=4 * count * features * 6400, bytes_accessed=90_000_000, transcendentals=30_000_000
        ),
        compiler_params=pltpu.CompilerParams(
            vmem_limit_bytes=60 << 20, collective_id=1, has_side_effects=True
        ),
        name="backward_pass",
    )(
        w_attn, w_up, w_down, tok, grad, first, second, joined, heads, middle, hidden, slope, totals,
        layer_own, layer_other, key_mask, gain_one, gain_two,
    )


def finish_kernel(*refs):
    z = lax.axis_index("tensor")
    large_in, attn, sums = refs[:4], refs[4], refs[5]
    large_out, grads, vectors, sem = refs[6:10], refs[10:14], refs[14:-1], refs[-1]
    copies = [
        pltpu.make_async_copy(source, target, sem.at[i])
        for i, (source, target) in enumerate(zip(large_in, large_out))
    ]
    for copy in copies:
        copy.start()
    width = UNIT // 2
    for i, grad in enumerate(grads):
        low = i * width
        halves = [attn[:, half * SPAN + low : half * SPAN + low + width] for half in range(2)]
        grad[...] = jnp.concatenate(halves, -1)
    for vector, row, start, size in zip(vectors, (16, 16, 8), (0, width, 0), (width, width, SPAN)):
        halves = [sums[row + 2 * z + half][:, start : start + size] for half in range(2)]
        vector[...] = jnp.concatenate(halves, -1)[0]
    for i, vector in enumerate(vectors[3:]):
        vector[...] = sums[i][0]
    for copy in copies:
        copy.wait()


def finish(layer_out, grad_tokens, grad_up, grad_down, grad_attn, sums):
    features = layer_out.shape[1]
    any_space = pl.BlockSpec(memory_space=pl.ANY)
    vmem = pl.BlockSpec(memory_space=pltpu.VMEM)
    large = (layer_out, grad_tokens, grad_up, grad_down)
    shapes = [jax.ShapeDtypeStruct(value.shape, value.dtype) for value in large]
    shapes += [jax.ShapeDtypeStruct((UNIT // 2, UNIT), F32)] * 4
    shapes += [jax.ShapeDtypeStruct((size,), F32) for size in (UNIT, UNIT, 2 * SPAN) + (features,) * 6]
    return pl.pallas_call(
        finish_kernel,
        in_specs=[any_space] * 4 + [vmem] * 2,
        out_specs=[any_space] * 4 + [vmem] * 13,
        out_shape=shapes,
        scratch_shapes=[pltpu.SemaphoreType.DMA((4,))],
        name="finish",
    )(*large, grad_attn, sums)


class Links:
    def __init__(self):
        self.dp = lax.axis_size("dp")
        self.tensor = lax.axis_size("tensor")
        self.tensor_pos = lax.axis_index("tensor")
        self.half = self.tensor_pos % 2

    def pair(self, value):
        return lax.ppermute(value, "tensor", [(i, i ^ 1) for i in range(self.tensor)])

    def columns(self, shard):
        rows, _, width = shard.shape
        whole = lax.all_gather(shard, ("dp", "tensor"), axis=0)
        whole = lax.dynamic_index_in_dim(whole, self.half, 2, keepdims=False)
        whole = whole.reshape(self.dp, self.tensor, rows, width)
        return [whole[:, k].reshape(self.dp * rows, width) for k in range(self.tensor)]

    def vectors(self, value):
        whole = lax.all_gather(value, "tensor", axis=0)
        return [whole[k] for k in range(self.tensor)]

    def place(self, pieces):
        halves = (jnp.arange(2) == self.half)[None, :, None]
        return jnp.where(halves, jnp.stack(pieces)[:, None, :], 0.0)

    def gradient(self, left, rights):
        whole = jnp.stack([dot_tn(left, right).astype(BF16) for right in rights], 0)
        features, width = whole.shape[1:]
        whole = whole.reshape(self.tensor, self.dp, features // self.dp, width)
        whole = jnp.moveaxis(whole, 1, 0)[:, :, :, None, :]
        halves = (jnp.arange(2) == self.half)[None, None, None, :, None]
        whole = jnp.where(halves, whole, jnp.zeros((), BF16))
        whole = whole.reshape((self.dp * self.tensor,) + whole.shape[2:])
        return lax.psum_scatter(whole, ("dp", "tensor"), tiled=False).astype(F32)

    def merged(self, partial_of):
        got = self.pair(partial_of(1).astype(BF16))
        return partial_of(0) + got.astype(F32)


def summed(vectors, total):
    whole = total(jnp.concatenate(vectors))
    at = 0
    result = []
    for vector in vectors:
        result.append(whole[at : at + vector.shape[0]])
        at += vector.shape[0]
    return result


def halves_of(weight):
    return weight.reshape(weight.shape[0], 2, weight.shape[1] // 2)


def flat(piece):
    return piece.reshape(piece.shape[0], -1)


def local_any(
    tokens,
    lengths,
    cotangent,
    norm1_gain,
    norm1_shift,
    query_weight,
    query_bias,
    key_weight,
    value_weight,
    value_bias,
    out_weight,
    out_bias,
    norm2_gain,
    norm2_shift,
    up_weight,
    up_bias,
    down_weight,
    down_bias,
):
    links = Links()
    rows = tokens.shape[0]
    scaling = HDIM ** (-0.5)
    width = query_weight.shape[1] // 2
    heads = width // HDIM
    units = up_weight.shape[1] // 2
    count = links.tensor

    shard_attn = [query_weight, key_weight, value_weight, out_weight.T]
    w_attn = links.columns(jnp.concatenate([halves_of(w) for w in shard_attn], -1))
    w_up = jnp.concatenate(links.columns(halves_of(up_weight)), 1)
    w_down = jnp.concatenate(links.columns(halves_of(down_weight.T)), 1)
    w_qkv = [block[:, : 3 * width] for block in w_attn]
    w_out = [block[:, 3 * width :] for block in w_attn]
    small = [query_bias.reshape(2, width), value_bias.reshape(2, width), up_bias.reshape(2, units)]
    small = jnp.concatenate(small, -1)
    small = links.vectors(jnp.where(links.half == 0, small[0], small[1]))
    bias_qkv = [
        jnp.concatenate([v[:width], jnp.zeros((width,), F32), v[width : 2 * width]]) for v in small
    ]
    bias_up = jnp.concatenate([v[2 * width :] for v in small])

    place = links.tensor_pos // 2
    clip_length = jnp.sum(jnp.where(jnp.arange(lengths.shape[0]) == place, lengths, 0))
    frames = jnp.arange(rows)
    frames = jnp.concatenate([links.half * rows + frames, (1 - links.half) * rows + frames])
    visible = frames < clip_length
    mask = jnp.where(visible, 0.0, -1e30).astype(F32)

    def part_of(value, part):
        return value[part * rows : (part + 1) * rows]

    def both(value):
        return jnp.concatenate([value, links.pair(value)])

    source = tokens.astype(F32)
    first = both(norm_rows(source, norm1_gain, norm1_shift).astype(BF16))
    joined, heads_out, totals = [], [], []
    for k in range(count):
        joined.append((dot_nn(first, w_qkv[k]) + bias_qkv[k]).astype(BF16))
        mixed, total = attend(joined[k], mask[None, :], heads, scaling)
        heads_out.append(mixed)
        totals.append(total)
    heads_all = jnp.concatenate(heads_out, 1)
    w_out_all = jnp.concatenate(w_out, 1)
    branch = links.merged(lambda part: dot_nt(part_of(heads_all, part), w_out_all))
    middle = source + branch + out_bias
    second = both(norm_rows(middle, norm2_gain, norm2_shift).astype(BF16))
    hidden, slope = up_gelu(second, w_up, bias_up[None, :])
    out_own = cotangent * visible[:rows].astype(BF16)[:, None]
    out_grad = both(out_own)

    def cut(value):
        return [value[:, k * units : (k + 1) * units] for k in range(count)]

    grad_down = links.gradient(out_grad, cut(hidden))
    down_out = links.merged(lambda part: dot_nt(part_of(hidden, part), w_down))
    layer_out = (middle + down_out + down_bias).astype(BF16)
    grad_pre = (dot_nn(out_grad, w_down) * slope.astype(F32)).astype(BF16)
    grad_up = links.gradient(second, cut(grad_pre))
    grad_second = links.merged(lambda part: dot_nt(part_of(grad_pre, part), w_up))
    back_two, grad_gain_two, grad_shift_two = norm_back(middle, norm2_gain, grad_second)
    grad_middle = out_own.astype(F32) + back_two
    branch_grad = both(grad_middle.astype(BF16))
    grad_heads = [dot_nn(branch_grad, w_out[k]).astype(BF16) for k in range(count)]
    grad_out_w = links.gradient(branch_grad, heads_out)
    grad_joined, sums = [], []
    for k in range(count):
        back, sum_k = attend_back(joined[k], grad_heads[k], totals[k], mask[:, None], heads, scaling)
        grad_joined.append(back)
        sums.append(sum_k)
    grad_qkv = links.gradient(first, grad_joined)
    grad_all = jnp.concatenate(grad_joined, 1)
    w_qkv_all = jnp.concatenate(w_qkv, 1)
    grad_first = links.merged(lambda part: dot_nt(part_of(grad_all, part), w_qkv_all))
    back_one, grad_gain_one, grad_shift_one = norm_back(source, norm1_gain, grad_first)
    grad_tokens = (grad_middle + back_one).astype(BF16)

    vectors = [
        links.place([v[0] for v in cut(jnp.sum(grad_pre.astype(F32), 0)[None, :])]).reshape(-1),
        links.place([s[0, :width] for s in sums]).reshape(-1),
        links.place([s[1, :width] for s in sums]).reshape(-1),
        grad_gain_one,
        grad_shift_one,
        jnp.sum(grad_middle, 0),
        grad_gain_two,
        grad_shift_two,
        jnp.sum(out_own.astype(F32), 0),
    ]
    sum_up, sum_query, sum_value, *rest = summed(
        vectors, lambda value: lax.psum(value, ("dp", "tensor"))
    )
    sum_gain_one, sum_shift_one, sum_out, sum_gain_two, sum_shift_two, sum_down = rest

    def own(vector):
        size = vector.shape[0] // count
        return lax.dynamic_slice_in_dim(vector, links.tensor_pos * size, size, 0)

    return (
        layer_out,
        grad_tokens,
        sum_gain_one,
        sum_shift_one,
        flat(grad_qkv[:, :, :width]),
        own(sum_query),
        flat(grad_qkv[:, :, width : 2 * width]),
        flat(grad_qkv[:, :, 2 * width :]),
        own(sum_value),
        flat(grad_out_w).T,
        sum_out,
        sum_gain_two,
        sum_shift_two,
        flat(grad_up),
        own(sum_up),
        flat(grad_down).T,
        sum_down,
    )


def local_chips(
    tokens,
    lengths,
    cotangent,
    norm1_gain,
    norm1_shift,
    query_weight,
    query_bias,
    key_weight,
    value_weight,
    value_bias,
    out_weight,
    out_bias,
    norm2_gain,
    norm2_shift,
    up_weight,
    up_bias,
    down_weight,
    down_bias,
):
    weights = (query_weight, key_weight, value_weight, out_weight.T)
    vectors = (
        query_bias, value_bias, up_bias, norm1_gain, norm1_shift, norm2_gain, norm2_shift, out_bias,
        down_bias,
    )
    (
        w_attn, w_up, w_down, tok, out_grad, mask, first, second, joined, heads, totals, middle, hidden,
        slope, layer_own, layer_other,
    ) = forward_pass(lengths, (up_weight, down_weight.T), tokens, cotangent, weights, vectors)
    lane = jnp.arange(128)[None, :] == 0
    key_mask = jnp.where(lane, mask[0][:, None], 0.0).astype(BF16)
    grad_tokens, grad_down, grad_up, grad_attn, sums, _, layer_out, _, _ = backward_pass(
        w_attn, w_up, w_down, tok, out_grad, first, second, joined, heads, middle, hidden, slope, totals,
        layer_own, layer_other, key_mask, norm1_gain, norm2_gain,
    )

    (
        layer_out, grad_tokens, grad_up, grad_down, grad_query, grad_key, grad_value, grad_out, sum_query,
        sum_value, sum_up, *sums,
    ) = finish(layer_out, grad_tokens, grad_up, grad_down, grad_attn, sums)
    sum_down, sum_out, sum_gain_two, sum_shift_two, sum_gain_one, sum_shift_one = sums
    return (
        layer_out,
        grad_tokens,
        sum_gain_one,
        sum_shift_one,
        grad_query,
        sum_query,
        grad_key,
        grad_value,
        sum_value,
        grad_out.T,
        sum_out,
        sum_gain_two,
        sum_shift_two,
        grad_up,
        sum_up,
        grad_down.T,
        sum_down,
    )


def solution(mesh):
    rows = P(("dp", "tensor"), None)
    wide, tall = P("dp", "tensor"), P("tensor", "dp")
    piece, same = P("tensor"), P()
    chips = mesh.shape["dp"] == 8 and mesh.shape["tensor"] == 4
    return jax.shard_map(
        local_chips if chips else local_any,
        mesh=mesh,
        in_specs=(
            rows, P("dp"), rows, same, same, wide, piece, wide, wide, piece, tall, same, same, same,
            wide, piece, tall, same,
        ),
        out_specs=(
            rows, rows, same, same, wide, piece, wide, wide, piece, tall, same, same, same, wide, piece,
            tall, same,
        ),
        check_vma=False,
    )
```

```python
import functools

import jax
import jax.numpy as jnp
from jax import lax
from jax.experimental import pallas as pl
from jax.experimental.pallas import tpu as pltpu
from jax.sharding import PartitionSpec as P

HDIM = 80
EPS = 1e-05
LOG2E = 1.4426950408889634
F32 = jnp.float32
BF16 = jnp.bfloat16


def norm_rows(values, norm_gain, norm_shift):
    center = values - jnp.mean(values, -1, keepdims=True)
    spread = jnp.mean(center * center, -1, keepdims=True)
    return center * lax.rsqrt(spread + EPS) * norm_gain + norm_shift


def norm_back(values, norm_gain, grad):
    center = values - jnp.mean(values, -1, keepdims=True)
    scale = lax.rsqrt(jnp.mean(center * center, -1, keepdims=True) + EPS)
    normed = center * scale
    scaled = grad * norm_gain
    back = scaled - jnp.mean(scaled, -1, keepdims=True)
    back = (back - normed * jnp.mean(scaled * normed, -1, keepdims=True)) * scale
    return back, jnp.sum(grad * normed, 0), jnp.sum(grad, 0)


def dot_nn(left, right):
    return jnp.dot(left, right, preferred_element_type=F32)


def dot_tn(left, right):
    return lax.dot_general(left, right, (((0,), (0,)), ((), ())), preferred_element_type=F32)


def dot_nt(left, right):
    return lax.dot_general(left, right, (((1,), (1,)), ((), ())), preferred_element_type=F32)


def up_kernel(rows_ref, weight_ref, bias_ref, hidden_ref, slope_ref):
    pre = dot_nn(rows_ref[...], weight_ref[...]) + bias_ref[...]
    cdf = 0.5 * lax.erf(pre * (0.5**0.5)) + 0.5
    density = jnp.exp(-0.5 * pre * pre) * 0.3989422804014327
    hidden_ref[...] = (pre * cdf).astype(BF16)
    slope_ref[...] = (cdf + pre * density).astype(BF16)


def up_gelu(rows, weight, bias):
    count, depth = rows.shape
    cols = weight.shape[1]
    block_rows, block_cols = min(512, count), min(640, cols)
    return pl.pallas_call(
        up_kernel,
        grid=(cols // block_cols, count // block_rows),
        in_specs=[
            pl.BlockSpec((block_rows, depth), lambda n, m: (m, 0)),
            pl.BlockSpec((depth, block_cols), lambda n, m: (0, n)),
            pl.BlockSpec((1, block_cols), lambda n, m: (0, n)),
        ],
        out_specs=[
            pl.BlockSpec((block_rows, block_cols), lambda n, m: (m, n)),
            pl.BlockSpec((block_rows, block_cols), lambda n, m: (m, n)),
        ],
        out_shape=[jax.ShapeDtypeStruct((count, cols), BF16)] * 2,
        cost_estimate=pl.CostEstimate(
            flops=2 * count * depth * cols, bytes_accessed=20_000_000, transcendentals=0
        ),
        compiler_params=pltpu.CompilerParams(vmem_limit_bytes=40 << 20),
        name="up_gelu",
    )(rows, weight, bias)


def attend_kernel(heads, scaling, query_ref, all_ref, mask_ref, out_ref, total_ref):
    width = heads * HDIM
    queries = query_ref[...]
    mask = mask_ref[...]
    outs, totals = [], []
    for head in range(heads):
        low = head * HDIM
        query = queries[:, low : low + HDIM]
        key = all_ref[:, width + low : width + low + HDIM]
        value = all_ref[:, 2 * width + low : 2 * width + low + HDIM]
        scores = dot_nt(query, key) * (scaling * LOG2E) + mask
        row_max = jnp.max(scores, -1, keepdims=True)
        exp_scores = jnp.exp2(scores - row_max)
        total = jnp.sum(exp_scores, -1, keepdims=True)
        mixed = dot_nn(exp_scores.astype(BF16), value)
        outs.append(mixed * (1.0 / total))
        totals.append(row_max + jnp.log2(total))
    out_ref[...] = jnp.concatenate(outs, -1).astype(BF16)
    for head in range(heads):
        wide = jnp.broadcast_to(totals[head], (totals[head].shape[0], 128))
        total_ref[head : head + 1, :] = wide.T[0:1, :]


def attend(joined, mask_row, heads, scaling):
    count, cols = joined.shape
    block_rows = min(256, count)
    width = heads * HDIM
    return pl.pallas_call(
        functools.partial(attend_kernel, heads, scaling),
        grid=(count // block_rows,),
        in_specs=[
            pl.BlockSpec((block_rows, cols), lambda m: (m, 0)),
            pl.BlockSpec((count, cols), lambda m: (0, 0)),
            pl.BlockSpec((1, count), lambda m: (0, 0)),
        ],
        out_specs=[
            pl.BlockSpec((block_rows, width), lambda m: (m, 0)),
            pl.BlockSpec((heads, block_rows), lambda m: (0, m)),
        ],
        out_shape=[
            jax.ShapeDtypeStruct((count, width), BF16),
            jax.ShapeDtypeStruct((heads, count), F32),
        ],
        cost_estimate=pl.CostEstimate(
            flops=2 * heads * count * count * 512,
            bytes_accessed=4_000_000,
            transcendentals=heads * count * count,
        ),
        compiler_params=pltpu.CompilerParams(vmem_limit_bytes=48 << 20),
        name="attend",
    )(joined, joined, mask_row)


def attend_back_kernel(
    heads, scaling, query_ref, all_ref, grad_ref, total_ref, mask_ref,
    out_ref, sums_ref, key_sum, value_sum,
):
    step = pl.program_id(0)
    steps = pl.num_programs(0)
    width = heads * HDIM
    block_rows = query_ref.shape[0]

    @pl.when(step == 0)
    def _():
        key_sum[...] = jnp.zeros_like(key_sum)
        value_sum[...] = jnp.zeros_like(value_sum)
        sums_ref[...] = jnp.zeros_like(sums_ref)

    queries = query_ref[...]
    grads = grad_ref[...]
    query_outs = []
    for head in range(heads):
        low = head * HDIM
        query = queries[:, low : low + HDIM]
        grad = grads[:, low : low + HDIM]
        key = all_ref[:, width + low : width + low + HDIM]
        value = all_ref[:, 2 * width + low : 2 * width + low + HDIM]
        scores = dot_nt(key, query) * (scaling * LOG2E) + mask_ref[...]
        probs = jnp.exp2(scores - total_ref[head : head + 1, :])
        grad_probs = dot_nt(value, grad)
        shared = jnp.sum(probs * grad_probs, 0, keepdims=True)
        grad_scores = (probs * (grad_probs - shared)).astype(BF16)
        value_sum[head, :, :HDIM] += dot_nn(probs.astype(BF16), grad)
        key_sum[head, :, :HDIM] += dot_nn(grad_scores, query)
        query_outs.append(dot_tn(grad_scores, key) * scaling)
    joined = jnp.concatenate(query_outs, -1)
    sums_ref[0:1, :width] += jnp.sum(joined, 0, keepdims=True)
    rows = pl.ds(pl.multiple_of(step * block_rows, block_rows), block_rows)
    out_ref[rows, :width] = joined.astype(BF16)

    @pl.when(step == steps - 1)
    def _():
        keys = jnp.concatenate([key_sum[head, :, :HDIM] for head in range(heads)], -1)
        values = jnp.concatenate([value_sum[head, :, :HDIM] for head in range(heads)], -1)
        sums_ref[1:2, :width] = jnp.sum(values, 0, keepdims=True)
        out_ref[:, width:] = jnp.concatenate([keys * scaling, values], -1).astype(BF16)


def attend_back(joined, grad_heads, totals, mask_col, heads, scaling):
    count, cols = joined.shape
    block_rows = min(256, count)
    width = heads * HDIM
    return pl.pallas_call(
        functools.partial(attend_back_kernel, heads, scaling),
        grid=(count // block_rows,),
        in_specs=[
            pl.BlockSpec((block_rows, cols), lambda m: (m, 0)),
            pl.BlockSpec((count, cols), lambda m: (0, 0)),
            pl.BlockSpec((block_rows, width), lambda m: (m, 0)),
            pl.BlockSpec((heads, block_rows), lambda m: (0, m)),
            pl.BlockSpec((count, 1), lambda m: (0, 0)),
        ],
        out_specs=[
            pl.BlockSpec((count, cols), lambda m: (0, 0)),
            pl.BlockSpec((8, 256), lambda m: (0, 0)),
        ],
        out_shape=[
            jax.ShapeDtypeStruct((count, cols), BF16),
            jax.ShapeDtypeStruct((8, 256), F32),
        ],
        scratch_shapes=[
            pltpu.VMEM((heads, count, 128), F32),
            pltpu.VMEM((heads, count, 128), F32),
        ],
        cost_estimate=pl.CostEstimate(
            flops=2 * heads * count * count * 1280,
            bytes_accessed=5_000_000,
            transcendentals=heads * count * count,
        ),
        compiler_params=pltpu.CompilerParams(vmem_limit_bytes=56 << 20),
        name="attend_back",
    )(joined, joined, grad_heads, totals, mask_col)


UNIT = 320
SPAN = 640
TURNS = 4


def clamp_rows(ref, start, size):
    return ref.at[pl.ds(pl.multiple_of(start, 16), size)]


FORWARD_STEPS = (
    ("pr", 0), ("tok",), ("pr", 1), ("zz", 0), ("pp", 0, 0), ("pp", 1, 0), ("pr", 2), ("fw", 0, 0),
    ("fw", 1, 0), ("tokw",), ("pp", 2, 0), ("norm",), ("send", "a"), ("wait", "a"), ("pp", 0, 1), ("proj",),
    ("fw", 2, 0), ("att",), ("att",), ("fw", 0, 1), ("zz", 1), ("pp", 0, 2), ("pp", 0, 3), ("proj",),
    ("att",), ("att",), ("zz", 2), ("fw", 0, 2), ("fw", 0, 3), ("pp", 1, 1), ("cot",), ("pp", 1, 2),
    ("proj",), ("att",), ("att",), ("pp", 1, 3), ("proj",), ("att",), ("pp", 2, 1), ("att",), ("fw", 1, 3),
    ("fw", 1, 2), ("both",), ("send", "b"), ("bown",), ("wait", "b"), ("fw", 1, 1), ("ntwo",),
    ("send", "c"), ("fw", 2, 1), ("pp", 2, 2), ("wait", "c"), ("pp", 2, 3), ("lift",), ("lift",), ("lift",),
    ("lift",), ("down",), ("fw", 2, 2), ("fw", 2, 3), ("cotx",), ("down",), ("down",), ("cotw",), ("down",),
)


def forward_kernel(
    scaling,
    lengths, up_shard, down_shard, tokens, cotangent, query_weight, key_weight, value_weight, out_weight,
    query_bias, value_bias, up_bias, gain_one, shift_one, gain_two, shift_two, bias_out, bias_down,
    w_attn_out, w_up_out, w_down, tokens_out, grad_out, mask_out, first_out, second_out, joined_out,
    heads_out, totals_out, middle_out, hidden_out, slope_out, layer_own_out, layer_other_out,
    w_attn, w_up, tok, first, second, joined, heads, middle, send_rows, got_rows, layer_other, slope,
    mask_own, mask, totals, bias, params, attn_shard, bias_in, send_sem, recv_sem, local_sem,
):
    dp, z = lax.axis_index("dp"), lax.axis_index("tensor")
    core, plane = lax.rem(dp, 2), lax.div(dp, 2)
    x_bit, y_bit = lax.rem(plane, 2), lax.div(plane, 2)
    half = tok.shape[0]
    count = 2 * half
    to_x = (y_bit * 4 + (1 - x_bit) * 2 + core, z)
    to_y = ((1 - y_bit) * 4 + x_bit * 2 + core, z)
    to_core = (plane * 2 + 1 - core, z)
    to_clip = (plane * 2 + 1 - core, z + 1 - 2 * lax.rem(z, 2))
    to_z = [(dp, lax.rem(z + k, TURNS)) for k in range(TURNS)]
    moves = core != lax.rem(z, 2)
    plane_x = y_bit * 2 + 1 - x_bit
    plane_y = (1 - y_bit) * 2 + x_bit
    plane_xy = (1 - y_bit) * 2 + 1 - x_bit
    turn = [lax.rem(z + TURNS - k, TURNS) for k in range(TURNS)]
    base = pl.multiple_of(core * half, 256)
    other = pl.multiple_of((1 - core) * half, 256)
    own_rows, other_rows = pl.ds(base, half), pl.ds(other, half)

    barrier = pltpu.get_barrier_semaphore()
    partners = [to_x, to_y, to_core, to_clip] + to_z[1:]
    for partner in partners:
        pl.semaphore_signal(barrier, inc=1, device_id=partner, device_id_type=pl.DeviceIdType.MESH)
    width = UNIT // 2
    parts = [query_weight[...], key_weight[...], value_weight[...], out_weight[...]]
    pieces = [part[:, i * width : (i + 1) * width] for i in range(2) for part in parts]
    attn_shard[...] = jnp.concatenate(pieces, -1)

    def half_of(vector):
        row = vector[...][None, :]
        size = row.shape[1] // 2
        return jnp.where(core == 0, row[:, :size], row[:, size:])

    gap = jnp.zeros((1, width), F32)
    bias_in[...] = jnp.zeros_like(bias_in)
    bias_in[0:1, :] = jnp.concatenate([half_of(query_bias), gap, half_of(value_bias), gap], -1)
    bias_in[1:2, :] = half_of(up_bias)

    pl.semaphore_wait(barrier, len(partners))

    def remote(source, target, sem, device):
        return pltpu.make_async_remote_copy(
            src_ref=source,
            dst_ref=target,
            send_sem=send_sem.at[sem],
            recv_sem=recv_sem.at[sem],
            device_id=device,
            device_id_type=pl.DeviceIdType.MESH,
        )

    sent = {}

    def send(source, target, sem, device):
        copy = remote(source, target, sem, device)
        copy.start()
        sent[sem] = copy
        return copy

    def arrived(target, sem):
        remote(target, target, sem, to_core).wait_recv()

    outs = {}

    def put(source, target, sem):
        copy = pltpu.make_async_copy(source, target, local_sem.at[sem])
        copy.start()
        outs[sem] = copy

    def done(sem):
        outs.pop(sem).wait()

    weights = [w_attn, w_up, w_down]
    shards = [attn_shard, up_shard, down_shard]
    rows_half = UNIT // 2

    def columns(k):
        return pl.ds(pl.multiple_of(turn[k] * SPAN, 128), SPAN)

    def block(array, k, where, part=None):
        if part is None:
            rows = pl.ds(pl.multiple_of(where * UNIT, 16), UNIT)
        else:
            rows = pl.ds(pl.multiple_of(where * UNIT + part * rows_half, 16), rows_half)
        return weights[array].at[rows, columns(k)]

    def own_piece(array, which):
        rows = pl.ds(pl.multiple_of(plane * UNIT + which * rows_half, 16), rows_half)
        return weights[array].at[rows, columns(0)]

    def shard_half(array, which):
        return shards[array].at[:, pl.ds(pl.multiple_of(which * SPAN, 128), SPAN)]

    pairs = [None] * 3

    def pair_start(array):
        send(shard_half(array, 1 - core), own_piece(array, core), 72 + array, to_core)
        copy = pltpu.make_async_copy(
            shard_half(array, core), own_piece(array, core), local_sem.at[array]
        )
        copy.start()
        pairs[array] = copy

    def pair_wait(array):
        if pairs[array] is not None:
            pairs[array].wait()
            arrived(own_piece(array, 1 - core), 72 + array)
            pairs[array] = None

    def sem_of(array, kind, k):
        return array * 24 + kind * 4 + k

    def plane_send(array, k):
        if k == 0:
            pair_wait(array)
        else:
            arrived(block(array, k, plane), sem_of(array, 0, k))
        source = block(array, k, plane)
        send(source, source, sem_of(array, 1, k), to_x)
        send(source, source, sem_of(array, 2, k), to_y)

    def line_send(array):
        pair_wait(array)
        source = block(array, 0, plane)
        for k in range(1, TURNS):
            send(source, source, sem_of(array, 0, k), to_z[k])

    def forward_on(array, k):
        arrived(block(array, k, plane_x), sem_of(array, 1, k))
        source = block(array, k, plane_x, 0)
        send(source, source, sem_of(array, 3, k), to_y)
        arrived(block(array, k, plane_y), sem_of(array, 2, k))
        source = block(array, k, plane_y, 1)
        send(source, source, sem_of(array, 4, k), to_x)

    def complete(array, k):
        for part in range(2):
            arrived(block(array, k, plane_xy, part), sem_of(array, 3 + part, k))

    there = grad_out.at[other_rows]
    here = grad_out.at[own_rows]
    length = lengths[lax.div(z, 2)]
    frames = lax.broadcasted_iota(jnp.int32, mask_own.shape, 1)
    mask_own[...] = jnp.where(frames < length, 0.0, -1e30).astype(F32)
    tok_copy = pltpu.make_async_copy(tokens, tok, local_sem.at[3])
    mask_copy = pltpu.make_async_copy(mask_own, mask, local_sem.at[4])
    clip_tok = remote(tokens, tok, 75, to_clip)
    clip_mask = remote(mask_own, mask, 76, to_clip)
    cot_copy = pltpu.make_async_copy(send_rows, here, local_sem.at[5])
    clip_cot = remote(send_rows, there, 77, to_clip)
    bias_copy = pltpu.make_async_copy(bias_in, bias.at[z], local_sem.at[6])
    exchange = {}
    for i, vector in enumerate((gain_one, shift_one, gain_two, shift_two, bias_out, bias_down)):
        params[i : i + 1, :] = vector[...][None, :]

    def tok_start():
        @pl.when(moves)
        def _():
            clip_mask.start()
            clip_tok.start()

        @pl.when(jnp.logical_not(moves))
        def _():
            tok_copy.start()
            mask_copy.start()

        bias_copy.start()
        for k in range(1, TURNS):
            send(bias_in, bias.at[z], 77 + k, to_z[k])
        put(cotangent, send_rows, 7)

    def tok_wait():
        @pl.when(moves)
        def _():
            clip_mask.wait()
            clip_tok.wait()

        @pl.when(jnp.logical_not(moves))
        def _():
            tok_copy.wait()
            mask_copy.wait()

        put(tok, tokens_out, 8)
        put(mask, mask_out, 9)

    def cot_start():
        done(7)

        def step_rows(step, _):
            rows = pl.ds(pl.multiple_of(step * 256, 256), 256)
            at = lax.broadcasted_iota(jnp.int32, (256, send_rows.shape[1]), 0)
            at = at + (lax.rem(z, 2) * half + step * 256)
            values = jnp.where(at < length, send_rows[rows, :].astype(F32), 0.0)
            send_rows[rows, :] = values.astype(BF16)
            return 0

        lax.fori_loop(0, half // 256, step_rows, 0)

        @pl.when(moves)
        def _():
            clip_cot.start()

        @pl.when(jnp.logical_not(moves))
        def _():
            cot_copy.start()

    def cot_pair():
        @pl.when(moves)
        def _():
            arrived(here, 77)

        send(here, here, 81, to_core)

    def cot_wait():
        arrived(there, 81)

    def norm():
        def step_rows(step, _):
            rows = pl.ds(pl.multiple_of(step * 256, 256), 256)
            values = tok[rows, :].astype(F32)
            normed = norm_rows(values, params[0:1, :], params[1:2, :])
            first[pl.ds(pl.multiple_of(base + step * 256, 256), 256), :] = normed.astype(BF16)
            return 0

        lax.fori_loop(0, half // 256, step_rows, 0)

    def hand(name):
        if name == "a":
            exchange[name] = send(first.at[own_rows], first.at[own_rows], 82, to_core)
        elif name == "b":
            exchange[name] = send(send_rows, got_rows, 83, to_core)
        else:
            exchange[name] = send(second.at[own_rows], second.at[own_rows], 84, to_core)

    def take(name):
        if name == "a":
            arrived(first.at[other_rows], 82)
            put(first, first_out, 10)
            bias_copy.wait()
            for k in range(1, TURNS):
                arrived(bias.at[turn[k]], 77 + k)
        elif name == "b":
            arrived(got_rows, 83)
        else:
            arrived(second.at[other_rows], 84)
            put(second, second_out, 11)

    steps_done = {"proj": 0, "att": 0, "lift": 0, "down": 0}

    def count_step(name):
        steps_done[name] += 1
        return steps_done[name] - 1

    def proj():
        k = count_step("proj")
        complete(0, k)
        slab = pl.ds(pl.multiple_of(turn[k] * SPAN, 128), 480)

        def step_rows(step, _):
            rows = pl.ds(pl.multiple_of(step * half, half), half)
            product = dot_nn(first[rows, :], w_attn[:, slab]) + bias[turn[k], 0:1, :480]
            joined[k, rows, :480] = product.astype(BF16)
            return 0

        lax.fori_loop(0, 2, step_rows, 0)
        put(joined.at[k], joined_out.at[turn[k]], 12 + k)
        if k == TURNS - 1:
            put(w_attn, w_attn_out, 24)

    def att():
        step_at = count_step("att")
        k, part = step_at // 2, step_at % 2

        def step_rows(step, _):
            rows = pl.ds(pl.multiple_of(step * 256, 256), 256)
            queries = joined[k, rows, :160]
            mixes, logs = [jnp.zeros((256, 96), F32)], []
            for head in range(2):
                low = head * HDIM
                query = queries[:, low : low + HDIM]
                key = joined[k, :, 160 + low : 160 + low + HDIM]
                value = joined[k, :, 320 + low : 320 + low + HDIM]
                scores = dot_nt(query, key) * (scaling * LOG2E) + mask[0:1, :]
                row_max = jnp.max(scores, -1, keepdims=True)
                exp_scores = jnp.exp2(scores - row_max)
                total = jnp.sum(exp_scores, -1, keepdims=True)
                mixes.append(dot_nn(exp_scores.astype(BF16), value) * (1.0 / total))
                logs.append(row_max + jnp.log2(total))
            heads[k, rows, :] = jnp.concatenate(mixes, -1).astype(BF16)
            for head in range(2):
                wide = jnp.broadcast_to(logs[head], (256, 128))
                totals[k, head : head + 1, rows] = wide.T[0:1, :]
            return 0

        lax.fori_loop(3 * part, 3 * part + 3, step_rows, 0)
        if part == 1:
            put(heads.at[k], heads_out.at[turn[k]], 16 + k)
            put(totals.at[k], totals_out.at[turn[k]], 20 + k)

    def branch(rows):
        total = None
        for k in range(TURNS):
            slab = pl.ds(pl.multiple_of(turn[k] * SPAN + 384, 128), 256)
            product = dot_nt(heads[k, rows, :], w_attn[:, slab])
            total = product if total is None else total + product
        return total

    def both():
        @pl.when(moves)
        def _():
            clip_cot.wait_send()

        @pl.when(jnp.logical_not(moves))
        def _():
            cot_copy.wait()

        def step_rows(step, _):
            rows = pl.ds(pl.multiple_of(other + step * 256, 256), 256)
            low = pl.ds(pl.multiple_of(step * 256, 256), 256)
            send_rows[low, :] = branch(rows).astype(BF16)
            return 0

        lax.fori_loop(0, half // 256, step_rows, 0)

    def bown():
        def step_rows(step, _):
            rows = pl.ds(pl.multiple_of(base + step * 256, 256), 256)
            low = pl.ds(pl.multiple_of(step * 256, 256), 256)
            middle[low, :] = branch(rows) + tok[low, :].astype(F32) + params[4:5, :]
            return 0

        lax.fori_loop(0, half // 256, step_rows, 0)

    def ntwo():
        def step_rows(step, _):
            low = pl.ds(pl.multiple_of(step * 256, 256), 256)
            values = middle[low, :] + got_rows[low, :].astype(F32)
            middle[low, :] = values
            normed = norm_rows(values, params[2:3, :], params[3:4, :])
            second[pl.ds(pl.multiple_of(base + step * 256, 256), 256), :] = normed.astype(BF16)
            return 0

        lax.fori_loop(0, half // 256, step_rows, 0)
        put(middle, middle_out, 25)

    def lift():
        k = count_step("lift")
        complete(1, k)
        if k == 0:
            for sem in range(12, 16):
                done(sem)
        if k >= 2:
            done(28 + k % 2)

        def step_rows(step, _):
            rows = pl.ds(pl.multiple_of(step * 256, 256), 256)
            pre = dot_nn(second[rows, :], w_up[:, columns(k)]) + bias[turn[k], 1:2, :]
            cdf = 0.5 * lax.erf(pre * (0.5**0.5)) + 0.5
            density = jnp.exp(-0.5 * pre * pre) * 0.3989422804014327
            joined[k, rows, :] = (pre * cdf).astype(BF16)
            slope[k % 2, rows, :] = (cdf + pre * density).astype(BF16)
            return 0

        lax.fori_loop(0, count // 256, step_rows, 0)
        put(joined.at[k], hidden_out.at[:, columns(k)], 12 + k)
        put(slope.at[k % 2], slope_out.at[:, columns(k)], 28 + k % 2)
        if k == TURNS - 1:
            put(w_up, w_up_out, 30)

    def down():
        k = count_step("down")
        complete(2, k)
        if k == 0:
            done(24)
            done(25)
            for sem in [83] + [sem for sem in sent if sem < 24]:
                sent.pop(sem).wait_send()
        slab = pltpu.make_async_copy(w_down.at[:, columns(k)], w_attn.at[:, columns(k)], local_sem.at[31])
        slab.start()
        slab.wait()

        def step_rows(step, _):
            low = pl.ds(pl.multiple_of(step * 256, 256), 256)
            own = pl.ds(pl.multiple_of(base + step * 256, 256), 256)
            away = pl.ds(pl.multiple_of(other + step * 256, 256), 256)
            mine = dot_nt(joined[k, own, :], w_attn[:, columns(k)])
            yours = dot_nt(joined[k, away, :], w_attn[:, columns(k)])
            if k == 0:
                mine = mine + params[5:6, :]
                layer_other[low, :] = yours
            elif k < TURNS - 1:
                layer_other[low, :] += yours
            else:
                send_rows[low, :] = (layer_other[low, :] + yours).astype(BF16)
            middle[low, :] += mine
            return 0

        lax.fori_loop(0, half // 256, step_rows, 0)
        if k == TURNS - 1:
            put(middle, layer_own_out, 26)
            put(send_rows, layer_other_out, 27)

    actions = {
        "pr": pair_start, "pp": plane_send, "zz": line_send, "fw": forward_on, "tok": tok_start,
        "tokw": tok_wait, "cot": cot_start, "cotx": cot_pair, "cotw": cot_wait, "norm": norm, "send": hand,
        "wait": take, "proj": proj, "att": att, "both": both, "bown": bown, "ntwo": ntwo, "lift": lift,
        "down": down,
    }
    for name, *numbers in FORWARD_STEPS:
        actions[name](*numbers)
    for sem in sorted(outs):
        outs[sem].wait()
    for copy in sent.values():
        copy.wait_send()


def forward_pass(lengths, shards, tokens, cotangent, weights, vectors):
    half, features = tokens.shape
    count = 2 * half
    any_space = pl.BlockSpec(memory_space=pl.ANY)
    vmem = pl.BlockSpec(memory_space=pltpu.VMEM)
    smem = pl.BlockSpec(memory_space=pltpu.SMEM)
    wide = (features, TURNS * SPAN)
    shapes = [
        (wide, BF16), (wide, BF16), (wide, BF16), ((half, features), BF16), ((count, features), BF16),
        ((8, count), F32), ((count, features), BF16), ((count, features), BF16),
        ((TURNS, count, SPAN), BF16), ((TURNS, count, 256), BF16), ((TURNS, 8, count), F32),
        ((half, features), F32), ((count, TURNS * SPAN), BF16), ((count, TURNS * SPAN), BF16),
        ((half, features), F32), ((half, features), BF16),
    ]
    return pl.pallas_call(
        functools.partial(forward_kernel, HDIM ** (-0.5)),
        in_specs=[smem] + [any_space] * 4 + [vmem] * 13,
        out_specs=[any_space] * len(shapes),
        out_shape=[jax.ShapeDtypeStruct(shape, kind) for shape, kind in shapes],
        scratch_shapes=[
            pltpu.VMEM(wide, BF16),
            pltpu.VMEM(wide, BF16),
            pltpu.VMEM((half, features), BF16),
            pltpu.VMEM((count, features), BF16),
            pltpu.VMEM((count, features), BF16),
            pltpu.VMEM((TURNS, count, SPAN), BF16),
            pltpu.VMEM((TURNS, count, 256), BF16),
            pltpu.VMEM((half, features), F32),
            pltpu.VMEM((half, features), BF16),
            pltpu.VMEM((half, features), BF16),
            pltpu.VMEM((half, features), F32),
            pltpu.VMEM((2, count, SPAN), BF16),
            pltpu.VMEM((8, count), F32),
            pltpu.VMEM((8, count), F32),
            pltpu.VMEM((TURNS, 8, count), F32),
            pltpu.VMEM((TURNS, 8, SPAN), F32),
            pltpu.VMEM((8, features), F32),
            pltpu.VMEM((UNIT // 2, 2 * SPAN), BF16),
            pltpu.VMEM((8, SPAN), F32),
            pltpu.SemaphoreType.DMA((88,)),
            pltpu.SemaphoreType.DMA((88,)),
            pltpu.SemaphoreType.DMA((32,)),
        ],
        cost_estimate=pl.CostEstimate(
            flops=2 * count * features * 9000, bytes_accessed=90_000_000, transcendentals=30_000_000
        ),
        compiler_params=pltpu.CompilerParams(
            vmem_limit_bytes=60 << 20, collective_id=0, has_side_effects=True
        ),
        name="forward_pass",
    )(lengths, *shards, tokens, cotangent, *weights, *vectors)


BACKWARD_STEPS = (
    ("load",), ("P", 0, 0), ("pre",), ("layer", 0), ("P", 0, 1), ("pre",), ("layer", 1), ("pre",),
    ("layer", 2), ("pre",), ("2", 0, 0), ("soth",), ("send", "a"), ("P", 0, 2), ("P", 0, 3), ("wait", "a"),
    ("ntwo",), ("send", "b"), ("3", 0, 0), ("2", 0, 1), ("2", 0, 2), ("P", 1, 0), ("wait", "b"), ("hb",),
    ("att",), ("3", 0, 1), ("2", 0, 3), ("att",), ("P", 1, 1), ("att",), ("3", 0, 3), ("3", 0, 2),
    ("aend",), ("P", 1, 2), ("hb",), ("2", 1, 0), ("att",), ("2", 1, 1), ("att",), ("P", 1, 3), ("2", 1, 2),
    ("F", 0), ("att",), ("aend",), ("3", 1, 1), ("3", 1, 0), ("P", 2, 0), ("2", 1, 3), ("P", 2, 1), ("hb",),
    ("3", 1, 2), ("att",), ("G", 0), ("att",), ("att",), ("3", 1, 3), ("aend",), ("P", 2, 2), ("2", 2, 1),
    ("hb",), ("att",), ("F", 1), ("att",), ("3", 2, 1), ("2", 2, 2), ("att",), ("aend",), ("3", 2, 2),
    ("foth",), ("send", "c"), ("P", 2, 3), ("tok",), ("2", 2, 0), ("wait", "c"), ("none",), ("reloc",),
    ("none",), ("2", 2, 3), ("reloc",), ("none",), ("hs", "c"), ("G", 1), ("3", 2, 0), ("hw", "c"),
    ("hs", "x"), ("hw", "x"), ("hs", "y"), ("3", 2, 3), ("hw", "y"), ("hs", "z1"), ("reloc",), ("F", 2),
    ("hw", "z1"), ("hs", "z2"), ("wreloc",), ("G", 2), ("hw", "z2"), ("layer", 3),
)


def backward_kernel(
    scaling,
    w_attn_in, w_up_in, w_down_in, tok_in, grad_in, first_in, second_in, joined_in, heads_in, middle_in,
    hidden_in, slope_in, totals_in, layer_own_in, layer_other_in, key_mask, gain_one, gain_two,
    tokens_out, down_out, up_out, attn_out, sums_out, pre_out, layer_out, layer_got, layer_low,
    weight, grad, left, wide, right, grad_heads, totals, middle, send_rows, got_rows, key_sum, value_sum,
    product, near_got, far_got, turn_got, line_got, line_own, final, final_got, sums, sums_got,
    send_sem, recv_sem, local_sem, credit,
):
    dp, z = lax.axis_index("dp"), lax.axis_index("tensor")
    core, plane = lax.rem(dp, 2), lax.div(dp, 2)
    x_bit, y_bit = lax.rem(plane, 2), lax.div(plane, 2)
    half = middle.shape[0]
    count = 2 * half
    features = middle.shape[1]
    to_x = (y_bit * 4 + (1 - x_bit) * 2 + core, z)
    to_y = ((1 - y_bit) * 4 + x_bit * 2 + core, z)
    to_core = (plane * 2 + 1 - core, z)
    to_clip = (plane * 2 + 1 - core, z + 1 - 2 * lax.rem(z, 2))
    to_z = [(dp, lax.rem(z + k, TURNS)) for k in range(TURNS)]
    to_z_pair = (dp, z + 1 - 2 * lax.rem(z, 2))
    moves = core != lax.rem(z, 2)
    plane_x = y_bit * 2 + 1 - x_bit
    plane_y = (1 - y_bit) * 2 + x_bit
    plane_xy = (1 - y_bit) * 2 + 1 - x_bit
    turn = [lax.rem(z + TURNS - k, TURNS) for k in range(TURNS)]
    base = pl.multiple_of(core * half, 256)
    other = pl.multiple_of((1 - core) * half, 256)
    own_rows, other_rows = pl.ds(base, half), pl.ds(other, half)

    barrier = pltpu.get_barrier_semaphore()
    partners = [to_x, to_y, to_core, to_clip] + to_z[1:]
    for partner in partners:
        pl.semaphore_signal(barrier, inc=1, device_id=partner, device_id_type=pl.DeviceIdType.MESH)
    pl.semaphore_wait(barrier, len(partners))

    def remote(source, target, sem, device):
        return pltpu.make_async_remote_copy(
            src_ref=source,
            dst_ref=target,
            send_sem=send_sem.at[sem],
            recv_sem=recv_sem.at[sem],
            device_id=device,
            device_id_type=pl.DeviceIdType.MESH,
        )

    def send(source, target, sem, device):
        copy = remote(source, target, sem, device)
        copy.start()
        return copy

    def arrived(target, sem):
        remote(target, target, sem, to_core).wait_recv()

    def tell(index, device):
        pl.semaphore_signal(
            credit.at[index], inc=1, device_id=device, device_id_type=pl.DeviceIdType.MESH
        )

    def local(source, target, sem):
        copy = pltpu.make_async_copy(source, target, local_sem.at[sem])
        copy.start()
        return copy

    def columns(k):
        return pl.ds(pl.multiple_of(turn[k] * SPAN, 128), SPAN)

    def load_right(source, k, slot):
        return local(source.at[:, columns(k)], right.at[slot], slot)

    grad_load = local(grad_in, grad, 2)
    right_loads = [load_right(hidden_in, 0, 0), None]
    weight_loads, slope_loads = [], []
    for k in range(TURNS):
        weight_loads.append(local(w_down_in.at[:, columns(k)], weight.at[:, columns(k)], 3 + k))
        slope_loads.append(local(slope_in.at[:, columns(k)], wide.at[:, columns(k)], 7 + k))
    right_loads[1] = load_right(hidden_in, 1, 1)
    left_load = local(second_in, left, 11)
    layer_sent = send(layer_other_in, layer_got, 98, to_core)
    layer_load = local(layer_own_in, middle, 12)
    totals_loads = [local(totals_in.at[turn[k]], totals.at[k], 21 + k) for k in range(TURNS)]
    sums[...] = jnp.zeros_like(sums)

    in_flight = [[] for _ in range(TURNS)]
    staged = [None] * TURNS
    rows_half = UNIT // 2

    def place(k, where, part=None):
        if part is None:
            return product.at[k, pl.ds(pl.multiple_of(where * UNIT, 16), UNIT)]
        start = pl.multiple_of(where * UNIT + part * rows_half, 16)
        return product.at[k, pl.ds(start, rows_half)]

    def slot(ref, k, part):
        return ref.at[k, part * rows_half : (part + 1) * rows_half]

    def sem_of(array, kind, k):
        return array * 28 + kind * 4 + k

    def ready(k):
        for copy in in_flight[k]:
            copy.wait_send()
        in_flight[k] = []

    def stage_one(array, k):
        for part, device, near in ((0, to_x, plane_x), (1, to_y, plane_y)):
            if array > 0:
                pl.semaphore_wait(credit.at[4 * part + k], 1)
            far = place(k, plane_xy, part)
            in_flight[k] += [
                send(far, slot(far_got, k, part), sem_of(array, part, k), device),
                send(place(k, near, part), slot(near_got, k, part), sem_of(array, 2 + part, k), device),
            ]

    def add_to(target, sources):
        total = target[...].astype(F32)
        for source in sources:
            total = total + source[...].astype(F32)
        return total

    def stage_two(array, k):
        for part, device, back, far in ((0, to_y, to_x, plane_y), (1, to_x, to_y, plane_x)):
            arrived(slot(far_got, k, part), sem_of(array, part, k))
            target = place(k, far, part)
            target[...] = add_to(target, [slot(far_got, k, part)]).astype(BF16)
            if array > 0:
                pl.semaphore_wait(credit.at[8 + 4 * part + k], 1)
            in_flight[k].append(send(target, slot(turn_got, k, part), sem_of(array, 4 + part, k), device))
        for part, back in ((0, to_x), (1, to_y)):
            arrived(slot(near_got, k, part), sem_of(array, 2 + part, k))
            target = place(k, plane, part)
            target[...] = add_to(target, [slot(near_got, k, part)]).astype(BF16)
            if array < 2:
                tell(4 * part + k, back)

    def stage_three(array, k):
        for part in range(2):
            arrived(slot(turn_got, k, part), sem_of(array, 4 + part, k))
        source = place(k, plane)
        total = add_to(source, [turn_got.at[k]]).astype(BF16)
        if array < 2:
            tell(8 + k, to_y)
            tell(12 + k, to_x)
        if k == 0:
            line_own[...] = total
            return
        if array < 2:
            if staged[k] is not None:
                staged[k].wait_send()
            row, col = (k - 1) % 2, (k - 1) // 2
            source = send_rows.at[
                row * UNIT : (row + 1) * UNIT, col * SPAN : (col + 1) * SPAN
            ]
        source[...] = total
        if array > 0:
            pl.semaphore_wait(credit.at[16 + k], 1)
        copy = send(source, line_got.at[k], sem_of(array, 6, k), to_z[(TURNS - k) % TURNS])
        if array < 2:
            staged[k] = copy
        else:
            in_flight[k].append(copy)

    results = [down_out, up_out, attn_out]
    final_moves = []
    last_moves = []

    def final_one(array):
        for wait in final_moves:
            wait()
        final_moves.clear()
        for k in range(1, TURNS):
            arrived(line_got.at[k], sem_of(array, 6, k))
        final[...] = add_to(line_own, [line_got.at[k] for k in range(1, TURNS)])
        if array < 2:
            for k in range(1, TURNS):
                tell(16 + k, to_z[k])
        keep = pl.ds(pl.multiple_of(core * rows_half, 16), rows_half)
        give = pl.ds(pl.multiple_of((1 - core) * rows_half, 16), rows_half)
        final_moves.append(send(final.at[give], final_got.at[array], 90 + array, to_core).wait_send)
        target = results[array].at[:, pl.ds(pl.multiple_of(core * SPAN, 128), SPAN)]
        final_moves.append(local(final.at[keep], target, 13).wait)

    def final_two(array):
        arrived(final_got.at[array], 90 + array)
        target = results[array].at[:, pl.ds(pl.multiple_of((1 - core) * SPAN, 128), SPAN)]
        last_moves.append(local(final_got.at[array], target, 14 + array).wait)

    pre_puts, pre_loads = [], [None, None]
    loads = {"left": left_load}
    exchange = {}
    start = jnp.zeros((1, 160), F32)
    att_total = [start]

    def load():
        grad_load.wait()

    def pre():
        k = len(pre_puts)
        weight_loads[k].wait()
        slope_loads[k].wait()

        def step_rows(step, total):
            rows = pl.ds(pl.multiple_of(step * 512, 512), 512)
            value = dot_nn(grad[rows, :], weight[:, columns(k)])
            value = value * wide[rows, columns(k)].astype(F32)
            wide[rows, columns(k)] = value.astype(BF16)
            return total + jnp.sum(value, 0, keepdims=True)

        total = lax.fori_loop(0, count // 512, step_rows, jnp.zeros((1, SPAN), F32))
        sums[8 + 2 * turn[k] + core, :, :SPAN] = total
        pre_puts.append(local(wide.at[:, columns(k)], pre_out.at[:, columns(k)], 17 + k))
        weight_loads[k] = local(w_up_in.at[:, columns(k)], weight.at[:, columns(k)], 3 + k)

    def second_part(rows):
        return dot_nt(wide[rows, :], weight[...])

    def soth():
        for copy in weight_loads:
            copy.wait()

        def step_rows(step, _):
            rows = pl.ds(pl.multiple_of(other + step * 256, 256), 256)
            low = pl.ds(pl.multiple_of(step * 256, 256), 256)
            send_rows[low, :] = second_part(rows).astype(BF16)
            return 0

        lax.fori_loop(0, half // 256, step_rows, 0)

    def norm_back_rows(values, gain, above):
        center = values - jnp.mean(values, -1, keepdims=True)
        scale = lax.rsqrt(jnp.mean(center * center, -1, keepdims=True) + EPS)
        normed = center * scale
        scaled = above * gain
        back = scaled - jnp.mean(scaled, -1, keepdims=True)
        back = (back - normed * jnp.mean(scaled * normed, -1, keepdims=True)) * scale
        return back, jnp.sum(above * normed, 0, keepdims=True), jnp.sum(above, 0, keepdims=True)

    zero = jnp.zeros((1, features), F32)

    def ntwo():
        loads["middle"].wait()

        def step_rows(step, total):
            low = pl.ds(pl.multiple_of(step * 256, 256), 256)
            rows = pl.ds(pl.multiple_of(base + step * 256, 256), 256)
            above = second_part(rows) + got_rows[low, :].astype(F32)
            back, by_gain, by_shift = norm_back_rows(middle[low, :], gain_two[...][None, :], above)
            out_grad = grad[rows, :].astype(F32)
            below = out_grad + back
            middle[low, :] = below
            grad[rows, :] = below.astype(BF16)
            by_down, by_out = jnp.sum(out_grad, 0, keepdims=True), jnp.sum(below, 0, keepdims=True)
            return (total[0] + by_down, total[1] + by_out, total[2] + by_gain, total[3] + by_shift)

        parts = lax.fori_loop(0, half // 256, step_rows, (zero,) * 4)
        for i in range(4):
            sums[i, :, :] = parts[i]
        exchange["a"].wait_send()
        for copy in pre_puts[2:]:
            copy.wait()
        loads["weight"] = local(w_attn_in, weight, 3)
        loads["joined"] = [
            local(joined_in.at[turn[k]], wide.at[:, k * SPAN : (k + 1) * SPAN], 7 + k)
            for k in range(TURNS)
        ]

    def hand(name):
        if name == "a":
            exchange[name] = send(send_rows, got_rows, 84, to_core)
        elif name == "b":
            pl.semaphore_wait(credit.at[20], 1)
            exchange[name] = send(grad.at[own_rows], grad.at[own_rows], 85, to_core)
        else:
            exchange[name] = send(send_rows, got_rows, 86, to_core)

    def take(name):
        if name == "a":
            arrived(got_rows, 84)
        elif name == "b":
            arrived(grad.at[other_rows], 85)
        else:
            arrived(got_rows, 86)
            loads["tok"].wait()

    def produce(array, k):
        ready(k)
        if array < 2:
            if array == 0:
                right_loads[k % 2].wait()
                factor = grad
            else:
                pre_loads[k % 2].wait()
                if k == 0:
                    loads["left"].wait()
                factor = left

            def step_part(part, _):
                rows = pl.ds(pl.multiple_of(part * 640, 640), 640)
                product[k, rows, :] = dot_tn(factor[:, rows], right[k % 2]).astype(BF16)
                return 0

            lax.fori_loop(0, 2, step_part, 0)
            if array == 0 and k < 2:
                right_loads[k] = load_right(hidden_in, k + 2, k)
            elif array == 0:
                pre_puts[k - 2].wait()
                pre_loads[k - 2] = load_right(pre_out, k - 2, k - 2)
                if k == 3:
                    tell(20, to_core)
            elif k < 2:
                pre_loads[k] = load_right(pre_out, k + 2, k)
            if array == 1 and k == 3:
                loads["left"] = local(first_in, left, 11)
                loads["first"] = loads["left"]
        else:
            heads_load = local(heads_in.at[turn[k]], grad_heads, 4)
            if "first" in loads:
                loads.pop("first").wait()
            heads_load.wait()

            def step_part(part, _):
                rows = pl.ds(pl.multiple_of(part * 640, 640), 640)
                by_first = dot_tn(left[:, rows], wide[:, k * SPAN : k * SPAN + 480])
                by_branch = dot_tn(grad[:, rows], grad_heads[:, 96:256])
                product[k, rows, :] = jnp.concatenate([by_first, by_branch], -1).astype(BF16)
                return 0

            lax.fori_loop(0, 2, step_part, 0)
        stage_one(array, k)

    steps_done = {"hb": 0, "att": 0, "aend": 0, "none": 0, "reloc": 0}

    def count_step(name):
        steps_done[name] += 1
        return steps_done[name] - 1

    def hb():
        k = count_step("hb")
        if k == 0:
            loads["weight"].wait()
        slab = pl.ds(pl.multiple_of(turn[k] * SPAN + 384, 128), 256)

        def step_rows(step, _):
            rows = pl.ds(pl.multiple_of(step * 512, 512), 512)
            grad_heads[rows, :] = dot_nn(grad[rows, :], weight[:, slab]).astype(BF16)
            return 0

        lax.fori_loop(0, count // 512, step_rows, 0)
        loads["joined"][k].wait()
        totals_loads[k].wait()
        key_sum[...] = jnp.zeros_like(key_sum)
        value_sum[...] = jnp.zeros_like(value_sum)
        att_total[0] = start

    one_lane = (lax.broadcasted_iota(jnp.int32, (256, 48), 1) == 0).astype(F32).astype(BF16)

    def att():
        step_at = count_step("att")
        k, part = step_at // 3, step_at % 3
        low = k * SPAN

        def step_rows(step, total):
            rows = pl.ds(pl.multiple_of(step * 256, 256), 256)
            queries = wide[rows, low : low + 160]
            grads = grad_heads[rows, :]
            outs = []
            for head in range(2):
                at = head * HDIM
                query = queries[:, at : at + HDIM]
                above = grads[:, 96 + at : 96 + at + HDIM]
                key = wide[:, low + 160 + at : low + 160 + at + HDIM]
                value = wide[:, low + 320 + at : low + 320 + at + HDIM]
                scores = dot_nt(
                    jnp.concatenate([key, key_mask[:, :48]], -1),
                    jnp.concatenate([query, one_lane], -1),
                )
                probs = jnp.exp2(scores * (scaling * LOG2E) - totals[k, head : head + 1, rows])
                grad_probs = dot_nt(value, above)
                shared = jnp.sum(probs * grad_probs, 0, keepdims=True)
                grad_scores = (probs * (grad_probs - shared)).astype(BF16)
                value_sum[head, :, :HDIM] += dot_nn(probs.astype(BF16), above)
                key_sum[head, :, :HDIM] += dot_nn(grad_scores, query)
                outs.append(dot_tn(grad_scores, key) * scaling)
            joined = jnp.concatenate(outs, -1)
            wide[rows, low : low + 160] = joined.astype(BF16)
            return total + jnp.sum(joined, 0, keepdims=True)

        att_total[0] = lax.fori_loop(2 * part, 2 * part + 2, step_rows, att_total[0])

    def aend():
        k = count_step("aend")
        low = k * SPAN

        def step_rows(step, value_total):
            rows = pl.ds(pl.multiple_of(step * 256, 256), 256)
            keys = [key_sum[head, rows, :HDIM] * scaling for head in range(2)]
            values = [value_sum[head, rows, :HDIM] for head in range(2)]
            joined = jnp.concatenate(keys + values, -1)
            wide[rows, low + 160 : low + 480] = joined.astype(BF16)
            return value_total + jnp.sum(joined[:, 160:], 0, keepdims=True)

        value_total = lax.fori_loop(0, count // 256, step_rows, start)
        sums[16 + 2 * turn[k] + core, :, :160] = att_total[0]
        sums[16 + 2 * turn[k] + core, :, 160:320] = value_total

    def first_part(rows):
        total = None
        for k in range(TURNS):
            slab = pl.ds(pl.multiple_of(turn[k] * SPAN, 128), 480)
            part = dot_nt(wide[rows, k * SPAN : k * SPAN + 480], weight[:, slab])
            total = part if total is None else total + part
        return total

    def foth():
        for copy in staged[1:]:
            copy.wait_send()

        def step_rows(step, _):
            rows = pl.ds(pl.multiple_of(other + step * 256, 256), 256)
            low = pl.ds(pl.multiple_of(step * 256, 256), 256)
            send_rows[low, :] = first_part(rows).astype(BF16)
            return 0

        lax.fori_loop(0, half // 256, step_rows, 0)

    def none():
        step = count_step("none")
        low = slice(step * 256, step * 256 + 256)
        rows = pl.ds(pl.multiple_of(base + step * 256, 256), 256)
        above = first_part(rows) + got_rows[low, :].astype(F32)
        values = got_tok[low, :].astype(F32)
        back, by_gain, by_shift = norm_back_rows(values, gain_one[...][None, :], above)
        grad[half + step * 256 : half + step * 256 + 256, :] = (middle[low, :] + back).astype(BF16)
        if step == 0:
            sums[4, :, :] = by_gain
            sums[5, :, :] = by_shift
        else:
            sums[4, :, :] += by_gain
            sums[5, :, :] += by_shift

    got_tok = grad.at[0:half]

    def tokens_move(step):
        rows = pl.ds(step * 256, 256)
        source = grad.at[half + step * 256 : half + step * 256 + 256]
        away = remote(source, tokens_out.at[rows], 87 + step, to_clip)
        here = pltpu.make_async_copy(source, tokens_out.at[rows], local_sem.at[25 + step])
        return away, here

    def reloc():
        away, here = tokens_move(count_step("reloc"))

        @pl.when(moves)
        def _():
            away.start()

        @pl.when(jnp.logical_not(moves))
        def _():
            here.start()

    def wreloc():
        for step in range(half // 256):
            away, here = tokens_move(step)

            @pl.when(moves)
            def _(away=away):
                away.wait()

            @pl.when(jnp.logical_not(moves))
            def _(here=here):
                here.wait()

    hops = {"c": (0, to_core), "x": (1, to_x), "y": (2, to_y), "z1": (3, to_z_pair), "z2": (4, to_z[2])}
    hop_copies = {}

    def hs(name):
        index, device = hops[name]
        hop_copies[name] = send(sums, sums_got.at[index], 93 + index, device)

    def hw(name):
        index, _ = hops[name]
        hop_copies[name].wait_send()
        arrived(sums_got.at[index], 93 + index)
        sums[...] = sums[...] + sums_got[index]

    layer_away = remote(layer_low, layer_out, 99, to_clip)
    layer_here = pltpu.make_async_copy(layer_low, layer_out, local_sem.at[30])

    def layer(stage):
        if stage == 0:
            arrived(layer_got, 98)
            loads["layer"] = local(layer_got, send_rows, 28)
        elif stage == 1:
            layer_load.wait()
            loads["layer"].wait()

            def step_rows(step, _):
                rows = pl.ds(pl.multiple_of(step * 256, 256), 256)
                send_rows[rows, :] = (middle[rows, :] + send_rows[rows, :].astype(F32)).astype(BF16)
                return 0

            lax.fori_loop(0, half // 256, step_rows, 0)
            loads["layer"] = local(send_rows, layer_low, 29)
            loads["middle"] = local(middle_in, middle, 12)
        elif stage == 2:
            loads["layer"].wait()

            @pl.when(moves)
            def _():
                layer_away.start()

            @pl.when(jnp.logical_not(moves))
            def _():
                layer_here.start()
        else:
            layer_sent.wait_send()

            @pl.when(moves)
            def _():
                layer_away.wait()

            @pl.when(jnp.logical_not(moves))
            def _():
                layer_here.wait()

    def token_load():
        exchange["b"].wait_send()
        loads["tok"] = local(tok_in, grad.at[0:half], 2)

    actions = {
        "load": load, "pre": pre, "soth": soth, "ntwo": ntwo, "hb": hb, "att": att, "aend": aend,
        "foth": foth, "none": none, "reloc": reloc, "wreloc": wreloc, "send": hand, "wait": take,
        "P": produce, "2": stage_two, "3": stage_three, "F": final_one, "G": final_two, "hs": hs, "hw": hw,
        "tok": token_load, "layer": layer,
    }
    for name, *numbers in BACKWARD_STEPS:
        actions[name](*numbers)
    sums_put = local(sums, sums_out, 5)
    exchange["c"].wait_send()
    for wait in final_moves + last_moves:
        wait()
    for k in range(TURNS):
        ready(k)
    sums_put.wait()


def backward_pass(
    w_attn, w_up, w_down, tok, grad, first, second, joined, heads, middle, hidden, slope, totals, layer_own,
    layer_other, key_mask, gain_one, gain_two,
):
    half, features = tok.shape
    count = 2 * half
    any_space = pl.BlockSpec(memory_space=pl.ANY)
    vmem = pl.BlockSpec(memory_space=pltpu.VMEM)
    cols = TURNS * SPAN
    shapes = [
        ((half, features), BF16), ((UNIT // 2, 2 * SPAN), F32), ((UNIT // 2, 2 * SPAN), F32),
        ((UNIT // 2, 2 * SPAN), F32), ((24, 1, features), F32), ((count, cols), BF16),
        ((half, features), BF16), ((half, features), BF16), ((half, features), BF16),
    ]
    return pl.pallas_call(
        functools.partial(backward_kernel, HDIM ** (-0.5)),
        in_specs=[any_space] * 15 + [vmem] * 3,
        out_specs=[any_space] * len(shapes),
        out_shape=[jax.ShapeDtypeStruct(shape, kind) for shape, kind in shapes],
        scratch_shapes=[
            pltpu.VMEM((features, cols), BF16),
            pltpu.VMEM((count, features), BF16),
            pltpu.VMEM((count, features), BF16),
            pltpu.VMEM((count, cols), BF16),
            pltpu.VMEM((2, count, SPAN), BF16),
            pltpu.VMEM((count, 256), BF16),
            pltpu.VMEM((TURNS, 8, count), F32),
            pltpu.VMEM((half, features), F32),
            pltpu.VMEM((half, features), BF16),
            pltpu.VMEM((half, features), BF16),
            pltpu.VMEM((2, count, 128), F32),
            pltpu.VMEM((2, count, 128), F32),
            pltpu.VMEM((TURNS, features, SPAN), BF16),
            pltpu.VMEM((TURNS, UNIT, SPAN), BF16),
            pltpu.VMEM((TURNS, UNIT, SPAN), BF16),
            pltpu.VMEM((TURNS, UNIT, SPAN), BF16),
            pltpu.VMEM((TURNS, UNIT, SPAN), BF16),
            pltpu.VMEM((UNIT, SPAN), BF16),
            pltpu.VMEM((UNIT, SPAN), F32),
            pltpu.VMEM((3, UNIT // 2, SPAN), F32),
            pltpu.VMEM((24, 1, features), F32),
            pltpu.VMEM((5, 24, 1, features), F32),
            pltpu.SemaphoreType.DMA((100,)),
            pltpu.SemaphoreType.DMA((100,)),
            pltpu.SemaphoreType.DMA((32,)),
            pltpu.SemaphoreType.REGULAR((24,)),
        ],
        cost_estimate=pl.CostEstimate(
            flops=4 * count * features * 6400, bytes_accessed=90_000_000, transcendentals=30_000_000
        ),
        compiler_params=pltpu.CompilerParams(
            vmem_limit_bytes=60 << 20, collective_id=1, has_side_effects=True
        ),
        name="backward_pass",
    )(
        w_attn, w_up, w_down, tok, grad, first, second, joined, heads, middle, hidden, slope, totals,
        layer_own, layer_other, key_mask, gain_one, gain_two,
    )


def finish_kernel(*refs):
    z = lax.axis_index("tensor")
    large_in, attn, sums = refs[:4], refs[4], refs[5]
    large_out, grads, vectors, held, sem = refs[6:10], refs[10:14], refs[14:-5], refs[-5:-1], refs[-1]
    loads = [pltpu.make_async_copy(large_in[i], held[i], sem.at[i]) for i in range(4)]
    copies = [pltpu.make_async_copy(held[i], large_out[i], sem.at[4 + i]) for i in range(4)]
    for load in loads:
        load.start()
    for load, copy in zip(loads, copies):
        load.wait()
        copy.start()
    width = UNIT // 2
    for i, grad in enumerate(grads):
        low = i * width
        halves = [attn[:, half * SPAN + low : half * SPAN + low + width] for half in range(2)]
        grad[...] = jnp.concatenate(halves, -1)
    for vector, row, start, size in zip(vectors, (16, 16, 8), (0, width, 0), (width, width, SPAN)):
        halves = [sums[row + 2 * z + half][:, start : start + size] for half in range(2)]
        vector[...] = jnp.concatenate(halves, -1)[0]
    for i, vector in enumerate(vectors[3:]):
        vector[...] = sums[i][0]
    for copy in copies:
        copy.wait()


def finish(layer_out, grad_tokens, grad_up, grad_down, grad_attn, sums):
    features = layer_out.shape[1]
    any_space = pl.BlockSpec(memory_space=pl.ANY)
    vmem = pl.BlockSpec(memory_space=pltpu.VMEM)
    large = (layer_out, grad_tokens, grad_up, grad_down)
    shapes = [jax.ShapeDtypeStruct(value.shape, value.dtype) for value in large]
    shapes += [jax.ShapeDtypeStruct((UNIT // 2, UNIT), F32)] * 4
    shapes += [jax.ShapeDtypeStruct((size,), F32) for size in (UNIT, UNIT, 2 * SPAN) + (features,) * 6]
    return pl.pallas_call(
        finish_kernel,
        in_specs=[any_space] * 4 + [vmem] * 2,
        out_specs=[any_space] * 4 + [vmem] * 13,
        out_shape=shapes,
        scratch_shapes=[pltpu.VMEM(value.shape, value.dtype) for value in large]
        + [pltpu.SemaphoreType.DMA((8,))],
        compiler_params=pltpu.CompilerParams(vmem_limit_bytes=24 << 20),
        name="finish",
    )(*large, grad_attn, sums)


class Links:
    def __init__(self):
        self.dp = lax.axis_size("dp")
        self.tensor = lax.axis_size("tensor")
        self.tensor_pos = lax.axis_index("tensor")
        self.half = self.tensor_pos % 2

    def pair(self, value):
        return lax.ppermute(value, "tensor", [(i, i ^ 1) for i in range(self.tensor)])

    def columns(self, shard):
        rows, _, width = shard.shape
        whole = lax.all_gather(shard, ("dp", "tensor"), axis=0)
        whole = lax.dynamic_index_in_dim(whole, self.half, 2, keepdims=False)
        whole = whole.reshape(self.dp, self.tensor, rows, width)
        return [whole[:, k].reshape(self.dp * rows, width) for k in range(self.tensor)]

    def vectors(self, value):
        whole = lax.all_gather(value, "tensor", axis=0)
        return [whole[k] for k in range(self.tensor)]

    def place(self, pieces):
        halves = (jnp.arange(2) == self.half)[None, :, None]
        return jnp.where(halves, jnp.stack(pieces)[:, None, :], 0.0)

    def gradient(self, left, rights):
        whole = jnp.stack([dot_tn(left, right).astype(BF16) for right in rights], 0)
        features, width = whole.shape[1:]
        whole = whole.reshape(self.tensor, self.dp, features // self.dp, width)
        whole = jnp.moveaxis(whole, 1, 0)[:, :, :, None, :]
        halves = (jnp.arange(2) == self.half)[None, None, None, :, None]
        whole = jnp.where(halves, whole, jnp.zeros((), BF16))
        whole = whole.reshape((self.dp * self.tensor,) + whole.shape[2:])
        return lax.psum_scatter(whole, ("dp", "tensor"), tiled=False).astype(F32)

    def merged(self, partial_of):
        got = self.pair(partial_of(1).astype(BF16))
        return partial_of(0) + got.astype(F32)


def summed(vectors, total):
    whole = total(jnp.concatenate(vectors))
    at = 0
    result = []
    for vector in vectors:
        result.append(whole[at : at + vector.shape[0]])
        at += vector.shape[0]
    return result


def halves_of(weight):
    return weight.reshape(weight.shape[0], 2, weight.shape[1] // 2)


def flat(piece):
    return piece.reshape(piece.shape[0], -1)


def local_any(
    tokens,
    lengths,
    cotangent,
    norm1_gain,
    norm1_shift,
    query_weight,
    query_bias,
    key_weight,
    value_weight,
    value_bias,
    out_weight,
    out_bias,
    norm2_gain,
    norm2_shift,
    up_weight,
    up_bias,
    down_weight,
    down_bias,
):
    links = Links()
    rows = tokens.shape[0]
    scaling = HDIM ** (-0.5)
    width = query_weight.shape[1] // 2
    heads = width // HDIM
    units = up_weight.shape[1] // 2
    count = links.tensor

    shard_attn = [query_weight, key_weight, value_weight, out_weight.T]
    w_attn = links.columns(jnp.concatenate([halves_of(w) for w in shard_attn], -1))
    w_up = jnp.concatenate(links.columns(halves_of(up_weight)), 1)
    w_down = jnp.concatenate(links.columns(halves_of(down_weight.T)), 1)
    w_qkv = [block[:, : 3 * width] for block in w_attn]
    w_out = [block[:, 3 * width :] for block in w_attn]
    small = [query_bias.reshape(2, width), value_bias.reshape(2, width), up_bias.reshape(2, units)]
    small = jnp.concatenate(small, -1)
    small = links.vectors(jnp.where(links.half == 0, small[0], small[1]))
    bias_qkv = [
        jnp.concatenate([v[:width], jnp.zeros((width,), F32), v[width : 2 * width]]) for v in small
    ]
    bias_up = jnp.concatenate([v[2 * width :] for v in small])

    place = links.tensor_pos // 2
    clip_length = jnp.sum(jnp.where(jnp.arange(lengths.shape[0]) == place, lengths, 0))
    frames = jnp.arange(rows)
    frames = jnp.concatenate([links.half * rows + frames, (1 - links.half) * rows + frames])
    visible = frames < clip_length
    mask = jnp.where(visible, 0.0, -1e30).astype(F32)

    def part_of(value, part):
        return value[part * rows : (part + 1) * rows]

    def both(value):
        return jnp.concatenate([value, links.pair(value)])

    source = tokens.astype(F32)
    first = both(norm_rows(source, norm1_gain, norm1_shift).astype(BF16))
    joined, heads_out, totals = [], [], []
    for k in range(count):
        joined.append((dot_nn(first, w_qkv[k]) + bias_qkv[k]).astype(BF16))
        mixed, total = attend(joined[k], mask[None, :], heads, scaling)
        heads_out.append(mixed)
        totals.append(total)
    heads_all = jnp.concatenate(heads_out, 1)
    w_out_all = jnp.concatenate(w_out, 1)
    branch = links.merged(lambda part: dot_nt(part_of(heads_all, part), w_out_all))
    middle = source + branch + out_bias
    second = both(norm_rows(middle, norm2_gain, norm2_shift).astype(BF16))
    hidden, slope = up_gelu(second, w_up, bias_up[None, :])
    out_own = cotangent * visible[:rows].astype(BF16)[:, None]
    out_grad = both(out_own)

    def cut(value):
        return [value[:, k * units : (k + 1) * units] for k in range(count)]

    grad_down = links.gradient(out_grad, cut(hidden))
    down_out = links.merged(lambda part: dot_nt(part_of(hidden, part), w_down))
    layer_out = (middle + down_out + down_bias).astype(BF16)
    grad_pre = (dot_nn(out_grad, w_down) * slope.astype(F32)).astype(BF16)
    grad_up = links.gradient(second, cut(grad_pre))
    grad_second = links.merged(lambda part: dot_nt(part_of(grad_pre, part), w_up))
    back_two, grad_gain_two, grad_shift_two = norm_back(middle, norm2_gain, grad_second)
    grad_middle = out_own.astype(F32) + back_two
    branch_grad = both(grad_middle.astype(BF16))
    grad_heads = [dot_nn(branch_grad, w_out[k]).astype(BF16) for k in range(count)]
    grad_out_w = links.gradient(branch_grad, heads_out)
    grad_joined, sums = [], []
    for k in range(count):
        back, sum_k = attend_back(joined[k], grad_heads[k], totals[k], mask[:, None], heads, scaling)
        grad_joined.append(back)
        sums.append(sum_k)
    grad_qkv = links.gradient(first, grad_joined)
    grad_all = jnp.concatenate(grad_joined, 1)
    w_qkv_all = jnp.concatenate(w_qkv, 1)
    grad_first = links.merged(lambda part: dot_nt(part_of(grad_all, part), w_qkv_all))
    back_one, grad_gain_one, grad_shift_one = norm_back(source, norm1_gain, grad_first)
    grad_tokens = (grad_middle + back_one).astype(BF16)

    vectors = [
        links.place([v[0] for v in cut(jnp.sum(grad_pre.astype(F32), 0)[None, :])]).reshape(-1),
        links.place([s[0, :width] for s in sums]).reshape(-1),
        links.place([s[1, :width] for s in sums]).reshape(-1),
        grad_gain_one,
        grad_shift_one,
        jnp.sum(grad_middle, 0),
        grad_gain_two,
        grad_shift_two,
        jnp.sum(out_own.astype(F32), 0),
    ]
    sum_up, sum_query, sum_value, *rest = summed(
        vectors, lambda value: lax.psum(value, ("dp", "tensor"))
    )
    sum_gain_one, sum_shift_one, sum_out, sum_gain_two, sum_shift_two, sum_down = rest

    def own(vector):
        size = vector.shape[0] // count
        return lax.dynamic_slice_in_dim(vector, links.tensor_pos * size, size, 0)

    return (
        layer_out,
        grad_tokens,
        sum_gain_one,
        sum_shift_one,
        flat(grad_qkv[:, :, :width]),
        own(sum_query),
        flat(grad_qkv[:, :, width : 2 * width]),
        flat(grad_qkv[:, :, 2 * width :]),
        own(sum_value),
        flat(grad_out_w).T,
        sum_out,
        sum_gain_two,
        sum_shift_two,
        flat(grad_up),
        own(sum_up),
        flat(grad_down).T,
        sum_down,
    )


def local_chips(
    tokens,
    lengths,
    cotangent,
    norm1_gain,
    norm1_shift,
    query_weight,
    query_bias,
    key_weight,
    value_weight,
    value_bias,
    out_weight,
    out_bias,
    norm2_gain,
    norm2_shift,
    up_weight,
    up_bias,
    down_weight,
    down_bias,
):
    weights = (query_weight, key_weight, value_weight, out_weight.T)
    vectors = (
        query_bias, value_bias, up_bias, norm1_gain, norm1_shift, norm2_gain, norm2_shift, out_bias,
        down_bias,
    )
    (
        w_attn, w_up, w_down, tok, out_grad, mask, first, second, joined, heads, totals, middle, hidden,
        slope, layer_own, layer_other,
    ) = forward_pass(lengths, (up_weight, down_weight.T), tokens, cotangent, weights, vectors)
    lane = jnp.arange(128)[None, :] == 0
    key_mask = jnp.where(lane, mask[0][:, None], 0.0).astype(BF16)
    grad_tokens, grad_down, grad_up, grad_attn, sums, _, layer_out, _, _ = backward_pass(
        w_attn, w_up, w_down, tok, out_grad, first, second, joined, heads, middle, hidden, slope, totals,
        layer_own, layer_other, key_mask, norm1_gain, norm2_gain,
    )

    (
        layer_out, grad_tokens, grad_up, grad_down, grad_query, grad_key, grad_value, grad_out, sum_query,
        sum_value, sum_up, *sums,
    ) = finish(layer_out, grad_tokens, grad_up, grad_down, grad_attn, sums)
    sum_down, sum_out, sum_gain_two, sum_shift_two, sum_gain_one, sum_shift_one = sums
    return (
        layer_out,
        grad_tokens,
        sum_gain_one,
        sum_shift_one,
        grad_query,
        sum_query,
        grad_key,
        grad_value,
        sum_value,
        grad_out.T,
        sum_out,
        sum_gain_two,
        sum_shift_two,
        grad_up,
        sum_up,
        grad_down.T,
        sum_down,
    )


def solution(mesh):
    rows = P(("dp", "tensor"), None)
    wide, tall = P("dp", "tensor"), P("tensor", "dp")
    piece, same = P("tensor"), P()
    chips = mesh.shape["dp"] == 8 and mesh.shape["tensor"] == 4
    return jax.shard_map(
        local_chips if chips else local_any,
        mesh=mesh,
        in_specs=(
            rows, P("dp"), rows, same, same, wide, piece, wide, wide, piece, tall, same, same, same,
            wide, piece, tall, same,
        ),
        out_specs=(
            rows, rows, same, same, wide, piece, wide, wide, piece, tall, same, same, same, wide, piece,
            tall, same,
        ),
        check_vma=False,
    )
```
